32 devices in a mesh: dp: 8 (over y, x, core), tensor: 4 (over z).
Axes of the slice: x: 2, y: 2, z: 4, core: 2. Of those that a mesh axis runs over, the one named last changes fastest.
Arguments:
- patches: bfloat16 [12544, 768], P(('dp', 'tensor')), may hold values from -6 to 6
- item_patches: int32 [8, 8], P('dp'), may hold values from 0 to 784, as said below
- attn_gain: float32 [768], replicated, may hold values from 0.25 to 1.75
- attn_bias: float32 [768], replicated, may hold values from -4 to 4
- qkv_weight: bfloat16 [768, 2304], P(None, 'tensor'), may hold values from -0.21875 to 0.21875
- proj_weight: bfloat16 [768, 768], P('tensor'), may hold values from -1.75 to 1.75
- mlp_gain: float32 [768], replicated, may hold values from 0.25 to 1.75
- mlp_bias: float32 [768], replicated, may hold values from -4 to 4
- up_weight: bfloat16 [768, 3072], P(None, 'tensor'), may hold values from -0.21875 to 0.21875
- up_bias: bfloat16 [3072], P('tensor'), may hold values from -4 to 4
- down_weight: bfloat16 [3072, 768], P('tensor'), may hold values from -0.15625 to 0.15625
- cotangent: bfloat16 [12544, 768], P(('dp', 'tensor')), may hold values from -6 to 6
Outputs:
- output: bfloat16 [12544, 768], P(('dp', 'tensor'))
- patches_grad: float32 [12544, 768], P(('dp', 'tensor'))
- attn_gain_grad: float32 [768], replicated
- attn_bias_grad: float32 [768], replicated
- qkv_weight_grad: float32 [768, 2304], P(None, 'tensor')
- proj_weight_grad: float32 [768, 768], P('tensor')
- mlp_gain_grad: float32 [768], replicated
- mlp_bias_grad: float32 [768], replicated
- up_weight_grad: float32 [768, 3072], P(None, 'tensor')
- up_bias_grad: float32 [3072], P('tensor')
- down_weight_grad: float32 [3072, 768], P('tensor')
The draws below stay inside these ranges and needn't reach their ends.
Inputs may be any that keep to these rules, and one draw needn't show every extreme that they name: `item_patches`: row g lists, in order, the items whose patches fill the rows of index g of dp. Each aligned group of four slots is either 784 followed by three zeros or four entries of 196, so every aligned block of 784 rows holds whole items; zeros are empty slots. Every row names at least one item of 784 patches; the rest are drawn at random.
All inputs are finite; a program needn't handle non-finite values.
Results may differ from the reference program's by a relative error of at most 0.012.
The reference program's roundings to bfloat16 on the way count: a program that leaves them out, or rounds other values in their place, can miss the bound.
Values may be sent and summed in bfloat16 or wider, within the bound.
No kernel may reach another device: no remote copies, remote signals or barrier semaphores. Data moves between devices by JAX's collectives and lax.ppermute only.
A program may use at most 128 MiB of HBM per device.

```python
import jax
import jax.numpy as jnp
from jax import lax

D = 768
HEADS = 12
HEAD_DIM = 64
FF = 3072
BLOCK = 784
BLOCKS_DEV = 2
TOKENS = 12544
N_DP = 8


def draw_item_patches(key, part):
    key_big = jax.random.fold_in(key, 11)
    key_force = jax.random.fold_in(key, 23)
    big_flags = jax.random.randint(key_big, (N_DP, BLOCKS_DEV), 0, 2)
    forced = jax.random.randint(key_force, (N_DP,), 0, BLOCKS_DEV)
    column_ids = jnp.arange(BLOCKS_DEV, dtype=jnp.int32)
    big_flags = jnp.where(column_ids[None, :] == forced[:, None], 1, big_flags)
    small_size = BLOCK // 4
    first_slot = jnp.where(big_flags == 1, BLOCK, small_size)
    other_slot = jnp.where(big_flags == 1, 0, small_size)
    slot_table = jnp.stack([first_slot, other_slot, other_slot, other_slot], axis=2)
    return slot_table.reshape(N_DP, 4 * BLOCKS_DEV).astype(jnp.int32)


def steps_of(rng, extent, pieces, low, largest):
    gain, own = 1.0, jax.random.fold_in(rng, 6)
    for dim, shards_of in pieces:
        steps = jnp.exp(jax.random.uniform(jax.random.fold_in(own, dim), (shards_of,), jnp.float32, low / len(pieces), largest / len(pieces)))
        gain = gain * jnp.repeat(steps, extent[dim] // shards_of).reshape([-1 if axis == dim else 1 for axis in range(len(extent))])
    return gain


def gaussian(rng, extent, width, bound, pieces=(), held_as=jnp.bfloat16):
    array = width * jax.random.normal(rng, extent, jnp.float32)
    if pieces:
        array = array * steps_of(rng, extent, pieces, -0.22, 0.18)
    return jnp.clip(array, -bound, bound).astype(held_as)


def setup_inputs(seed: int = 0) -> dict:
    streams_of = jax.random.split(jax.random.key(seed), 13)
    patches = gaussian(streams_of[0], (TOKENS, D), 1.0, 6.0, ((0, 32),))
    item_patches = draw_item_patches(jax.random.fold_in(streams_of[12], 71), 0)
    attn_gain = jnp.clip(1.0 + 0.15 * jax.random.normal(streams_of[2], (D,), jnp.float32), 0.25, 1.75)
    attn_bias = gaussian(streams_of[3], (D,), 0.3, 4.0, (), jnp.float32)
    qkv_weight = gaussian(streams_of[4], (D, 3 * D), D ** -0.5, 0.21875, ((1, 4),))
    proj_weight = gaussian(streams_of[5], (D, D), (D // 64) ** -0.5, 1.75, ((0, 4),))
    mlp_gain = jnp.clip(1.0 + 0.15 * jax.random.normal(streams_of[6], (D,), jnp.float32), 0.25, 1.75)
    mlp_bias = gaussian(streams_of[7], (D,), 0.3, 4.0, (), jnp.float32)
    up_weight = gaussian(streams_of[8], (D, FF), D ** -0.5, 0.21875, ((1, 4),))
    up_bias = gaussian(streams_of[9], (FF,), 0.5, 4.0, ((0, 4),))
    down_weight = gaussian(streams_of[10], (FF, D), (FF // 2) ** -0.5, 0.15625, ((0, 4),))
    cotangent = gaussian(streams_of[11], (TOKENS, D), 1.0, 6.0, ((0, 32),))
    return dict(patches=patches, item_patches=item_patches, attn_gain=attn_gain, attn_bias=attn_bias, qkv_weight=qkv_weight, proj_weight=proj_weight, mlp_gain=mlp_gain, mlp_bias=mlp_bias, up_weight=up_weight, up_bias=up_bias, down_weight=down_weight, cotangent=cotangent)


NORM_EPS = 1e-06

@jax.custom_vjp
def low(v):
    return lax.optimization_barrier(v.astype(jnp.bfloat16)).astype(jnp.float32)

@jax.custom_vjp
def low_back(v):
    return v

def low_keep(v):
    return (low(v), None)

def low_pass(kept, grad):
    return (grad,)

def back_keep(v):
    return (v, None)

def back_low(kept, grad):
    return (low(grad),)
low.defvjp(low_keep, low_pass)
low_back.defvjp(back_keep, back_low)

def layer_norm(row_block, gain_vec, shift_vec):
    centre = row_block - lax.optimization_barrier(jnp.mean(row_block, axis=-1, keepdims=True))
    spread = lax.optimization_barrier(jnp.mean(centre * centre, axis=-1, keepdims=True))
    return centre * lax.rsqrt(spread + NORM_EPS) * gain_vec + shift_vec

def matmul_high(left_side, right_side):
    return jnp.dot(left_side, right_side, precision=lax.Precision.HIGHEST, preferred_element_type=jnp.float32)

def block_forward(params, row_block, labels):
    attn_gain, attn_bias, qkv_weight, proj_weight, mlp_gain, mlp_bias, up_weight, up_bias, down_weight = params
    normed = low(layer_norm(row_block, attn_gain, attn_bias))
    packed = low(low_back(matmul_high(normed, qkv_weight)))
    packed = packed.reshape(BLOCK, HEADS, 3, HEAD_DIM)
    queries = packed[:, :, 0]
    key_rows = packed[:, :, 1]
    value_rows = packed[:, :, 2]
    scores = jnp.einsum('qhd,khd->hqk', queries, key_rows, precision=lax.Precision.HIGHEST) * HEAD_DIM ** (-0.5)
    same_item = labels[:, None] == labels[None, :]
    scores = low_back(jnp.where(same_item[None], scores, -1e+30))
    prob_rows = low(jax.nn.softmax(scores, axis=-1))
    mixed_heads = jnp.einsum('hqk,khd->qhd', prob_rows, value_rows, precision=lax.Precision.HIGHEST)
    mixed_heads = low(low_back(mixed_heads.reshape(BLOCK, D)))
    middle = row_block + low_back(matmul_high(mixed_heads, proj_weight))
    second = low(layer_norm(middle, mlp_gain, mlp_bias))
    hidden = low(jax.nn.gelu(low_back(matmul_high(second, up_weight) + up_bias), approximate=False))
    return middle + matmul_high(hidden, down_weight)

def reference(patches, item_patches, attn_gain, attn_bias, qkv_weight, proj_weight, mlp_gain, mlp_bias, up_weight, up_bias, down_weight, cotangent):
    group_rows = BLOCKS_DEV * BLOCK
    item_ends = jnp.cumsum(item_patches, axis=1).astype(jnp.int32)
    places = jnp.arange(group_rows, dtype=jnp.int32)
    labels = lax.optimization_barrier(jnp.sum((places[None, :, None] >= item_ends[:, None, :]).astype(jnp.int32), axis=2))
    labels = labels.reshape(-1, BLOCK)
    stepper = jax.checkpoint(block_forward)

    def forward(inputs, gain_one, bias_one, wqkv, wproj, gain_two, bias_two, wup, bup, wdown):
        params = (gain_one, bias_one, wqkv, wproj, gain_two, bias_two, wup, bup, wdown)
        blocks_in = inputs.reshape(-1, BLOCK, D)

        def advance(carry, operands):
            return (carry, stepper(params, operands[0], operands[1]))
        unused, outputs = lax.scan(advance, jnp.int32(0), (blocks_in, labels))
        return outputs.reshape(-1, D)
    floats = (patches.astype(jnp.float32), attn_gain.astype(jnp.float32), attn_bias.astype(jnp.float32), qkv_weight.astype(jnp.float32), proj_weight.astype(jnp.float32), mlp_gain.astype(jnp.float32), mlp_bias.astype(jnp.float32), up_weight.astype(jnp.float32), up_bias.astype(jnp.float32), down_weight.astype(jnp.float32))
    result, pullback = jax.vjp(forward, *floats)
    grads = pullback(cotangent.astype(jnp.float32))
    return (result.astype(jnp.bfloat16), grads[0], grads[1], grads[2], grads[3], grads[4], grads[5], grads[6], grads[7], grads[8], grads[9])
```

```python
import jax
import jax.numpy as jnp
from jax import lax
from jax.experimental import pallas as pl
from jax.experimental.pallas import tpu as pltpu
from jax.sharding import Mesh
from jax.sharding import PartitionSpec as P

HEAD_DIM = 64
BLOCK = 784
NORM_EPS = 1e-06
SCALE = HEAD_DIM**-0.5
LOG2E = 1.4426950408889634
F32 = jnp.float32
BF16 = jnp.bfloat16
VMEM_LIMIT = 58 * 1024 * 1024
SWAP = [(0, 1), (1, 0)]
CORE_T = ("c", "t")
ROUND_ONE = [(0, 1), (4, 2), (1, 0), (5, 3), (6, 7), (2, 5), (7, 6), (3, 4)]
ROUND_TWO = [(0, 3), (1, 2), (6, 4), (7, 5)]
ROUND_ONE_BACK = [(b, a) for a, b in ROUND_ONE]
ROUND_TWO_BACK = [(b, a) for a, b in ROUND_TWO]
ROW_SWAP = [(4, 1), (1, 4), (6, 3), (3, 6)]


def dot(left, right, left_dim=1, right_dim=0):
    return lax.dot_general(
        left, right, (((left_dim,), (right_dim,)), ((), ())), preferred_element_type=F32
    )


def normal(rows):
    centre = rows - jnp.mean(rows, axis=-1, keepdims=True)
    spread = jnp.mean(centre * centre, axis=-1, keepdims=True)
    inverse = lax.rsqrt(spread + NORM_EPS)
    return centre * inverse, inverse


def row_labels(ends_ref, first, shape, dim):
    places = lax.broadcasted_iota(jnp.int32, shape, dim) + first
    labels = jnp.zeros(shape, jnp.int32)
    for slot in range(ends_ref.shape[0]):
        labels = labels + (places >= ends_ref[slot]).astype(jnp.int32)
    return labels


def chunks_of(rows):
    edges = [min(256 * i, rows) for i in range(rows // 256 + 1)]
    edges[-1] = rows
    return [(a, b) for a, b in zip(edges[:-1], edges[1:]) if b > a]


def attention_kernel(
    ends_ref, first_ref, x_ref, gain_ref, bias_ref, w_ref, normed_ref, packed_ref, heads_ref, lse_ref
):
    rows = x_ref.shape[0]
    heads = heads_ref.shape[0] // HEAD_DIM
    unit, _ = normal(x_ref[...].astype(F32))
    normed_ref[...] = (unit * gain_ref[...] + bias_ref[...]).astype(BF16)
    label_col = row_labels(ends_ref, first_ref[0], (rows, 1), 0)
    label_row = row_labels(ends_ref, first_ref[0], (1, rows), 1)

    def head(h, carry):
        base = pl.multiple_of(h * 3 * HEAD_DIM, 3 * HEAD_DIM)
        w_head = w_ref[pl.ds(base, 3 * HEAD_DIM), :]
        packed = dot(w_head, normed_ref[...], 1, 1).astype(BF16)
        packed_ref[pl.ds(base, 3 * HEAD_DIM), :] = packed
        queries = packed[:HEAD_DIM] * SCALE
        key_rows = packed[HEAD_DIM : 2 * HEAD_DIM].T
        values = packed[2 * HEAD_DIM :]
        for a, b in chunks_of(rows):
            scores = dot(key_rows, queries[:, a:b]) * LOG2E
            scores = jnp.where(label_col == label_row[:, a:b], scores, -1e30)
            top = jnp.max(scores, axis=0, keepdims=True)
            weights = jnp.exp2(scores - top)
            total = jnp.sum(weights, axis=0, keepdims=True)
            mixed = dot(values, weights.astype(BF16)) * (1.0 / total)
            heads_ref[pl.ds(pl.multiple_of(h * HEAD_DIM, HEAD_DIM), HEAD_DIM), a:b] = mixed.astype(
                BF16
            )
            lse_ref[pl.ds(h, 1), a:b] = top + jnp.log2(total)
        return carry

    lax.fori_loop(0, heads, head, 0)


def vmem(count):
    return [pl.BlockSpec(memory_space=pltpu.VMEM)] * count


def attention(ends, first, x, gain, bias, w):
    rows, width = x.shape
    depth = w.shape[0]
    heads = depth // (3 * HEAD_DIM)
    return pl.pallas_call(
        attention_kernel,
        out_shape=(
            jax.ShapeDtypeStruct((rows, width), BF16),
            jax.ShapeDtypeStruct((depth, rows), BF16),
            jax.ShapeDtypeStruct((heads * HEAD_DIM, rows), BF16),
            jax.ShapeDtypeStruct((8, rows), F32),
        ),
        in_specs=[pl.BlockSpec(memory_space=pltpu.SMEM)] * 2 + vmem(4),
        out_specs=tuple(vmem(4)),
        compiler_params=pltpu.CompilerParams(vmem_limit_bytes=VMEM_LIMIT),
        cost_estimate=pl.CostEstimate(flops=int(3e9), bytes_accessed=int(8e6), transcendentals=0),
        name="attention",
    )(ends, first, x, gain.reshape(1, -1), bias.reshape(1, -1), w)


def project_kernel(heads_ref, proj_ref, out_ref):
    out_ref[...] = dot(heads_ref[...], proj_ref[...], 0, 0).astype(BF16)


def project(heads_out, proj):
    rows = heads_out.shape[1]
    return pl.pallas_call(
        project_kernel,
        out_shape=jax.ShapeDtypeStruct((rows, proj.shape[1]), BF16),
        in_specs=vmem(2),
        out_specs=vmem(1)[0],
        compiler_params=pltpu.CompilerParams(vmem_limit_bytes=VMEM_LIMIT),
        cost_estimate=pl.CostEstimate(flops=int(5e8), bytes_accessed=int(3e6), transcendentals=0),
        name="project",
    )(heads_out, proj)


def feed_kernel(
    x_ref,
    mine_ref,
    other_ref,
    cot_ref,
    gain_ref,
    shift_ref,
    up_ref,
    bias_ref,
    down_ref,
    middle_ref,
    out_ref,
    back_ref,
    up_grad_ref,
    down_grad_ref,
    bias_grad_ref,
    second,
    second_t,
    out_sum,
    back_sum,
):
    step = pl.program_id(0)

    @pl.when(step == 0)
    def _():
        middle = x_ref[...].astype(F32) + (mine_ref[...].astype(F32) + other_ref[...].astype(F32))
        middle_ref[...] = middle
        unit, _ = normal(middle)
        low = (unit * gain_ref[...] + shift_ref[...]).astype(BF16)
        second[...] = low
        second_t[...] = low.T
        out_sum[...] = jnp.zeros_like(out_sum)
        back_sum[...] = jnp.zeros_like(back_sum)

    pre = dot(second[...], up_ref[0]) + bias_ref[0].astype(F32)
    gate = 0.5 * (1.0 + lax.erf(pre * (2.0**-0.5)))
    slope = gate + pre * (jnp.exp2(pre * pre * (-0.5 * LOG2E)) * (0.5 / 3.141592653589793) ** 0.5)
    hidden = (pre * gate).astype(BF16)
    out_sum[...] += dot(hidden, down_ref[0])
    down_grad_ref[0] = dot(hidden, cot_ref[...], 0, 0).astype(BF16)
    act = (dot(cot_ref[...], down_ref[0], 1, 1) * slope).astype(BF16)
    bias_grad_ref[0] = jnp.sum(act.astype(F32), axis=0, keepdims=True)
    back_sum[...] += dot(act, up_ref[0], 1, 1)
    up_grad_ref[0] = dot(second_t[...], act).astype(BF16)

    @pl.when(step == pl.num_programs(0) - 1)
    def _():
        out_ref[...] = out_sum[...].astype(BF16)
        back_ref[...] = back_sum[...].astype(BF16)


def feed(x, mine, other, cot, gain, shift, up, bias, down):
    rows, width = x.shape
    slots, _, units = up.shape
    tile = 256
    per = units // tile
    whole = pl.BlockSpec((rows, width), lambda j: (0, 0))
    vector = pl.BlockSpec((1, width), lambda j: (0, 0))
    return pl.pallas_call(
        feed_kernel,
        grid=(slots * per,),
        out_shape=(
            jax.ShapeDtypeStruct((rows, width), F32),
            jax.ShapeDtypeStruct((rows, width), BF16),
            jax.ShapeDtypeStruct((rows, width), BF16),
            jax.ShapeDtypeStruct((slots, width, units), BF16),
            jax.ShapeDtypeStruct((slots, units, width), BF16),
            jax.ShapeDtypeStruct((slots, 1, units), F32),
        ),
        in_specs=[whole] * 4
        + [vector] * 2
        + [
            pl.BlockSpec((1, width, tile), lambda j: (j // per, 0, j % per)),
            pl.BlockSpec((1, 1, tile), lambda j: (j // per, 0, j % per)),
            pl.BlockSpec((1, tile, width), lambda j: (j // per, j % per, 0)),
        ],
        out_specs=(
            whole,
            whole,
            whole,
            pl.BlockSpec((1, width, tile), lambda j: (j // per, 0, j % per)),
            pl.BlockSpec((1, tile, width), lambda j: (j // per, j % per, 0)),
            pl.BlockSpec((1, 1, tile), lambda j: (j // per, 0, j % per)),
        ),
        scratch_shapes=[
            pltpu.VMEM((rows, width), BF16),
            pltpu.VMEM((width, rows), BF16),
            pltpu.VMEM((rows, width), F32),
            pltpu.VMEM((rows, width), F32),
        ],
        compiler_params=pltpu.CompilerParams(vmem_limit_bytes=VMEM_LIMIT),
        cost_estimate=pl.CostEstimate(flops=int(11e9), bytes_accessed=int(2e7), transcendentals=0),
        name="feed",
    )(x, mine, other, cot, gain.reshape(1, -1), shift.reshape(1, -1), up, bias, down)


def back_kernel(
    ends_ref,
    first_ref,
    middle_ref,
    mine_ref,
    other_ref,
    cot_ref,
    gain_ref,
    normed_ref,
    packed_ref,
    heads_ref,
    lse_ref,
    w_ref,
    proj_ref,
    middle_grad_ref,
    first_grad_ref,
    w_grad_ref,
    proj_grad_ref,
    sums_ref,
    branch,
    packed_grad,
):
    rows = middle_ref.shape[0]
    heads = heads_ref.shape[0] // HEAD_DIM
    unit, inverse = normal(middle_ref[...])
    grad = mine_ref[...].astype(F32) + other_ref[...].astype(F32)
    sums_ref[0:1, :] = jnp.sum(grad * unit, axis=0, keepdims=True)
    sums_ref[1:2, :] = jnp.sum(grad, axis=0, keepdims=True)
    scaled = grad * gain_ref[...]
    mean_one = jnp.mean(scaled, axis=-1, keepdims=True)
    mean_two = jnp.mean(scaled * unit, axis=-1, keepdims=True)
    middle_grad = cot_ref[...].astype(F32) + (scaled - mean_one - unit * mean_two) * inverse
    middle_grad_ref[...] = middle_grad
    branch[...] = middle_grad.astype(BF16)
    proj_grad_ref[...] = dot(heads_ref[...], branch[...]).astype(BF16)
    label_col = row_labels(ends_ref, first_ref[0], (rows, 1), 0)
    label_row = row_labels(ends_ref, first_ref[0], (1, rows), 1)

    def head(h, carry):
        base = pl.multiple_of(h * 3 * HEAD_DIM, 3 * HEAD_DIM)
        part = pl.ds(pl.multiple_of(h * HEAD_DIM, HEAD_DIM), HEAD_DIM)
        mixed = heads_ref[part, :]
        mixed_grad = dot(proj_ref[part, :], branch[...], 1, 1).astype(BF16)
        packed = packed_ref[pl.ds(base, 3 * HEAD_DIM), :]
        queries = packed[:HEAD_DIM] * SCALE
        keys = packed[HEAD_DIM : 2 * HEAD_DIM]
        key_rows = keys.T
        value_rows = packed[2 * HEAD_DIM :].T
        inner = jnp.sum(mixed.astype(F32) * mixed_grad.astype(F32), axis=0, keepdims=True)
        key_grad = jnp.zeros((HEAD_DIM, rows), F32)
        value_grad = jnp.zeros((HEAD_DIM, rows), F32)
        for a, b in chunks_of(rows):
            scores = dot(key_rows, queries[:, a:b]) * LOG2E
            scores = jnp.where(label_col == label_row[:, a:b], scores, -1e30)
            prob = jnp.exp2(scores - lse_ref[pl.ds(h, 1), a:b])
            value_grad += dot(mixed_grad[:, a:b], prob.astype(BF16), 1, 1)
            prob_grad = dot(value_rows, mixed_grad[:, a:b])
            score_grad = (prob * (prob_grad - inner[:, a:b])).astype(BF16)
            packed_grad[pl.ds(base, HEAD_DIM), a:b] = (dot(keys, score_grad) * SCALE).astype(BF16)
            key_grad += dot(queries[:, a:b], score_grad, 1, 1)
        packed_grad[pl.ds(base + HEAD_DIM, HEAD_DIM), :] = key_grad.astype(BF16)
        packed_grad[pl.ds(base + 2 * HEAD_DIM, HEAD_DIM), :] = value_grad.astype(BF16)
        w_grad_ref[pl.ds(base, 3 * HEAD_DIM), :] = dot(
            packed_grad[pl.ds(base, 3 * HEAD_DIM), :], normed_ref[...]
        ).astype(BF16)
        return carry

    lax.fori_loop(0, heads, head, 0)
    first_grad_ref[...] = dot(packed_grad[...], w_ref[...], 0, 0).astype(BF16)


def back(ends, first, middle, mine, other, cot, gain, normed, packed, heads_out, lse, w, proj):
    rows, width = middle.shape
    depth = w.shape[0]
    return pl.pallas_call(
        back_kernel,
        out_shape=(
            jax.ShapeDtypeStruct((rows, width), F32),
            jax.ShapeDtypeStruct((rows, width), BF16),
            jax.ShapeDtypeStruct((depth, width), BF16),
            jax.ShapeDtypeStruct(proj.shape, BF16),
            jax.ShapeDtypeStruct((2, width), F32),
        ),
        in_specs=[pl.BlockSpec(memory_space=pltpu.SMEM)] * 2 + vmem(11),
        out_specs=tuple(vmem(5)),
        scratch_shapes=[pltpu.VMEM((rows, width), BF16), pltpu.VMEM((depth, rows), BF16)],
        compiler_params=pltpu.CompilerParams(vmem_limit_bytes=VMEM_LIMIT),
        cost_estimate=pl.CostEstimate(flops=int(6e9), bytes_accessed=int(2e7), transcendentals=0),
        name="back",
    )(
        ends,
        first,
        middle,
        mine,
        other,
        cot,
        gain.reshape(1, -1),
        normed,
        packed,
        heads_out,
        lse,
        w,
        proj,
    )


def pair(place, held, received, axis=0):
    return jnp.where(
        place == 0,
        jnp.stack([held, received], axis),
        jnp.stack([received, held], axis),
    )


def gather_weights(piece, c, t, x, y):
    home = t // 2 == c
    one = lax.ppermute(piece, CORE_T, ROUND_ONE)
    two = lax.ppermute(piece, CORE_T, ROUND_TWO)
    rest = jnp.where(home, piece, two)
    first_slot = jnp.where(home, 1 - (t & 1), (t & 1) ^ c)
    held_a = jnp.where(first_slot == 0, one, rest)
    held_b = jnp.where(first_slot == 0, rest, one)
    got_a = lax.ppermute(held_a, "x", SWAP)
    got_b = lax.ppermute(held_b, "y", SWAP)
    half_a = pair(x, held_a, got_a)
    half_b = pair(y, held_b, got_b)
    far_a = lax.ppermute(half_a, "y", SWAP)
    far_b = lax.ppermute(half_b, "x", SWAP)

    def take(start, stop):
        parts = []
        for half, far, place, axis in ((half_a, far_a, y, 0), (half_b, far_b, x, 1)):
            full = pair(place, half[:, start:stop], far[:, start:stop], axis)
            parts.append(full.reshape(-1, full.shape[-1]))
        return parts

    return take


def add_low(left, right):
    return (left.astype(F32) + right.astype(F32)).astype(BF16)


def reduce_grads(grads_a, grads_b, c, t, x, y, outer):
    pick = lambda array, place, axis: lax.dynamic_index_in_dim(array, place, axis, keepdims=False)
    got_a = lax.ppermute(pick(grads_a, 1 - y, 0), "y", SWAP)
    got_b = lax.ppermute(pick(grads_b, 1 - x, 1), "x", SWAP)
    half_a = add_low(pick(grads_a, y, 0), got_a)
    half_b = add_low(pick(grads_b, x, 1), got_b)
    got_a = lax.ppermute(pick(half_a, 1 - x, 0), "x", SWAP)
    got_b = lax.ppermute(pick(half_b, 1 - y, 0), "y", SWAP)
    held_a = add_low(pick(half_a, x, 0), got_a)
    held_b = add_low(pick(half_b, y, 0), got_b)
    home = t // 2 == c
    first_slot = jnp.where(home, 1 - (t & 1), (t & 1) ^ c)
    one = jnp.where(first_slot == 0, held_a, held_b)
    rest = jnp.where(first_slot == 0, held_b, held_a)
    got_one = lax.ppermute(one, CORE_T, ROUND_ONE_BACK)
    got_two = lax.ppermute(rest, CORE_T, ROUND_TWO_BACK)
    part = (
        got_one.astype(F32)
        + got_two.astype(F32)
        + jnp.where(home, rest.astype(F32), jnp.zeros((), F32))
    ).astype(BF16)
    size = part.shape[0]
    part = part.reshape(2, size // 2, part.shape[1])
    share = add_low(pick(part, c, 0), lax.ppermute(pick(part, 1 - c, 0), "c", SWAP))
    if outer > 1:
        share = lax.psum(share.astype(F32), "o").astype(BF16)
    by_x = lax.ppermute(share, "x", SWAP)
    by_y = lax.ppermute(share, "y", SWAP)
    by_xy = lax.ppermute(share, ("y", "x"), [(0, 3), (1, 2), (2, 1), (3, 0)])
    near = pair(x, share, by_x)
    far = pair(x, by_y, by_xy)
    mine = pair(y, near, far)
    other = lax.ppermute(mine, "c", SWAP)
    return pair(c, mine, other, 2).reshape(2, 2, size, -1)


def local(
    patches,
    item_patches,
    attn_gain,
    attn_bias,
    qkv_weight,
    proj_weight,
    mlp_gain,
    mlp_bias,
    up_weight,
    up_bias,
    down_weight,
    cotangent,
):
    c, t, x, y = (lax.axis_index(name) for name in ("c", "t", "x", "y"))
    outer = lax.axis_size("o")
    quarter = 2 * y + x
    member = t & 1
    own_rows, width = patches.shape
    stays = c == member

    def exchange(array):
        return lax.ppermute(array, "c", SWAP)

    def swap_rows(array):
        return jnp.where(stays, array, lax.ppermute(array, CORE_T, ROW_SWAP))

    def both_halves(array):
        return pair(c, array, exchange(array)).reshape(2 * own_rows, -1)

    def cut(array, pieces=4):
        rows = array.shape[0] // pieces
        return lax.dynamic_slice_in_dim(array, quarter * rows, rows, 0)

    qkv_t = qkv_weight.T
    depth = qkv_t.shape[0]
    units = down_weight.shape[0]
    inner = proj_weight.shape[0]
    bias_rows = jnp.broadcast_to(up_bias[None, :], (16, units))
    piece_one = jnp.concatenate([cut(qkv_t), bias_rows], 0)
    piece_two = jnp.concatenate([cut(proj_weight), cut(up_weight), cut(down_weight)], 0)
    take_one = gather_weights(piece_one, c, t, x, y)
    inputs = swap_rows(patches)
    block_in = both_halves(inputs)
    q_rows = depth // 4
    w = jnp.concatenate(take_one(0, q_rows), 0)
    bias = jnp.stack([part[:1] for part in take_one(q_rows, q_rows + 16)])
    cot = swap_rows(cotangent)
    block_cot = both_halves(cot)
    take_two = gather_weights(piece_two, c, t, x, y)
    p_rows, u_rows = inner // 4, width // 4
    proj = jnp.concatenate(take_two(0, p_rows), 0)
    up = jnp.stack(take_two(p_rows, p_rows + u_rows))
    down = jnp.stack(take_two(p_rows + u_rows, p_rows + u_rows + units // 4))

    items = pair(c, item_patches[0], exchange(item_patches)[0])
    ends = jnp.cumsum(lax.dynamic_index_in_dim(items, member, 0, keepdims=False))
    first = (t // 2 * BLOCK).astype(jnp.int32).reshape(1)

    normed, packed, heads_out, lse = attention(ends, first, block_in, attn_gain, attn_bias, w)
    mine = project(heads_out, proj)
    middle, out_part, back_part, up_grad, down_grad, bias_grad = feed(
        block_in, mine, exchange(mine), block_cot, mlp_gain, mlp_bias, up, bias, down
    )

    def own(array):
        return lax.dynamic_slice_in_dim(array, c * own_rows, own_rows, 0)

    middle_grad, first_part, w_grad, proj_grad, mlp_sums = back(
        ends,
        first,
        middle,
        back_part,
        exchange(back_part),
        block_cot,
        mlp_gain,
        normed,
        packed,
        heads_out,
        lse,
        w,
        proj,
    )

    def quarters(array):
        return array.reshape(2, 2, -1, array.shape[-1])

    feed_sum = reduce_grads(
        *(jnp.concatenate([quarters(up_grad[s]), quarters(down_grad[s])], 2) for s in range(2)),
        c, t, x, y, outer,
    )
    up_sum = feed_sum[:, :, :u_rows].reshape(width, units)
    down_sum = feed_sum[:, :, u_rows:].reshape(units, width)

    result = own(middle) + own(out_part).astype(F32) + own(exchange(out_part)).astype(F32)
    result = swap_rows(result.astype(BF16))

    attn_sum = reduce_grads(
        *(
            jnp.concatenate(
                [
                    quarters(w_grad[s * depth : (s + 1) * depth]),
                    quarters(proj_grad[s * inner : (s + 1) * inner]),
                ],
                2,
            )
            for s in range(2)
        ),
        c, t, x, y, outer,
    )
    qkv_sum = attn_sum[:, :, :q_rows].reshape(depth, width).T
    proj_sum = attn_sum[:, :, q_rows:].reshape(inner, width)

    unit, inverse = normal(inputs.astype(F32))
    first_grad = own(first_part).astype(F32) + own(exchange(first_part)).astype(F32)
    scaled = first_grad * attn_gain
    mean_one = jnp.mean(scaled, axis=-1, keepdims=True)
    mean_two = jnp.mean(scaled * unit, axis=-1, keepdims=True)
    grad_in = own(middle_grad) + (scaled - mean_one - unit * mean_two) * inverse
    low_in = lax.ppermute(grad_in.astype(BF16), CORE_T, ROW_SWAP)
    patches_grad = jnp.where(stays, grad_in, low_in.astype(F32))

    bias_place = jnp.zeros((2, 2, units), F32)
    bias_place = lax.dynamic_update_slice_in_dim(
        bias_place, bias_grad.reshape(1, 2, units), c, 0
    ).reshape(4, units)
    sums = jnp.concatenate(
        [
            jnp.sum(first_grad * unit, axis=0, keepdims=True),
            jnp.sum(first_grad, axis=0, keepdims=True),
            mlp_sums * 0.5,
            bias_place,
        ],
        0,
    )
    for name in ("c", "x", "y"):
        sums = sums + lax.ppermute(sums, name, SWAP)
    for bit in (1, 2):
        sums = sums + lax.ppermute(sums, "t", [(i, i ^ bit) for i in range(4)])
    if outer > 1:
        sums = lax.psum(sums, "o")
    up_bias_sum = lax.dynamic_index_in_dim(sums, 4 + t, 0, keepdims=False)
    return (
        result,
        patches_grad,
        sums[0],
        sums[1],
        qkv_sum.astype(F32),
        proj_sum.astype(F32),
        sums[2],
        sums[3],
        up_sum.astype(F32),
        up_bias_sum,
        down_sum.astype(F32),
    )


def solution(mesh):
    dp, tensor = mesh.shape["dp"], mesh.shape["tensor"]
    grid = Mesh(mesh.devices.reshape(dp // 8, 2, 2, 2, tensor), ("o", "y", "x", "c", "t"))
    dp_axes = ("o", "y", "x", "c")
    rows = P(dp_axes + ("t",), None)
    return jax.shard_map(
        local,
        mesh=grid,
        in_specs=(
            rows,
            P(dp_axes, None),
            P(),
            P(),
            P(None, "t"),
            P("t", None),
            P(),
            P(),
            P(None, "t"),
            P("t"),
            P("t", None),
            rows,
        ),
        out_specs=(
            rows,
            rows,
            P(),
            P(),
            P(None, "t"),
            P("t", None),
            P(),
            P(),
            P(None, "t"),
            P("t"),
            P("t", None),
        ),
        check_vma=False,
    )
```

```python
import jax
import jax.numpy as jnp
from jax import lax
from jax.experimental import pallas as pl
from jax.experimental.pallas import tpu as pltpu
from jax.sharding import Mesh
from jax.sharding import PartitionSpec as P

HEAD_DIM = 64
BLOCK = 784
NORM_EPS = 1e-06
SCALE = HEAD_DIM**-0.5
LOG2E = 1.4426950408889634
F32 = jnp.float32
BF16 = jnp.bfloat16
VMEM_LIMIT = 58 * 1024 * 1024
SWAP = [(0, 1), (1, 0)]
TILE = 256
PAD = 16

CORE_T = ("c", "t")
ROUND_ONE = [(0, 1), (4, 2), (1, 0), (5, 3), (6, 7), (2, 5), (7, 6), (3, 4)]
ROUND_TWO = [(4, 3), (5, 2), (2, 4), (3, 5), (0, 7), (1, 6), (6, 0), (7, 1)]
ROUND_ONE_BACK = [(b, a) for a, b in ROUND_ONE]
ROUND_TWO_BACK = [(3, 4), (2, 5), (4, 2), (5, 3), (0, 0), (1, 1), (6, 6), (7, 7)]
ROW_SWAP = [(4, 1), (1, 4), (6, 3), (3, 6), (0, 0), (2, 2), (5, 5), (7, 7)]
LAYER = ("y", "x", "c")
FIRST = [(i, i ^ (4 if i & 1 else 2)) for i in range(8)]
SECOND = [(i, i ^ (2 if i & 1 else 4)) for i in range(8)]
BOTH = [(i, i ^ 6) for i in range(8)]


def dot(left, right, left_dim=1, right_dim=0):
    return lax.dot_general(
        left, right, (((left_dim,), (right_dim,)), ((), ())), preferred_element_type=F32
    )


def normal(rows):
    centre = rows - jnp.mean(rows, axis=-1, keepdims=True)
    spread = jnp.mean(centre * centre, axis=-1, keepdims=True)
    inverse = lax.rsqrt(spread + NORM_EPS)
    return centre * inverse, inverse


def row_labels(ends_ref, first, shape, dim):
    places = lax.broadcasted_iota(jnp.int32, shape, dim) + first
    labels = jnp.zeros(shape, jnp.int32)
    for slot in range(ends_ref.shape[0]):
        labels = labels + (places >= ends_ref[slot]).astype(jnp.int32)
    return labels


def chunks_of(rows):
    edges = [256 * i for i in range(rows // 256 + 1)]
    edges[-1] = rows
    return list(zip(edges[:-1], edges[1:]))


def smem(count):
    return [pl.BlockSpec(memory_space=pltpu.SMEM)] * count


def vmem(count):
    return [pl.BlockSpec(memory_space=pltpu.VMEM)] * count


def anywhere(count):
    return [pl.BlockSpec(memory_space=pl.ANY)] * count


def settings():
    return dict(
        compiler_params=pltpu.CompilerParams(vmem_limit_bytes=VMEM_LIMIT),
        cost_estimate=pl.CostEstimate(
            flops=int(1e9), bytes_accessed=int(1e6), transcendentals=0
        ),
    )


def heads_forward(labels, normed_ref, w_ref, packed_ref, heads_ref, base_head, lse_ref):
    rows = normed_ref.shape[0]
    label_col, label_row = labels

    def head(h, carry):
        part = pl.ds(pl.multiple_of(h * 3 * HEAD_DIM, 3 * HEAD_DIM), 3 * HEAD_DIM)
        packed = dot(w_ref[part, :], normed_ref[...], 1, 1).astype(BF16)
        packed_ref[part, :] = packed
        queries = packed[:HEAD_DIM] * SCALE
        key_rows = packed[HEAD_DIM : 2 * HEAD_DIM].T
        values = packed[2 * HEAD_DIM :]
        place = pl.ds(pl.multiple_of((h + base_head) * HEAD_DIM, HEAD_DIM), HEAD_DIM)
        for a, b in chunks_of(rows):
            scores = dot(key_rows, queries[:, a:b]) * LOG2E
            scores = jnp.where(label_col == label_row[:, a:b], scores, -1e30)
            top = jnp.max(scores, axis=0, keepdims=True)
            weights = jnp.exp2(scores - top)
            total = jnp.sum(weights, axis=0, keepdims=True)
            mixed = dot(values, weights.astype(BF16)) * (1.0 / total)
            heads_ref[place, a:b] = mixed.astype(BF16)
            lse_ref[pl.ds(h, 1), a:b] = top + jnp.log2(total)
        return carry

    lax.fori_loop(0, w_ref.shape[0] // (3 * HEAD_DIM), head, 0)


CROSSED = (0, 2, 1, 3)


def place(order_ref, index, rows):
    return pl.ds(pl.multiple_of(order_ref[index] * rows, 16), rows)


def attention_kernel(*refs):
    ends_ref, first_ref, order_ref, x_ref, vectors_ref, own_w_ref, own_proj_ref = refs[:7]
    pieces, crossed_ref, refs = refs[7:11], refs[11], refs[12:]
    normed_ref, mine_ref, heads_ref, proj_ref = refs[:4]
    w_one, packed_one, lse_one, w_two, packed_two, lse_two = refs[4:]
    rows = x_ref.shape[0]
    depth, inner = own_w_ref.shape[0], own_proj_ref.shape[0]
    w_rows, p_rows = depth // 4, inner // 4
    size = w_rows + p_rows
    half = size // 2
    rest = w_rows - half
    for index, piece in enumerate(pieces):
        w_one[place(order_ref, index, w_rows), :] = piece[:w_rows, :]
        proj_ref[place(order_ref, index, p_rows), :] = piece[w_rows:size, :]

    @pl.when(order_ref[4] == 1)
    def _():
        w_two[...] = own_w_ref[...]
        proj_ref[inner:, :] = own_proj_ref[...]

    @pl.when(order_ref[4] == 0)
    def _():
        for index, piece in enumerate(pieces):
            base = pl.multiple_of(order_ref[index] * w_rows, 16)
            w_two[pl.ds(base, half), :] = piece[size:, :]
            start = CROSSED[index] * half
            w_two[pl.ds(base + half, rest), :] = crossed_ref[start : start + rest, :]
            base = pl.multiple_of(order_ref[index] * p_rows + inner, 16)
            proj_ref[pl.ds(base, p_rows), :] = crossed_ref[start + rest : start + half, :]

    unit, _ = normal(x_ref[...].astype(F32))
    normed_ref[...] = (unit * vectors_ref[0:1, :] + vectors_ref[1:2, :]).astype(BF16)
    labels = [row_labels(ends_ref, first_ref[0], shape, dim) for dim, shape in ((0, (rows, 1)), (1, (1, rows)))]
    heads_forward(labels, normed_ref, w_one, packed_one, heads_ref, 0, lse_one)
    heads_forward(labels, normed_ref, w_two, packed_two, heads_ref, inner // HEAD_DIM, lse_two)
    mine_ref[...] = dot(heads_ref[...], proj_ref[...], 0, 0).astype(BF16)


def attention(ends, first, order, x, vectors, own, pieces, crossed):
    rows, width = x.shape
    depth, inner = own[0].shape[0], own[1].shape[0]
    rows_low = jax.ShapeDtypeStruct((rows, width), BF16)
    slot = (
        jax.ShapeDtypeStruct((depth, width), BF16),
        jax.ShapeDtypeStruct((depth, rows), BF16),
        jax.ShapeDtypeStruct((8, rows), F32),
    )
    outs = pl.pallas_call(
        attention_kernel,
        out_shape=(
            rows_low,
            rows_low,
            jax.ShapeDtypeStruct((2 * inner, rows), BF16),
            jax.ShapeDtypeStruct((2 * inner, width), BF16),
        )
        + slot
        + slot,
        in_specs=smem(3) + vmem(9),
        out_specs=tuple(vmem(10)),
        name="attention",
        **settings(),
    )(ends, first, order, x, vectors, *own, *pieces, crossed)
    return outs[:4], outs[4:7], outs[7:]


def feed_slot(places_ref, second, second_t, cot_ref, up, down, bias, grads, out_sum, back_sum, bias_grad):
    width, units = up.shape
    quarter = units // 4

    def step(j, carry):
        columns = pl.ds(pl.multiple_of(j * TILE, TILE), TILE)
        up_tile = up[:, columns]
        down_tile = down[columns, :]
        pre = dot(second[...], up_tile) + bias[0:1, columns]
        gate = 0.5 * (1.0 + lax.erf(pre * (2.0**-0.5)))
        slope = gate + pre * (
            jnp.exp2(pre * pre * (-0.5 * LOG2E)) * (0.5 / 3.141592653589793) ** 0.5
        )
        hidden = (pre * gate).astype(BF16)
        out_sum[...] += dot(hidden, down_tile)
        down_grad = dot(hidden, cot_ref[...], 0, 0).astype(BF16)
        for i in range(TILE // 64):
            chunk = j * (TILE // 64) + i
            start = width // 4 + lax.rem(chunk, quarter // 64) * 64
            grads[places_ref[lax.div(chunk, quarter // 64)], pl.ds(pl.multiple_of(start, 64), 64), :] = down_grad[i * 64 : (i + 1) * 64]
        act = (dot(cot_ref[...], down_tile, 1, 1) * slope).astype(BF16)
        bias_grad[:, columns] = jnp.sum(act.astype(F32), axis=0, keepdims=True)
        back_sum[...] += dot(act, up_tile, 1, 1)
        up_grad = dot(second_t[...], act).astype(BF16)
        for i in range(4):
            size = width // 4
            grads[places_ref[i], 0:size, columns] = up_grad[i * size : (i + 1) * size]
        return carry

    lax.fori_loop(0, units // TILE, step, 0)


def feed_kernel(*refs):
    order_ref, places_ref, x_ref, mine_ref, other_ref, cot_ref, vectors_ref = refs[:7]
    own_up_ref, own_down_ref, own_bias_ref, pieces, crossed_ref, refs = (
        refs[7], refs[8], refs[9], refs[10:14], refs[14], refs[15:],
    )
    middle_ref, out_ref, back_ref, bias_one, bias_two, send_ref, keep_ref = refs[:7]
    second, second_t, up, down, bias, grads, out_sum, back_sum, sems = refs[7:]
    width, units = up.shape
    u_rows, d_rows = width // 4, units // 4
    size = u_rows + d_rows + PAD
    half = crossed_ref.shape[0] // 4
    for index, piece in enumerate(pieces):
        up[place(order_ref, index, u_rows), :] = piece[:u_rows, :]
        down[place(order_ref, index, d_rows), :] = piece[u_rows : u_rows + d_rows, :]
    bias[...] = pieces[0][size - PAD : size, :].astype(F32)
    middle = x_ref[...].astype(F32) + (mine_ref[...].astype(F32) + other_ref[...].astype(F32))
    middle_ref[...] = middle
    unit, _ = normal(middle)
    low = (unit * vectors_ref[2:3, :] + vectors_ref[3:4, :]).astype(BF16)
    second[...] = low
    second_t[...] = low.T
    out_sum[...] = jnp.zeros_like(out_sum)
    back_sum[...] = jnp.zeros_like(back_sum)
    copies = [
        pltpu.make_async_copy(grads.at[slot, pl.ds(2 * part, 2)], ref.at[slot], sems.at[2 * slot + part])
        for slot in range(2)
        for part, ref in ((0, send_ref), (1, keep_ref))
    ]
    feed_slot(places_ref, second, second_t, cot_ref, up, down, bias, grads.at[0], out_sum, back_sum, bias_one)
    copies[0].start()
    copies[1].start()

    @pl.when(order_ref[4] == 1)
    def _():
        up[...] = own_up_ref[...]
        down[...] = own_down_ref[...]
        bias[...] = own_bias_ref[...].astype(F32)

    @pl.when(order_ref[4] == 0)
    def _():
        for index, piece in enumerate(pieces):
            up[place(order_ref, index, u_rows), :] = piece[size : size + u_rows, :]
            start = CROSSED[index] * half
            down[place(order_ref, index, d_rows), :] = crossed_ref[start : start + d_rows, :]
        bias[...] = pieces[0][size + u_rows : size + u_rows + PAD, :].astype(F32)

    feed_slot(places_ref, second, second_t, cot_ref, up, down, bias, grads.at[1], out_sum, back_sum, bias_two)
    copies[2].start()
    copies[3].start()
    out_ref[...] = out_sum[...].astype(BF16)
    back_ref[...] = back_sum[...].astype(BF16)
    for copy in copies:
        copy.wait()


def feed(order, places, x, mine, other, cot, vectors, own, pieces, crossed):
    rows, width = x.shape
    units = own[1].shape[0]
    size = (width + units) // 4
    rows_low = jax.ShapeDtypeStruct((rows, width), BF16)
    rows_full = jax.ShapeDtypeStruct((rows, width), F32)
    half = jax.ShapeDtypeStruct((2, 2, size, width), BF16)
    bias_grad = jax.ShapeDtypeStruct((1, units), F32)
    return pl.pallas_call(
        feed_kernel,
        out_shape=(rows_full, rows_low, rows_low, bias_grad, bias_grad, half, half),
        in_specs=smem(2) + vmem(13),
        out_specs=tuple(vmem(5) + anywhere(2)),
        scratch_shapes=[
            pltpu.VMEM((rows, width), BF16),
            pltpu.VMEM((width, rows), BF16),
            pltpu.VMEM((width, units), BF16),
            pltpu.VMEM((units, width), BF16),
            pltpu.VMEM((PAD, units), F32),
            pltpu.VMEM((2, 4, size, width), BF16),
            pltpu.VMEM((rows, width), F32),
            pltpu.VMEM((rows, width), F32),
            pltpu.SemaphoreType.DMA((4,)),
        ],
        name="feed",
        **settings(),
    )(order, places, x, mine, other, cot, vectors, *own, *pieces, crossed)


def heads_back(slot, labels, places_ref, branch_ref, normed_ref, w_ref, proj_ref, packed_ref, heads_ref,
               lse_ref, packed_grad, w_grad, grads):
    rows = branch_ref.shape[0]
    depth, inner = w_ref.shape[0], proj_ref.shape[0] // 2
    label_col, label_row = labels

    def head(h, carry):
        base = pl.multiple_of(h * 3 * HEAD_DIM, 3 * HEAD_DIM)
        part = pl.ds(pl.multiple_of(h * HEAD_DIM + slot * inner, HEAD_DIM), HEAD_DIM)
        mixed = heads_ref[part, :]
        mixed_grad = dot(proj_ref[part, :], branch_ref[...], 1, 1).astype(BF16)
        packed = packed_ref[pl.ds(base, 3 * HEAD_DIM), :]
        queries = packed[:HEAD_DIM] * SCALE
        keys = packed[HEAD_DIM : 2 * HEAD_DIM]
        key_rows = keys.T
        value_rows = packed[2 * HEAD_DIM :].T
        inner_sum = jnp.sum(mixed.astype(F32) * mixed_grad.astype(F32), axis=0, keepdims=True)
        key_grad = jnp.zeros((HEAD_DIM, rows), F32)
        value_grad = jnp.zeros((HEAD_DIM, rows), F32)
        for a, b in chunks_of(rows):
            scores = dot(key_rows, queries[:, a:b]) * LOG2E
            scores = jnp.where(label_col == label_row[:, a:b], scores, -1e30)
            prob = jnp.exp2(scores - lse_ref[pl.ds(h, 1), a:b])
            value_grad += dot(mixed_grad[:, a:b], prob.astype(BF16), 1, 1)
            prob_grad = dot(value_rows, mixed_grad[:, a:b])
            score_grad = (prob * (prob_grad - inner_sum[:, a:b])).astype(BF16)
            packed_grad[pl.ds(base, HEAD_DIM), a:b] = (dot(keys, score_grad) * SCALE).astype(BF16)
            key_grad += dot(queries[:, a:b], score_grad, 1, 1)
        packed_grad[pl.ds(base + HEAD_DIM, HEAD_DIM), :] = key_grad.astype(BF16)
        packed_grad[pl.ds(base + 2 * HEAD_DIM, HEAD_DIM), :] = value_grad.astype(BF16)
        return carry

    lax.fori_loop(0, depth // (3 * HEAD_DIM), head, 0)
    w_grad[:depth, :] = dot(packed_grad[...], normed_ref[...]).astype(BF16)
    w_grad[depth:, :] = dot(heads_ref[slot * inner : (slot + 1) * inner, :], branch_ref[...]).astype(BF16)
    w_size, p_size = depth // 4, inner // 4
    size = w_size + p_size
    for i in range(4):
        grads[places_ref[i], PAD : PAD + w_size, :] = w_grad[i * w_size : (i + 1) * w_size, :]
        grads[places_ref[i], PAD + w_size : PAD + size, :] = w_grad[depth + i * p_size : depth + (i + 1) * p_size, :]


def send_grads(grads, start, out_refs, sems):
    copies = [
        pltpu.make_async_copy(grads.at[i, pl.ds(start, grads.shape[1] - start)], out_ref, sems.at[i])
        for i, out_ref in enumerate(out_refs)
    ]
    for copy in copies:
        copy.start()
    for copy in copies:
        copy.wait()


def back_one_kernel(
    ends_ref,
    first_ref,
    places_ref,
    middle_ref,
    mine_ref,
    other_ref,
    cot_ref,
    vectors_ref,
    normed_ref,
    heads_ref,
    proj_ref,
    w_ref,
    packed_ref,
    lse_ref,
    middle_grad_ref,
    branch_ref,
    sums_ref,
    packed_grad_ref,
    far_ref,
    near_ref,
    side_ref,
    keep_ref,
    w_grad,
    grads,
    sems,
):
    rows = middle_ref.shape[0]
    unit, inverse = normal(middle_ref[...])
    grad = mine_ref[...].astype(F32) + other_ref[...].astype(F32)
    sums_ref[0:1, :] = jnp.sum(grad * unit, axis=0, keepdims=True) * 0.5
    sums_ref[1:2, :] = jnp.sum(grad, axis=0, keepdims=True) * 0.5
    scaled = grad * vectors_ref[2:3, :]
    mean_one = jnp.mean(scaled, axis=-1, keepdims=True)
    mean_two = jnp.mean(scaled * unit, axis=-1, keepdims=True)
    middle_grad = cot_ref[...].astype(F32) + (scaled - mean_one - unit * mean_two) * inverse
    middle_grad_ref[...] = middle_grad
    branch_ref[...] = middle_grad.astype(BF16)
    labels = [row_labels(ends_ref, first_ref[0], shape, dim) for dim, shape in ((0, (rows, 1)), (1, (1, rows)))]
    heads_back(0, labels, places_ref, branch_ref, normed_ref, w_ref, proj_ref, packed_ref, heads_ref,
                        lse_ref, packed_grad_ref, w_grad, grads)
    send_grads(grads, PAD, (far_ref, near_ref, side_ref, keep_ref), sems)


def back_two_kernel(
    ends_ref,
    first_ref,
    places_ref,
    branch_ref,
    x_ref,
    normed_ref,
    heads_ref,
    proj_ref,
    packed_grad_one_ref,
    w_one_ref,
    w_ref,
    packed_ref,
    lse_ref,
    sums_ref,
    first_grad_ref,
    far_ref,
    near_ref,
    side_ref,
    keep_ref,
    packed_grad,
    w_grad,
    grads,
    sems,
):
    rows = branch_ref.shape[0]
    labels = [row_labels(ends_ref, first_ref[0], shape, dim) for dim, shape in ((0, (rows, 1)), (1, (1, rows)))]
    heads_back(1, labels, places_ref, branch_ref, normed_ref, w_ref, proj_ref, packed_ref, heads_ref,
                        lse_ref, packed_grad, w_grad, grads)
    grad = dot(packed_grad_one_ref[...], w_one_ref[...], 0, 0) + dot(
        packed_grad[...], w_ref[...], 0, 0
    )
    first_grad_ref[...] = grad.astype(BF16)
    unit, _ = normal(x_ref[...].astype(F32))
    sums = [jnp.sum(grad * unit, axis=0, keepdims=True), jnp.sum(grad, axis=0, keepdims=True)]
    for i in range(4):
        pair = sums if i == 0 else [sums_ref[2 * i - 2 : 2 * i - 1, :], sums_ref[2 * i - 1 : 2 * i, :]]
        lines = lax.broadcasted_iota(jnp.int32, (PAD, grads.shape[2]), 0)
        grads[places_ref[i], :PAD, :] = jnp.where(
            lines == 0, pair[0], jnp.where(lines == 1, pair[1], 0.0)
        ).astype(BF16)
    send_grads(grads, 0, (far_ref, near_ref, side_ref, keep_ref), sems)


def back_scratch(depth, inner, width):
    return [
        pltpu.VMEM((depth + inner, width), BF16),
        pltpu.VMEM((4, PAD + (depth + inner) // 4, width), BF16),
        pltpu.SemaphoreType.DMA((4,)),
    ]


def back_one(ends, first, places, middle, mine, other, cot, vectors, shared, slot):
    rows, width = middle.shape
    depth, inner = slot[0].shape[0], shared[2].shape[0] // 2
    part = jax.ShapeDtypeStruct(((depth + inner) // 4, width), BF16)
    outs = pl.pallas_call(
        back_one_kernel,
        out_shape=(
            jax.ShapeDtypeStruct((rows, width), F32),
            jax.ShapeDtypeStruct((rows, width), BF16),
            jax.ShapeDtypeStruct((2, width), F32),
            jax.ShapeDtypeStruct((depth, rows), BF16),
            part,
            part,
            part,
            part,
        ),
        in_specs=smem(3) + vmem(11),
        out_specs=tuple(vmem(4) + anywhere(4)),
        scratch_shapes=back_scratch(depth, inner, width),
        name="back_one",
        **settings(),
    )(ends, first, places, middle, mine, other, cot, vectors, *shared, *slot)
    return outs[:4], outs[4:]


def back_two(ends, first, places, branch, x, shared, grad_one, w_one, slot, sums):
    rows, width = branch.shape
    depth, inner = slot[0].shape[0], shared[2].shape[0] // 2
    part = jax.ShapeDtypeStruct(((depth + inner) // 4 + PAD, width), BF16)
    outs = pl.pallas_call(
        back_two_kernel,
        out_shape=(
            jax.ShapeDtypeStruct((rows, width), BF16),
            part,
            part,
            part,
            part,
        ),
        in_specs=smem(3) + vmem(11),
        out_specs=tuple(vmem(1) + anywhere(4)),
        scratch_shapes=[pltpu.VMEM((depth, rows), BF16)] + back_scratch(depth, inner, width),
        name="back_two",
        **settings(),
    )(ends, first, places, branch, x, *shared, grad_one, w_one, *slot, sums)
    return outs[0], outs[1:]


def settle_kernel(order_ref, *refs):
    pieces, others_ref, far_ref, refs = refs[:4], refs[4], refs[5], refs[6:]
    up_ref, down_ref, qkv_ref, proj_ref, sums_ref = refs
    feed_rows = up_ref.shape[0] // 4
    qkv_rows, proj_rows = qkv_ref.shape[0] // 4, proj_ref.shape[0] // 4
    size = pieces[0].shape[0]
    early = size - feed_rows - PAD
    late = qkv_rows - early

    def put(out, index, rows, offset, count, value):
        start = pl.multiple_of(order_ref[index] * rows + offset, 8)
        out[pl.ds(start, count), :] = value.astype(F32)

    def first_half(index, ref, base):
        put(up_ref, index, feed_rows, 0, feed_rows, ref[base : base + feed_rows, :])
        base = base + feed_rows
        put(sums_ref, index, PAD, 0, PAD, ref[base : base + PAD, :])
        put(qkv_ref, index, qkv_rows, 0, early, ref[base + PAD : base + PAD + early, :])

    def second_half(index, ref, base):
        put(down_ref, index, feed_rows, 0, feed_rows, ref[base : base + feed_rows, :])
        base = base + feed_rows
        put(qkv_ref, index, qkv_rows, early, late, ref[base : base + late, :])
        base = base + late
        put(proj_ref, index, proj_rows, 0, proj_rows, ref[base : base + proj_rows, :])

    halves = (first_half, second_half)
    for core in range(2):

        @pl.when(order_ref[5] == core)
        def _():
            for index, piece in enumerate(pieces):
                halves[core](index, piece, 0)
                if index < 3:
                    halves[1 - core](index, others_ref, CROSSED[index] * size)
            halves[1 - core](3, far_ref, 0)


def settle(order, pieces, others, other_far, width, units, depth, inner):
    return pl.pallas_call(
        settle_kernel,
        out_shape=(
            jax.ShapeDtypeStruct((width, units), F32),
            jax.ShapeDtypeStruct((units, width), F32),
            jax.ShapeDtypeStruct((depth, width), F32),
            jax.ShapeDtypeStruct((inner, width), F32),
            jax.ShapeDtypeStruct((4 * PAD, width), F32),
        ),
        in_specs=smem(1) + vmem(6),
        out_specs=tuple(vmem(5)),
        name="settle",
        **settings(),
    )(order, *pieces, others, other_far)


def spread(piece, *before):
    near = lax.ppermute(piece, LAYER, FIRST)
    side = lax.ppermute(piece, LAYER, SECOND)
    far = lax.ppermute(after(near, side, *before) if before else near, LAYER, SECOND)
    return piece, near, side, far


def scatter_at_once(far, near, side, keep):
    return keep, tuple(
        lax.ppermute(part, LAYER, pairs)
        for part, pairs in ((near, FIRST), (side, SECOND), (far, BOTH))
    )


def add_low(*parts):
    total = parts[0].astype(F32)
    for part in parts[1:]:
        total = total + part.astype(F32)
    return total.astype(BF16)


def to_shard(sum_one, sum_two):
    return (
        lax.ppermute(sum_one, CORE_T, ROUND_ONE_BACK),
        lax.ppermute(sum_two, CORE_T, ROUND_TWO_BACK),
    )


def over_outer(share, outer):
    return lax.psum(share.astype(F32), "o").astype(BF16) if outer > 1 else share


def half_rows(parts, place):
    rows = parts[0].shape[0] // 2
    return add_low(*(lax.dynamic_slice_in_dim(part, place * rows, rows, 0) for part in parts))


def after(value, *others):
    return lax.optimization_barrier((value,) + others)[0] if others else value


def local(
    patches,
    item_patches,
    attn_gain,
    attn_bias,
    qkv_weight,
    proj_weight,
    mlp_gain,
    mlp_bias,
    up_weight,
    up_bias,
    down_weight,
    cotangent,
):
    c, t, x, y = (lax.axis_index(name) for name in ("c", "t", "x", "y"))
    outer = lax.axis_size("o")
    quarter = 2 * y + x
    member = t & 1
    own_rows, width = patches.shape
    first_bit = 1 + c
    home = (t // 2 == c).astype(jnp.int32)
    order = jnp.stack([quarter, quarter ^ first_bit, quarter ^ (3 - first_bit), quarter ^ 3, home, c])
    steps = jnp.arange(4) ^ quarter
    places = jnp.where(
        steps == 3, 0, jnp.where(steps == first_bit, 1, jnp.where(steps == 0, 3, 2))
    )

    def exchange(array):
        return lax.ppermute(array, "c", SWAP)

    def both_halves(array, *before):
        other = exchange(after(array, *before))
        return jnp.where(
            c == 0, jnp.concatenate([array, other], 0), jnp.concatenate([other, array], 0)
        )

    def cut(array):
        rows = array.shape[0] // 4
        return lax.dynamic_slice_in_dim(array, quarter * rows, rows, 0)

    qkv_t = qkv_weight.T
    depth, units, inner = qkv_t.shape[0], down_weight.shape[0], proj_weight.shape[0]
    piece_a = jnp.concatenate([cut(qkv_t), cut(proj_weight)], 0)
    half_a = piece_a.shape[0] // 2
    piece_a_two = lax.dynamic_slice_in_dim(piece_a, home * half_a, half_a, 0)
    piece_a, piece_a_two, patches = lax.optimization_barrier((piece_a, piece_a_two, patches))
    a_one = lax.ppermute(piece_a, CORE_T, ROUND_ONE)
    a_two = lax.ppermute(piece_a_two, CORE_T, ROUND_TWO)
    inputs = lax.ppermute(patches, CORE_T, ROW_SWAP)
    items = exchange(item_patches)
    ends = jnp.cumsum(jnp.where(member == c, item_patches, items)[0])
    first = (t // 2 * BLOCK).astype(jnp.int32).reshape(1)
    vectors = jnp.stack([attn_gain, attn_bias, mlp_gain, mlp_bias])
    bias_rows = jnp.broadcast_to(up_bias[None, :], (PAD, units))
    cut_up, cut_down = cut(up_weight), cut(down_weight)
    piece_b = jnp.concatenate([cut_up, cut_down, bias_rows], 0)
    half_b = jnp.concatenate([jnp.where(home == 1, cut_down, cut_up), bias_rows], 0)
    block_in = both_halves(inputs)
    a_one, a_two, block_in, ends, first, order, places, vectors, piece_b, half_b, bias_rows = (
        lax.optimization_barrier(
            (a_one, a_two, block_in, ends, first, order, places, vectors, piece_b, half_b, bias_rows)
        )
    )
    b_one = lax.ppermute(piece_b, CORE_T, ROUND_ONE)
    b_two = lax.ppermute(half_b, CORE_T, ROUND_TWO)
    pieces_a = spread(jnp.concatenate([a_one, a_two], 0))
    crossed_a = lax.ppermute(
        jnp.concatenate([piece[2 * half_a :] for piece in pieces_a], 0), "c", SWAP
    )
    both_b = jnp.concatenate([b_one, b_two], 0)
    shared, one, two = attention(
        ends, first, order, after(block_in, both_b), vectors, (qkv_t, proj_weight), pieces_a, crossed_a
    )
    normed, mine, heads_out, proj = shared
    shared = (normed, heads_out, proj)
    pieces_b = spread(both_b, mine)
    other = exchange(mine)
    block_cot = both_halves(lax.ppermute(after(cotangent, both_b), CORE_T, ROW_SWAP), mine)
    pieces_b, other, block_cot = lax.optimization_barrier((pieces_b, other, block_cot))
    crossed_b = lax.ppermute(
        jnp.concatenate([piece[piece_b.shape[0] :] for piece in pieces_b], 0), "c", SWAP
    )
    middle, out_part, back_part, bias_one, bias_two, send, keep = feed(
        order, places, block_in, mine, other, block_cot, vectors,
        (up_weight, down_weight, bias_rows), pieces_b, crossed_b,
    )
    hop = lax.ppermute(send, LAYER, FIRST)

    def own(array):
        return lax.dynamic_slice_in_dim(array, c * own_rows, own_rows, 0)

    (middle_grad, branch, mlp_sums, grad_one), back_one_out = back_one(
        ends, first, places, middle, back_part, exchange(back_part), block_cot, vectors, shared, one
    )
    hop = after(hop, branch)
    next_hop = add_low(keep[:, 0], hop[:, 0])
    far = lax.ppermute(next_hop, LAYER, SECOND)
    keep_one, got_one = scatter_at_once(*back_one_out)
    slot_one = 2 * c + jnp.where(t // 2 == c, 1 - member, member ^ c)
    shards = jnp.arange(4)[:, None]
    bias_part = jnp.where(shards == slot_one, bias_one, 0.0) + jnp.where(
        shards == (slot_one ^ 1), bias_two, 0.0
    )
    small = jnp.concatenate([mlp_sums, bias_part], 0)
    first_part, back_two_out = back_two(
        ends, first, places, after(branch, next_hop), block_in, shared, grad_one, one[0], two, small
    )
    feed_sums = [add_low(keep[i, 1], hop[i, 1], part) for i, part in enumerate(after(far, first_part))]
    feed_parts = to_shard(*feed_sums)
    keep_one, back_two_out, first_part, out_part, _ = lax.optimization_barrier(
        (keep_one, back_two_out, first_part, out_part, feed_sums)
    )
    keep_two, got_two = scatter_at_once(*back_two_out)

    unit, inverse = normal(inputs.astype(F32))
    first_grad = own(first_part).astype(F32) + own(exchange(first_part)).astype(F32)
    scaled = first_grad * attn_gain
    mean_one = jnp.mean(scaled, axis=-1, keepdims=True)
    mean_two = jnp.mean(scaled * unit, axis=-1, keepdims=True)
    grad_in = own(middle_grad) + (scaled - mean_one - unit * mean_two) * inverse
    grad_in = grad_in.astype(BF16)
    result = own(middle) + own(out_part).astype(F32) + own(exchange(out_part)).astype(F32)
    result = result.astype(BF16)
    got_one, got_two = after((got_one, got_two), feed_parts)
    back_sum_two = add_low(keep_two, *got_two)
    small = add_low(back_sum_two[:PAD], exchange(back_sum_two[:PAD]))
    blank = jnp.zeros((PAD, width), BF16)
    back_sum_one = jnp.concatenate([small, add_low(keep_one, *got_one), blank], 0)
    back_sum_two = jnp.concatenate([small, back_sum_two[PAD:], blank], 0)
    back_parts = to_shard(back_sum_one, back_sum_two)
    grad_in, result, back_parts = lax.optimization_barrier((grad_in, result, back_parts))
    patches_grad = lax.ppermute(grad_in, CORE_T, ROW_SWAP).astype(F32)
    result = lax.ppermute(result, CORE_T, ROW_SWAP)

    def halves(place):
        return jnp.concatenate([half_rows(feed_parts, place), half_rows(back_parts, place)], 0)

    share = add_low(halves(c), exchange(halves(1 - c)))
    share = over_outer(share, outer)
    pieces = spread(share)
    up_sum, down_sum, qkv_sum, proj_sum, sums = settle(
        order, pieces, exchange(jnp.concatenate(pieces[:3], 0)), exchange(pieces[3]), width, units, depth, inner
    )
    sums = sums.reshape(4, PAD, width)[:, :2].reshape(8, width)
    up_bias_sum = lax.dynamic_index_in_dim(sums, 4 + t, 0, keepdims=False)
    return (
        result,
        patches_grad,
        sums[0],
        sums[1],
        qkv_sum.T,
        proj_sum,
        sums[2],
        sums[3],
        up_sum,
        up_bias_sum,
        down_sum,
    )


def solution(mesh):
    dp, tensor = mesh.shape["dp"], mesh.shape["tensor"]
    grid = Mesh(mesh.devices.reshape(dp // 8, 2, 2, 2, tensor), ("o", "y", "x", "c", "t"))
    dp_axes = ("o", "y", "x", "c")
    rows = P(dp_axes + ("t",), None)
    return jax.shard_map(
        local,
        mesh=grid,
        in_specs=(
            rows,
            P(dp_axes, None),
            P(),
            P(),
            P(None, "t"),
            P("t", None),
            P(),
            P(),
            P(None, "t"),
            P("t"),
            P("t", None),
            rows,
        ),
        out_specs=(
            rows,
            rows,
            P(),
            P(),
            P(None, "t"),
            P("t", None),
            P(),
            P(),
            P(None, "t"),
            P("t"),
            P("t", None),
        ),
        check_vma=False,
    )
```

```python
import jax
import jax.numpy as jnp
from jax import lax
from jax.experimental import pallas as pl
from jax.experimental.pallas import tpu as pltpu
from jax.sharding import Mesh
from jax.sharding import PartitionSpec as P

HEAD_DIM = 64
BLOCK = 784
NORM_EPS = 1e-06
SCALE = HEAD_DIM**-0.5
LOG2E = 1.4426950408889634
F32 = jnp.float32
BF16 = jnp.bfloat16
VMEM_LIMIT = 58 * 1024 * 1024
SWAP = [(0, 1), (1, 0)]
TILE = 768
PAD = 16

CORE_T = ("c", "t")
ROUND_ONE = [(0, 1), (4, 2), (1, 0), (5, 3), (6, 7), (2, 5), (7, 6), (3, 4)]
ROUND_TWO = [(4, 3), (5, 2), (2, 4), (3, 5), (0, 7), (1, 6), (6, 0), (7, 1)]
ROUND_ONE_BACK = [(b, a) for a, b in ROUND_ONE]
ROUND_TWO_BACK = [(3, 4), (2, 5), (4, 2), (5, 3), (0, 0), (1, 1), (6, 6), (7, 7)]
ROW_SWAP = [(4, 1), (1, 4), (6, 3), (3, 6), (0, 0), (2, 2), (5, 5), (7, 7)]
LAYER = ("y", "x", "c")
FIRST = [(i, i ^ (4 if i & 1 else 2)) for i in range(8)]
SECOND = [(i, i ^ (2 if i & 1 else 4)) for i in range(8)]
BOTH = [(i, i ^ 6) for i in range(8)]


def dot(left, right, left_dim=1, right_dim=0):
    return lax.dot_general(
        left, right, (((left_dim,), (right_dim,)), ((), ())), preferred_element_type=F32
    )


def normal(rows):
    centre = rows - jnp.mean(rows, axis=-1, keepdims=True)
    spread = jnp.mean(centre * centre, axis=-1, keepdims=True)
    inverse = lax.rsqrt(spread + NORM_EPS)
    return centre * inverse, inverse


def row_labels(ends_ref, first, shape, dim):
    places = lax.broadcasted_iota(jnp.int32, shape, dim) + first
    labels = jnp.zeros(shape, jnp.int32)
    for slot in range(ends_ref.shape[0]):
        labels = labels + (places >= ends_ref[slot]).astype(jnp.int32)
    return labels


def smem(count):
    return [pl.BlockSpec(memory_space=pltpu.SMEM)] * count


def vmem(count):
    return [pl.BlockSpec(memory_space=pltpu.VMEM)] * count


def anywhere(count):
    return [pl.BlockSpec(memory_space=pl.ANY)] * count


def settings():
    return dict(
        compiler_params=pltpu.CompilerParams(vmem_limit_bytes=VMEM_LIMIT),
        cost_estimate=pl.CostEstimate(
            flops=int(1e9), bytes_accessed=int(1e6), transcendentals=0
        ),
    )


def heads_forward(labels, normed_ref, w_ref, packed_ref, heads_ref, base_head, lse_ref):
    rows = normed_ref.shape[0]
    label_col, label_row = labels

    def head(h):
        part = slice(h * 3 * HEAD_DIM, (h + 1) * 3 * HEAD_DIM)
        packed = dot(w_ref[part, :], normed_ref[...], 1, 1).astype(BF16)
        packed_ref[part, :] = packed
        queries = packed[:HEAD_DIM] * SCALE
        key_rows = packed[HEAD_DIM : 2 * HEAD_DIM].T
        values = packed[2 * HEAD_DIM :]
        scores = dot(key_rows, queries) * LOG2E
        scores = jnp.where(label_col == label_row, scores, -1e30)
        top = jnp.max(scores, axis=0, keepdims=True)
        weights = jnp.exp2(scores - top)
        total = jnp.sum(weights, axis=0, keepdims=True)
        mixed = dot(values, weights.astype(BF16)) * (1.0 / total)
        start = (h + base_head) * HEAD_DIM
        heads_ref[start : start + HEAD_DIM, :] = mixed.astype(BF16)
        lse_ref[h : h + 1, :] = top + jnp.log2(total)

    for h in range(w_ref.shape[0] // (3 * HEAD_DIM)):
        head(h)


CROSSED = (0, 2, 1, 3)


def place(order_ref, index, rows):
    return pl.ds(pl.multiple_of(order_ref[index] * rows, 16), rows)


def attention_kernel(*refs):
    ends_ref, first_ref, order_ref, x_ref, vectors_ref, own_w_ref, own_proj_ref = refs[:7]
    pieces, crossed_ref, refs = refs[7:11], refs[11], refs[12:]
    normed_ref, mine_ref, heads_ref, proj_ref = refs[:4]
    w_one, packed_one, lse_one, w_two, packed_two, lse_two = refs[4:]
    rows = x_ref.shape[0]
    depth, inner = own_w_ref.shape[0], own_proj_ref.shape[0]
    w_rows, p_rows = depth // 4, inner // 4
    size = w_rows + p_rows
    half = size // 2
    rest = w_rows - half
    for index, piece in enumerate(pieces):
        w_one[place(order_ref, index, w_rows), :] = piece[:w_rows, :]
        proj_ref[place(order_ref, index, p_rows), :] = piece[w_rows:size, :]

    @pl.when(order_ref[4] == 1)
    def _():
        w_two[...] = own_w_ref[...]
        proj_ref[inner:, :] = own_proj_ref[...]

    @pl.when(order_ref[4] == 0)
    def _():
        for index, piece in enumerate(pieces):
            base = pl.multiple_of(order_ref[index] * w_rows, 16)
            w_two[pl.ds(base, half), :] = piece[size:, :]
            start = CROSSED[index] * half
            w_two[pl.ds(base + half, rest), :] = crossed_ref[start : start + rest, :]
            base = pl.multiple_of(order_ref[index] * p_rows + inner, 16)
            proj_ref[pl.ds(base, p_rows), :] = crossed_ref[start + rest : start + half, :]

    unit, _ = normal(x_ref[...].astype(F32))
    normed_ref[...] = (unit * vectors_ref[0:1, :] + vectors_ref[1:2, :]).astype(BF16)
    labels = [row_labels(ends_ref, first_ref[0], shape, dim) for dim, shape in ((0, (rows, 1)), (1, (1, rows)))]
    heads_forward(labels, normed_ref, w_one, packed_one, heads_ref, 0, lse_one)
    heads_forward(labels, normed_ref, w_two, packed_two, heads_ref, inner // HEAD_DIM, lse_two)
    mine_ref[...] = dot(heads_ref[...], proj_ref[...], 0, 0).astype(BF16)


def attention(ends, first, order, x, vectors, own, pieces, crossed):
    rows, width = x.shape
    depth, inner = own[0].shape[0], own[1].shape[0]
    rows_low = jax.ShapeDtypeStruct((rows, width), BF16)
    slot = (
        jax.ShapeDtypeStruct((depth, width), BF16),
        jax.ShapeDtypeStruct((depth, rows), BF16),
        jax.ShapeDtypeStruct((8, rows), F32),
    )
    outs = pl.pallas_call(
        attention_kernel,
        out_shape=(
            rows_low,
            rows_low,
            jax.ShapeDtypeStruct((2 * inner, rows), BF16),
            jax.ShapeDtypeStruct((2 * inner, width), BF16),
        )
        + slot
        + slot,
        in_specs=smem(3) + vmem(9),
        out_specs=tuple(vmem(10)),
        name="attention",
        **settings(),
    )(ends, first, order, x, vectors, *own, *pieces, crossed)
    return outs[:4], outs[4:7], outs[7:]


def feed_slot(places_ref, second, second_t, cot_ref, cot_t, up, down, bias, grads, out_sum, back_sum, bias_grad):
    width, units = up.shape
    quarter = units // 4

    def step(j, carry):
        columns = pl.ds(pl.multiple_of(j * TILE, TILE), TILE)
        up_tile = up[:, columns]
        down_tile = down[columns, :]
        pre = dot(second[...], up_tile) + bias[:, columns].astype(F32)[0:1]
        gate = 0.5 * (1.0 + lax.erf(pre * (2.0**-0.5)))
        slope = gate + pre * (
            jnp.exp2(pre * pre * (-0.5 * LOG2E)) * (0.5 / 3.141592653589793) ** 0.5
        )
        hidden = (pre * gate).astype(BF16)
        out_sum[...] += dot(hidden, down_tile)
        down_grad = dot(cot_t[...], hidden).T.astype(BF16)
        for i in range(TILE // 64):
            chunk = j * (TILE // 64) + i
            start = width // 4 + lax.rem(chunk, quarter // 64) * 64
            grads[places_ref[lax.div(chunk, quarter // 64)], pl.ds(pl.multiple_of(start, 64), 64), :] = down_grad[i * 64 : (i + 1) * 64]
        act = (dot(cot_ref[...], down_tile, 1, 1) * slope).astype(BF16)
        bias_grad[:, columns] = jnp.sum(act.astype(F32), axis=0, keepdims=True)
        back_sum[...] += dot(act, up_tile, 1, 1)
        up_grad = dot(second_t[...], act).astype(BF16)
        for i in range(4):
            size = width // 4
            grads[places_ref[i], 0:size, columns] = up_grad[i * size : (i + 1) * size]
        return carry

    lax.fori_loop(0, units // TILE, step, 0)


def fetch(source, target, sem):
    copy = pltpu.make_async_copy(source, target, sem)
    copy.start()
    return copy


def wait_all(copies):
    for copy in copies:
        copy.wait()


def feed_kernel(*refs):
    order_ref, places_ref, vectors_ref, x_hbm, mine_hbm, other_hbm, cot_hbm = refs[:7]
    own_up_hbm, own_down_hbm, own_bias_hbm, pieces, crossed_hbm, far_hbm, refs = (
        refs[7], refs[8], refs[9], refs[10:14], refs[14], refs[15], refs[16:],
    )
    middle_hbm, out_ref, back_ref, bias_one, bias_two, send_ref, keep_ref = refs[:7]
    x_ref, mine_ref, other_ref, cot_ref, middle_ref, second, second_t, cot_t, up, down, bias, grads, out_sum, back_sum, sems = refs[7:]
    _, width, units = up.shape
    u_rows, d_rows = width // 4, units // 4
    size = u_rows + d_rows + PAD
    half = u_rows + PAD
    free = iter(range(40))
    sem = lambda: sems.at[next(free)]
    early = [fetch(*pair, sem()) for pair in ((x_hbm, x_ref), (mine_hbm, mine_ref), (other_hbm, other_ref))]
    first = [fetch(pieces[0].at[pl.ds(size - PAD, PAD)], bias.at[0], sem())]
    for index, piece in enumerate(pieces):
        first.append(fetch(piece.at[pl.ds(0, u_rows)], up.at[0, place(order_ref, index, u_rows)], sem()))
        first.append(fetch(piece.at[pl.ds(u_rows, d_rows)], down.at[0, place(order_ref, index, d_rows)], sem()))
    cot_copy = fetch(cot_hbm, cot_ref, sem())
    home = [
        pltpu.make_async_copy(own_up_hbm, up.at[1], sem()),
        pltpu.make_async_copy(own_down_hbm, down.at[1], sem()),
        pltpu.make_async_copy(own_bias_hbm, bias.at[1], sem()),
    ]
    away = [pltpu.make_async_copy(pieces[0].at[pl.ds(size + u_rows, PAD)], bias.at[1], sem())]
    for index, piece in enumerate(pieces):
        part = piece.at[pl.ds(size, u_rows)]
        away.append(pltpu.make_async_copy(part, up.at[1, place(order_ref, index, u_rows)], sem()))
        part = far_hbm if index == 3 else crossed_hbm.at[pl.ds(CROSSED[index] * half, half)]
        part = part.at[pl.ds(0, d_rows)]
        away.append(pltpu.make_async_copy(part, down.at[1, place(order_ref, index, d_rows)], sem()))

    @pl.when(order_ref[4] == 1)
    def _():
        for copy in home:
            copy.start()

    @pl.when(order_ref[4] == 0)
    def _():
        for copy in away:
            copy.start()

    wait_all(early)
    middle = x_ref[...].astype(F32) + (mine_ref[...].astype(F32) + other_ref[...].astype(F32))
    middle_ref[...] = middle
    late = [fetch(middle_ref, middle_hbm, sem())]
    unit, _ = normal(middle)
    low = (unit * vectors_ref[2:3, :] + vectors_ref[3:4, :]).astype(BF16)
    second[...] = low
    second_t[...] = low.T
    cot_copy.wait()
    cot_t[...] = cot_ref[...].T
    out_sum[...] = jnp.zeros_like(out_sum)
    back_sum[...] = jnp.zeros_like(back_sum)
    wait_all(first)
    leave = lambda slot: [
        fetch(grads.at[slot, pl.ds(2 * part, 2)], ref.at[slot], sem())
        for part, ref in ((0, send_ref), (1, keep_ref))
    ]
    shared = (places_ref, second, second_t, cot_ref, cot_t)
    feed_slot(*shared, up.at[0], down.at[0], bias.at[0], grads.at[0], out_sum, back_sum, bias_one)
    late += leave(0)

    @pl.when(order_ref[4] == 1)
    def _():
        wait_all(home)

    @pl.when(order_ref[4] == 0)
    def _():
        wait_all(away)

    feed_slot(*shared, up.at[1], down.at[1], bias.at[1], grads.at[1], out_sum, back_sum, bias_two)
    late += leave(1)
    out_ref[...] = out_sum[...].astype(BF16)
    back_ref[...] = back_sum[...].astype(BF16)
    wait_all(late)


def feed(order, places, x, mine, other, cot, vectors, own, pieces, crossed, crossed_far):
    rows, width = x.shape
    units = own[1].shape[0]
    size = (width + units) // 4
    rows_low = jax.ShapeDtypeStruct((rows, width), BF16)
    rows_full = jax.ShapeDtypeStruct((rows, width), F32)
    half = jax.ShapeDtypeStruct((2, 2, size, width), BF16)
    bias_grad = jax.ShapeDtypeStruct((1, units), F32)
    return pl.pallas_call(
        feed_kernel,
        out_shape=(rows_full, rows_low, rows_low, bias_grad, bias_grad, half, half),
        in_specs=smem(2) + vmem(1) + anywhere(13),
        out_specs=tuple(anywhere(1) + vmem(4) + anywhere(2)),
        scratch_shapes=[pltpu.VMEM((rows, width), BF16)] * 4
        + [
            pltpu.VMEM((rows, width), F32),
            pltpu.VMEM((rows, width), BF16),
            pltpu.VMEM((width, rows), BF16),
            pltpu.VMEM((width, rows), BF16),
            pltpu.VMEM((2, width, units), BF16),
            pltpu.VMEM((2, units, width), BF16),
            pltpu.VMEM((2, PAD, units), BF16),
            pltpu.VMEM((2, 4, size, width), BF16),
            pltpu.VMEM((rows, width), F32),
            pltpu.VMEM((rows, width), F32),
            pltpu.SemaphoreType.DMA((40,)),
        ],
        name="feed",
        **settings(),
    )(order, places, vectors, x, mine, other, cot, *own, *pieces, crossed, crossed_far)


def heads_back(slot, labels, places_ref, branch_ref, normed_ref, w_ref, proj_ref, packed_ref, heads_ref,
               lse_ref, packed_grad, w_grad, grads):
    rows = branch_ref.shape[0]
    depth, inner = w_ref.shape[0], proj_ref.shape[0] // 2
    label_col, label_row = labels

    def head(h):
        base = h * 3 * HEAD_DIM
        part = slice(h * HEAD_DIM + slot * inner, (h + 1) * HEAD_DIM + slot * inner)
        mixed = heads_ref[part, :]
        mixed_grad = dot(proj_ref[part, :], branch_ref[...], 1, 1).astype(BF16)
        packed = packed_ref[base : base + 3 * HEAD_DIM, :]
        queries = packed[:HEAD_DIM] * SCALE
        keys = packed[HEAD_DIM : 2 * HEAD_DIM]
        key_rows = keys.T
        value_rows = packed[2 * HEAD_DIM :].T
        inner_sum = jnp.sum(mixed.astype(F32) * mixed_grad.astype(F32), axis=0, keepdims=True)
        scores = dot(key_rows, queries) * LOG2E
        scores = jnp.where(label_col == label_row, scores, -1e30)
        prob = jnp.exp2(scores - lse_ref[h : h + 1, :])
        value_grad = dot(mixed_grad, prob.astype(BF16), 1, 1)
        prob_grad = dot(value_rows, mixed_grad)
        score_grad = (prob * (prob_grad - inner_sum)).astype(BF16)
        query_grad = dot(keys, score_grad) * SCALE
        key_grad = dot(queries, score_grad, 1, 1)
        for i, grad in enumerate((query_grad, key_grad, value_grad)):
            start = base + i * HEAD_DIM
            packed_grad[start : start + HEAD_DIM, :] = grad.astype(BF16)

    for h in range(depth // (3 * HEAD_DIM)):
        head(h)
    w_grad[:depth, :] = dot(packed_grad[...], normed_ref[...]).astype(BF16)
    w_grad[depth:, :] = dot(heads_ref[slot * inner : (slot + 1) * inner, :], branch_ref[...]).astype(BF16)
    w_size, p_size = depth // 4, inner // 4
    size = w_size + p_size
    for i in range(4):
        grads[places_ref[i], PAD : PAD + w_size, :] = w_grad[i * w_size : (i + 1) * w_size, :]
        grads[places_ref[i], PAD + w_size : PAD + size, :] = w_grad[depth + i * p_size : depth + (i + 1) * p_size, :]


def send_grads(grads, start, out_refs, sems):
    copies = [
        pltpu.make_async_copy(grads.at[i, pl.ds(start, grads.shape[1] - start)], out_ref, sems.at[i])
        for i, out_ref in enumerate(out_refs)
    ]
    for copy in copies:
        copy.start()
    for copy in copies:
        copy.wait()


def back_one_kernel(
    ends_ref,
    first_ref,
    places_ref,
    middle_ref,
    mine_ref,
    other_ref,
    cot_ref,
    vectors_ref,
    normed_ref,
    heads_ref,
    proj_ref,
    w_ref,
    packed_ref,
    lse_ref,
    middle_grad_ref,
    branch_ref,
    sums_ref,
    packed_grad_ref,
    far_ref,
    near_ref,
    side_ref,
    keep_ref,
    w_grad,
    grads,
    sems,
):
    rows = middle_ref.shape[0]
    unit, inverse = normal(middle_ref[...])
    grad = mine_ref[...].astype(F32) + other_ref[...].astype(F32)
    sums_ref[0:1, :] = jnp.sum(grad * unit, axis=0, keepdims=True) * 0.5
    sums_ref[1:2, :] = jnp.sum(grad, axis=0, keepdims=True) * 0.5
    scaled = grad * vectors_ref[2:3, :]
    mean_one = jnp.mean(scaled, axis=-1, keepdims=True)
    mean_two = jnp.mean(scaled * unit, axis=-1, keepdims=True)
    middle_grad = cot_ref[...].astype(F32) + (scaled - mean_one - unit * mean_two) * inverse
    middle_grad_ref[...] = middle_grad
    branch_ref[...] = middle_grad.astype(BF16)
    labels = [row_labels(ends_ref, first_ref[0], shape, dim) for dim, shape in ((0, (rows, 1)), (1, (1, rows)))]
    heads_back(0, labels, places_ref, branch_ref, normed_ref, w_ref, proj_ref, packed_ref, heads_ref,
                        lse_ref, packed_grad_ref, w_grad, grads)
    send_grads(grads, PAD, (far_ref, near_ref, side_ref, keep_ref), sems)


def back_two_kernel(
    ends_ref,
    first_ref,
    places_ref,
    branch_ref,
    x_ref,
    normed_ref,
    heads_ref,
    proj_ref,
    packed_grad_one_ref,
    w_one_ref,
    w_ref,
    packed_ref,
    lse_ref,
    sums_ref,
    first_grad_ref,
    far_ref,
    near_ref,
    side_ref,
    keep_ref,
    packed_grad,
    w_grad,
    grads,
    sems,
):
    rows = branch_ref.shape[0]
    labels = [row_labels(ends_ref, first_ref[0], shape, dim) for dim, shape in ((0, (rows, 1)), (1, (1, rows)))]
    heads_back(1, labels, places_ref, branch_ref, normed_ref, w_ref, proj_ref, packed_ref, heads_ref,
                        lse_ref, packed_grad, w_grad, grads)
    grad = dot(packed_grad_one_ref[...], w_one_ref[...], 0, 0) + dot(
        packed_grad[...], w_ref[...], 0, 0
    )
    first_grad_ref[...] = grad.astype(BF16)
    unit, _ = normal(x_ref[...].astype(F32))
    sums = [jnp.sum(grad * unit, axis=0, keepdims=True), jnp.sum(grad, axis=0, keepdims=True)]
    for i in range(4):
        pair = sums if i == 0 else [sums_ref[2 * i - 2 : 2 * i - 1, :], sums_ref[2 * i - 1 : 2 * i, :]]
        lines = lax.broadcasted_iota(jnp.int32, (PAD, grads.shape[2]), 0)
        grads[places_ref[i], :PAD, :] = jnp.where(
            lines == 0, pair[0], jnp.where(lines == 1, pair[1], 0.0)
        ).astype(BF16)
    send_grads(grads, 0, (far_ref, near_ref, side_ref, keep_ref), sems)


def back_scratch(depth, inner, width):
    return [
        pltpu.VMEM((depth + inner, width), BF16),
        pltpu.VMEM((4, PAD + (depth + inner) // 4, width), BF16),
        pltpu.SemaphoreType.DMA((4,)),
    ]


def back_one(ends, first, places, middle, mine, other, cot, vectors, shared, slot):
    rows, width = middle.shape
    depth, inner = slot[0].shape[0], shared[2].shape[0] // 2
    part = jax.ShapeDtypeStruct(((depth + inner) // 4, width), BF16)
    outs = pl.pallas_call(
        back_one_kernel,
        out_shape=(
            jax.ShapeDtypeStruct((rows, width), F32),
            jax.ShapeDtypeStruct((rows, width), BF16),
            jax.ShapeDtypeStruct((2, width), F32),
            jax.ShapeDtypeStruct((depth, rows), BF16),
            part,
            part,
            part,
            part,
        ),
        in_specs=smem(3) + vmem(11),
        out_specs=tuple(vmem(4) + anywhere(4)),
        scratch_shapes=back_scratch(depth, inner, width),
        name="back_one",
        **settings(),
    )(ends, first, places, middle, mine, other, cot, vectors, *shared, *slot)
    return outs[:4], outs[4:]


def back_two(ends, first, places, branch, x, shared, grad_one, w_one, slot, sums):
    rows, width = branch.shape
    depth, inner = slot[0].shape[0], shared[2].shape[0] // 2
    part = jax.ShapeDtypeStruct(((depth + inner) // 4 + PAD, width), BF16)
    outs = pl.pallas_call(
        back_two_kernel,
        out_shape=(
            jax.ShapeDtypeStruct((rows, width), BF16),
            part,
            part,
            part,
            part,
        ),
        in_specs=smem(3) + vmem(11),
        out_specs=tuple(vmem(1) + anywhere(4)),
        scratch_shapes=[pltpu.VMEM((depth, rows), BF16)] + back_scratch(depth, inner, width),
        name="back_two",
        **settings(),
    )(ends, first, places, branch, x, *shared, grad_one, w_one, *slot, sums)
    return outs[0], outs[1:]


def settle_some_kernel(order_ref, *refs):
    pieces, others_ref, outs = refs[:3], refs[3], refs[4:]
    up_ref, down_ref, qkv_ref, proj_ref, sums_ref = outs
    feed_rows = up_ref.shape[0] // 4
    qkv_rows, proj_rows = qkv_ref.shape[0] // 4, proj_ref.shape[0] // 4
    size = pieces[0].shape[0]
    early = size - feed_rows - PAD
    late = qkv_rows - early

    def put(out, index, rows, offset, count, value):
        start = pl.multiple_of(order_ref[index] * rows + offset, 8)
        out[pl.ds(start, count), :] = value.astype(F32)

    def first_half(index, ref, base):
        put(up_ref, index, feed_rows, 0, feed_rows, ref[base : base + feed_rows, :])
        base = base + feed_rows
        put(sums_ref, index, PAD, 0, PAD, ref[base : base + PAD, :])
        put(qkv_ref, index, qkv_rows, 0, early, ref[base + PAD : base + PAD + early, :])

    def second_half(index, ref, base):
        put(down_ref, index, feed_rows, 0, feed_rows, ref[base : base + feed_rows, :])
        base = base + feed_rows
        put(qkv_ref, index, qkv_rows, early, late, ref[base : base + late, :])
        base = base + late
        put(proj_ref, index, proj_rows, 0, proj_rows, ref[base : base + proj_rows, :])

    halves = (first_half, second_half)
    for core in range(2):

        @pl.when(order_ref[5] == core)
        def _():
            for index, piece in enumerate(pieces):
                halves[core](index, piece, 0)
                halves[1 - core](index, others_ref, CROSSED[index] * size)


def settle_last_kernel(order_ref, piece_ref, others_ref, *refs):
    outs, buffers, sems = refs[5:10], refs[10:15], refs[15]
    up, down, qkv, proj, sums = buffers
    size, feed_rows = piece_ref.shape[0], up.shape[0]
    early = size - feed_rows - PAD
    late = qkv.shape[0] - early

    def first_half(ref):
        up[...] = ref[:feed_rows, :].astype(F32)
        sums[...] = ref[feed_rows : feed_rows + PAD, :].astype(F32)
        qkv[:early, :] = ref[feed_rows + PAD :, :].astype(F32)

    def second_half(ref):
        down[...] = ref[:feed_rows, :].astype(F32)
        qkv[early:, :] = ref[feed_rows : feed_rows + late, :].astype(F32)
        proj[...] = ref[feed_rows + late : feed_rows + late + proj.shape[0], :].astype(F32)

    @pl.when(order_ref[5] == 0)
    def _():
        first_half(piece_ref)
        second_half(others_ref)

    @pl.when(order_ref[5] == 1)
    def _():
        first_half(others_ref)
        second_half(piece_ref)

    copies = []
    for i, (buffer, out) in enumerate(zip(buffers, outs)):
        rows = buffer.shape[0]
        start = pl.multiple_of(order_ref[3] * rows, 8)
        copies.append(pltpu.make_async_copy(buffer, out.at[pl.ds(start, rows)], sems.at[i]))
    for copy in copies:
        copy.start()
    for copy in copies:
        copy.wait()


def settle(order, pieces, others, sizes, settled):
    width, units, depth, inner = sizes
    shapes = [(width, units), (units, width), (depth, width), (inner, width), (4 * PAD, width)]
    out_shape = tuple(jax.ShapeDtypeStruct(shape, F32) for shape in shapes)
    if not settled:
        return pl.pallas_call(
            settle_some_kernel,
            out_shape=out_shape,
            in_specs=smem(1) + vmem(4),
            out_specs=tuple(vmem(5)),
            name="settle",
            **settings(),
        )(order, *pieces, others)
    return pl.pallas_call(
        settle_last_kernel,
        out_shape=out_shape,
        in_specs=smem(1) + vmem(2) + anywhere(5),
        out_specs=tuple(anywhere(5)),
        scratch_shapes=[pltpu.VMEM((rows // 4, columns), F32) for rows, columns in shapes]
        + [pltpu.SemaphoreType.DMA((5,))],
        input_output_aliases={3 + i: i for i in range(5)},
        name="settle_last",
        **settings(),
    )(order, *pieces, others, *settled)


def spread(piece, *before):
    near = lax.ppermute(piece, LAYER, FIRST)
    side = lax.ppermute(piece, LAYER, SECOND)
    far = lax.ppermute(after(near, side, *before) if before else near, LAYER, SECOND)
    return piece, near, side, far


def scatter_at_once(far, near, side, keep):
    return keep, tuple(
        lax.ppermute(part, LAYER, pairs)
        for part, pairs in ((near, FIRST), (side, SECOND), (far, BOTH))
    )


def add_low(*parts):
    total = parts[0].astype(F32)
    for part in parts[1:]:
        total = total + part.astype(F32)
    return total.astype(BF16)


def to_shard(sum_one, sum_two):
    return (
        lax.ppermute(sum_one, CORE_T, ROUND_ONE_BACK),
        lax.ppermute(sum_two, CORE_T, ROUND_TWO_BACK),
    )


def over_outer(share, outer):
    return lax.psum(share.astype(F32), "o").astype(BF16) if outer > 1 else share


def half_rows(parts, place):
    rows = parts[0].shape[0] // 2
    return add_low(*(lax.dynamic_slice_in_dim(part, place * rows, rows, 0) for part in parts))


def after(value, *others):
    return lax.optimization_barrier((value,) + others)[0] if others else value


def local(
    patches,
    item_patches,
    attn_gain,
    attn_bias,
    qkv_weight,
    proj_weight,
    mlp_gain,
    mlp_bias,
    up_weight,
    up_bias,
    down_weight,
    cotangent,
):
    c, t, x, y = (lax.axis_index(name) for name in ("c", "t", "x", "y"))
    outer = lax.axis_size("o")
    quarter = 2 * y + x
    member = t & 1
    own_rows, width = patches.shape
    first_bit = 1 + c
    home = (t // 2 == c).astype(jnp.int32)
    order = jnp.stack([quarter, quarter ^ first_bit, quarter ^ (3 - first_bit), quarter ^ 3, home, c])
    steps = jnp.arange(4) ^ quarter
    places = jnp.where(
        steps == 3, 0, jnp.where(steps == first_bit, 1, jnp.where(steps == 0, 3, 2))
    )

    def exchange(array):
        return lax.ppermute(array, "c", SWAP)

    def both_halves(array, *before):
        other = exchange(after(array, *before))
        return jnp.where(
            c == 0, jnp.concatenate([array, other], 0), jnp.concatenate([other, array], 0)
        )

    def cut(array):
        rows = array.shape[0] // 4
        return lax.dynamic_slice_in_dim(array, quarter * rows, rows, 0)

    qkv_t = qkv_weight.T
    depth, units, inner = qkv_t.shape[0], down_weight.shape[0], proj_weight.shape[0]
    piece_a = jnp.concatenate([cut(qkv_t), cut(proj_weight)], 0)
    half_a = piece_a.shape[0] // 2
    piece_a_two = lax.dynamic_slice_in_dim(piece_a, home * half_a, half_a, 0)
    piece_a, piece_a_two, patches = lax.optimization_barrier((piece_a, piece_a_two, patches))
    a_one = lax.ppermute(piece_a, CORE_T, ROUND_ONE)
    a_two = lax.ppermute(piece_a_two, CORE_T, ROUND_TWO)
    inputs = lax.ppermute(patches, CORE_T, ROW_SWAP)
    items = exchange(item_patches)
    ends = jnp.cumsum(jnp.where(member == c, item_patches, items)[0])
    first = (t // 2 * BLOCK).astype(jnp.int32).reshape(1)
    vectors = jnp.stack([attn_gain, attn_bias, mlp_gain, mlp_bias])
    bias_rows = jnp.broadcast_to(up_bias[None, :], (PAD, units))
    cut_up, cut_down = cut(up_weight), cut(down_weight)
    piece_b = jnp.concatenate([cut_up, cut_down, bias_rows], 0)
    half_b = jnp.concatenate([jnp.where(home == 1, cut_down, cut_up), bias_rows], 0)
    block_in = both_halves(inputs)
    a_one, a_two, block_in, ends, first, order, places, vectors, piece_b, half_b, bias_rows = (
        lax.optimization_barrier(
            (a_one, a_two, block_in, ends, first, order, places, vectors, piece_b, half_b, bias_rows)
        )
    )
    b_one = lax.ppermute(piece_b, CORE_T, ROUND_ONE)
    b_two = lax.ppermute(half_b, CORE_T, ROUND_TWO)
    pieces_a = spread(jnp.concatenate([a_one, a_two], 0))
    crossed_a = lax.ppermute(
        jnp.concatenate([piece[2 * half_a :] for piece in pieces_a], 0), "c", SWAP
    )
    both_b = jnp.concatenate([b_one, b_two], 0)
    shared, one, two = attention(
        ends, first, order, after(block_in, both_b), vectors, (qkv_t, proj_weight), pieces_a, crossed_a
    )
    normed, mine, heads_out, proj = shared
    shared = (normed, heads_out, proj)
    pieces_b = spread(both_b, mine)
    other = exchange(mine)
    block_cot = both_halves(lax.ppermute(after(cotangent, both_b), CORE_T, ROW_SWAP), mine)
    crossed_b = exchange(jnp.concatenate([piece[piece_b.shape[0] :] for piece in pieces_b[:3]], 0))
    crossed_far = exchange(pieces_b[3][piece_b.shape[0] :])
    middle, out_part, back_part, bias_one, bias_two, send, keep = feed(
        order, places, block_in, mine, other, block_cot, vectors,
        (up_weight, down_weight, bias_rows), pieces_b, crossed_b, crossed_far,
    )
    hop = lax.ppermute(send, LAYER, FIRST)

    def own(array):
        return lax.dynamic_slice_in_dim(array, c * own_rows, own_rows, 0)

    (middle_grad, branch, mlp_sums, grad_one), back_one_out = back_one(
        ends, first, places, middle, back_part, exchange(back_part), block_cot, vectors, shared, one
    )
    hop = after(hop, branch)
    next_hop = add_low(keep[:, 0], hop[:, 0])
    far = lax.ppermute(next_hop, LAYER, SECOND)
    keep_one, got_one = scatter_at_once(*back_one_out)
    slot_one = 2 * c + jnp.where(t // 2 == c, 1 - member, member ^ c)
    shards = jnp.arange(4)[:, None]
    bias_part = jnp.where(shards == slot_one, bias_one, 0.0) + jnp.where(
        shards == (slot_one ^ 1), bias_two, 0.0
    )
    small = jnp.concatenate([mlp_sums, bias_part], 0)
    first_part, back_two_out = back_two(
        ends, first, places, after(branch, next_hop), block_in, shared, grad_one, one[0], two, small
    )
    feed_sums = [add_low(keep[i, 1], hop[i, 1], part) for i, part in enumerate(after(far, first_part))]
    feed_parts = to_shard(*feed_sums)
    keep_one, back_two_out, first_part, out_part, _ = lax.optimization_barrier(
        (keep_one, back_two_out, first_part, out_part, feed_sums)
    )
    keep_two, got_two = scatter_at_once(*back_two_out)

    unit, inverse = normal(inputs.astype(F32))
    first_grad = own(first_part).astype(F32) + own(exchange(first_part)).astype(F32)
    scaled = first_grad * attn_gain
    mean_one = jnp.mean(scaled, axis=-1, keepdims=True)
    mean_two = jnp.mean(scaled * unit, axis=-1, keepdims=True)
    grad_in = own(middle_grad) + (scaled - mean_one - unit * mean_two) * inverse
    grad_in = grad_in.astype(BF16)
    result = own(middle) + own(out_part).astype(F32) + own(exchange(out_part)).astype(F32)
    result = result.astype(BF16)
    got_one, got_two = after((got_one, got_two), feed_parts[0])
    back_sum_two = add_low(keep_two, *got_two)
    small = add_low(back_sum_two[:PAD], exchange(back_sum_two[:PAD]))
    blank = jnp.zeros((PAD, width), BF16)
    back_sum_one = jnp.concatenate([small, add_low(keep_one, *got_one), blank], 0)
    back_sum_two = jnp.concatenate([small, back_sum_two[PAD:], blank], 0)
    back_parts = to_shard(back_sum_one, back_sum_two)

    def halves(place):
        return jnp.concatenate([half_rows(feed_parts, place), half_rows(back_parts, place)], 0)

    share = add_low(halves(c), exchange(halves(1 - c)))
    share = over_outer(share, outer)
    share, grad_in, result = lax.optimization_barrier((share, grad_in, result))
    patches_grad = lax.ppermute(grad_in, CORE_T, ROW_SWAP).astype(F32)
    result = lax.ppermute(result, CORE_T, ROW_SWAP)
    near = lax.ppermute(share, LAYER, FIRST)
    side = lax.ppermute(share, LAYER, SECOND)
    near, side, patches_grad, result = lax.optimization_barrier((near, side, patches_grad, result))
    far = lax.ppermute(near, LAYER, SECOND)
    others = exchange(jnp.concatenate([share, near, side], 0))
    settled = settle(order, (share, near, side), others, (width, units, depth, inner), ())
    up_sum, down_sum, qkv_sum, proj_sum, sums = settle(
        order, (far,), exchange(far), (width, units, depth, inner), settled
    )
    sums = sums.reshape(4, PAD, width)[:, :2].reshape(8, width)
    up_bias_sum = lax.dynamic_index_in_dim(sums, 4 + t, 0, keepdims=False)
    return (
        result,
        patches_grad,
        sums[0],
        sums[1],
        qkv_sum.T,
        proj_sum,
        sums[2],
        sums[3],
        up_sum,
        up_bias_sum,
        down_sum,
    )


def solution(mesh):
    dp, tensor = mesh.shape["dp"], mesh.shape["tensor"]
    grid = Mesh(mesh.devices.reshape(dp // 8, 2, 2, 2, tensor), ("o", "y", "x", "c", "t"))
    dp_axes = ("o", "y", "x", "c")
    rows = P(dp_axes + ("t",), None)
    return jax.shard_map(
        local,
        mesh=grid,
        in_specs=(
            rows,
            P(dp_axes, None),
            P(),
            P(),
            P(None, "t"),
            P("t", None),
            P(),
            P(),
            P(None, "t"),
            P("t"),
            P("t", None),
            rows,
        ),
        out_specs=(
            rows,
            rows,
            P(),
            P(),
            P(None, "t"),
            P("t", None),
            P(),
            P(),
            P(None, "t"),
            P("t"),
            P("t", None),
        ),
        check_vma=False,
    )
```

```python
import jax
import jax.numpy as jnp
from jax import lax
from jax.experimental import pallas as pl
from jax.experimental.pallas import tpu as pltpu
from jax.sharding import Mesh
from jax.sharding import PartitionSpec as P

HEAD_DIM = 64
BLOCK = 784
NORM_EPS = 1e-06
SCALE = HEAD_DIM**-0.5
LOG2E = 1.4426950408889634
F32 = jnp.float32
BF16 = jnp.bfloat16
VMEM_LIMIT = 58 * 1024 * 1024
SWAP = [(0, 1), (1, 0)]
TILE = 768
PAD = 16

CORE_T = ("c", "t")
ROUND_ONE = [(0, 1), (4, 2), (1, 0), (5, 3), (6, 7), (2, 5), (7, 6), (3, 4)]
ROUND_TWO = [(4, 3), (5, 2), (2, 4), (3, 5), (0, 7), (1, 6), (6, 0), (7, 1)]
ROUND_ONE_BACK = [(b, a) for a, b in ROUND_ONE]
ROUND_TWO_BACK = [(3, 4), (2, 5), (4, 2), (5, 3), (0, 0), (1, 1), (6, 6), (7, 7)]
ROW_SWAP = [(4, 1), (1, 4), (6, 3), (3, 6), (0, 0), (2, 2), (5, 5), (7, 7)]
LAYER = ("y", "x", "c")
FIRST = [(i, i ^ (4 if i & 1 else 2)) for i in range(8)]
SECOND = [(i, i ^ (2 if i & 1 else 4)) for i in range(8)]
BOTH = [(i, i ^ 6) for i in range(8)]


def dot(left, right, left_dim=1, right_dim=0):
    return lax.dot_general(
        left, right, (((left_dim,), (right_dim,)), ((), ())), preferred_element_type=F32
    )


def normal(rows):
    centre = rows - jnp.mean(rows, axis=-1, keepdims=True)
    spread = jnp.mean(centre * centre, axis=-1, keepdims=True)
    inverse = lax.rsqrt(spread + NORM_EPS)
    return centre * inverse, inverse


def row_labels(ends_ref, first, shape, dim):
    places = lax.broadcasted_iota(jnp.int32, shape, dim) + first
    labels = jnp.zeros(shape, jnp.int32)
    for slot in range(ends_ref.shape[0]):
        labels = labels + (places >= ends_ref[slot]).astype(jnp.int32)
    return labels


def smem(count):
    return [pl.BlockSpec(memory_space=pltpu.SMEM)] * count


def vmem(count):
    return [pl.BlockSpec(memory_space=pltpu.VMEM)] * count


def anywhere(count):
    return [pl.BlockSpec(memory_space=pl.ANY)] * count


def settings():
    return dict(
        compiler_params=pltpu.CompilerParams(vmem_limit_bytes=VMEM_LIMIT),
        cost_estimate=pl.CostEstimate(
            flops=int(1e9), bytes_accessed=int(1e6), transcendentals=0
        ),
    )


def heads_forward(labels, normed_ref, w_ref, packed_ref, heads_ref, base_head, lse_ref):
    rows = normed_ref.shape[0]
    label_col, label_row = labels

    def head(h):
        part = slice(h * 3 * HEAD_DIM, (h + 1) * 3 * HEAD_DIM)
        packed = dot(w_ref[part, :], normed_ref[...], 1, 1).astype(BF16)
        packed_ref[part, :] = packed
        queries = packed[:HEAD_DIM] * SCALE
        key_rows = packed[HEAD_DIM : 2 * HEAD_DIM].T
        values = packed[2 * HEAD_DIM :]
        scores = dot(key_rows, queries) * LOG2E
        scores = jnp.where(label_col == label_row, scores, -1e30)
        top = jnp.max(scores, axis=0, keepdims=True)
        weights = jnp.exp2(scores - top)
        total = jnp.sum(weights, axis=0, keepdims=True)
        mixed = dot(values, weights.astype(BF16)) * (1.0 / total)
        start = (h + base_head) * HEAD_DIM
        heads_ref[start : start + HEAD_DIM, :] = mixed.astype(BF16)
        lse_ref[h : h + 1, :] = top + jnp.log2(total)

    for h in range(w_ref.shape[0] // (3 * HEAD_DIM)):
        head(h)


CROSSED = (0, 2, 1, 3)


def place(order_ref, index, rows):
    return pl.ds(pl.multiple_of(order_ref[index] * rows, 16), rows)


def attention_kernel(*refs):
    ends_ref, first_ref, order_ref, x_ref, vectors_ref, own_w_ref, own_proj_ref = refs[:7]
    pieces, crossed_ref, refs = refs[7:11], refs[11], refs[12:]
    normed_ref, mine_ref, heads_ref, proj_ref = refs[:4]
    w_one, packed_one, lse_one, w_two, packed_two, lse_two = refs[4:]
    rows = x_ref.shape[0]
    depth, inner = own_w_ref.shape[0], own_proj_ref.shape[0]
    w_rows, p_rows = depth // 4, inner // 4
    size = w_rows + p_rows
    half = size // 2
    rest = w_rows - half
    for index, piece in enumerate(pieces):
        w_one[place(order_ref, index, w_rows), :] = piece[:w_rows, :]
        proj_ref[place(order_ref, index, p_rows), :] = piece[w_rows:size, :]

    @pl.when(order_ref[4] == 1)
    def _():
        w_two[...] = own_w_ref[...]
        proj_ref[inner:, :] = own_proj_ref[...]

    @pl.when(order_ref[4] == 0)
    def _():
        for index, piece in enumerate(pieces):
            base = pl.multiple_of(order_ref[index] * w_rows, 16)
            w_two[pl.ds(base, half), :] = piece[size:, :]
            start = CROSSED[index] * half
            w_two[pl.ds(base + half, rest), :] = crossed_ref[start : start + rest, :]
            base = pl.multiple_of(order_ref[index] * p_rows + inner, 16)
            proj_ref[pl.ds(base, p_rows), :] = crossed_ref[start + rest : start + half, :]

    unit, _ = normal(x_ref[...].astype(F32))
    normed_ref[...] = (unit * vectors_ref[0:1, :] + vectors_ref[1:2, :]).astype(BF16)
    labels = [row_labels(ends_ref, first_ref[0], shape, dim) for dim, shape in ((0, (rows, 1)), (1, (1, rows)))]
    heads_forward(labels, normed_ref, w_one, packed_one, heads_ref, 0, lse_one)
    heads_forward(labels, normed_ref, w_two, packed_two, heads_ref, inner // HEAD_DIM, lse_two)
    mine_ref[...] = dot(heads_ref[...], proj_ref[...], 0, 0).astype(BF16)


def attention(ends, first, order, x, vectors, own, pieces, crossed):
    rows, width = x.shape
    depth, inner = own[0].shape[0], own[1].shape[0]
    rows_low = jax.ShapeDtypeStruct((rows, width), BF16)
    slot = (
        jax.ShapeDtypeStruct((depth, width), BF16),
        jax.ShapeDtypeStruct((depth, rows), BF16),
        jax.ShapeDtypeStruct((8, rows), F32),
    )
    outs = pl.pallas_call(
        attention_kernel,
        out_shape=(
            rows_low,
            rows_low,
            jax.ShapeDtypeStruct((2 * inner, rows), BF16),
            jax.ShapeDtypeStruct((2 * inner, width), BF16),
        )
        + slot
        + slot,
        in_specs=smem(3) + vmem(9),
        out_specs=tuple(vmem(10)),
        name="attention",
        **settings(),
    )(ends, first, order, x, vectors, *own, *pieces, crossed)
    return outs[:4], outs[4:7], outs[7:]


def feed_slot(places_ref, second, second_t, cot_ref, cot_t, up, down, bias, grads, out_sum, back_sum, bias_grad):
    width, units = up.shape
    quarter = units // 4

    def step(j, carry):
        columns = pl.ds(pl.multiple_of(j * TILE, TILE), TILE)
        up_tile = up[:, columns]
        down_tile = down[columns, :]
        pre = dot(second[...], up_tile) + bias[:, columns].astype(F32)[0:1]
        gate = 0.5 * (1.0 + lax.erf(pre * (2.0**-0.5)))
        slope = gate + pre * (
            jnp.exp2(pre * pre * (-0.5 * LOG2E)) * (0.5 / 3.141592653589793) ** 0.5
        )
        hidden = (pre * gate).astype(BF16)
        out_sum[...] += dot(hidden, down_tile)
        down_grad = dot(cot_t[...], hidden).T.astype(BF16)
        for i in range(TILE // 64):
            chunk = j * (TILE // 64) + i
            start = width // 4 + lax.rem(chunk, quarter // 64) * 64
            grads[places_ref[lax.div(chunk, quarter // 64)], pl.ds(pl.multiple_of(start, 64), 64), :] = down_grad[i * 64 : (i + 1) * 64]
        act = (dot(cot_ref[...], down_tile, 1, 1) * slope).astype(BF16)
        bias_grad[:, columns] = jnp.sum(act.astype(F32), axis=0, keepdims=True)
        back_sum[...] += dot(act, up_tile, 1, 1)
        up_grad = dot(second_t[...], act).astype(BF16)
        for i in range(4):
            size = width // 4
            grads[places_ref[i], 0:size, columns] = up_grad[i * size : (i + 1) * size]
        return carry

    lax.fori_loop(0, units // TILE, step, 0)


def fetch(source, target, sem):
    copy = pltpu.make_async_copy(source, target, sem)
    copy.start()
    return copy


def wait_all(copies):
    for copy in copies:
        copy.wait()


def feed_kernel(*refs):
    order_ref, places_ref, vectors_ref, x_hbm, mine_hbm, other_hbm, cot_hbm = refs[:7]
    own_up_hbm, own_down_hbm, own_bias_hbm, pieces, crossed_hbm, far_hbm, refs = (
        refs[7], refs[8], refs[9], refs[10:14], refs[14], refs[15], refs[16:],
    )
    middle_hbm, out_ref, back_ref, bias_one, bias_two, *leave_refs = refs[:9]
    x_ref, mine_ref, other_ref, cot_ref, middle_ref, second, second_t, cot_t, up, down, bias, grads, out_sum, back_sum, sems = refs[9:]
    _, width, units = up.shape
    u_rows, d_rows = width // 4, units // 4
    size = u_rows + d_rows + PAD
    half = u_rows + PAD
    free = iter(range(40))
    sem = lambda: sems.at[next(free)]
    early = [fetch(*pair, sem()) for pair in ((x_hbm, x_ref), (mine_hbm, mine_ref), (other_hbm, other_ref))]
    first = [fetch(pieces[0].at[pl.ds(size - PAD, PAD)], bias.at[0], sem())]
    for index, piece in enumerate(pieces):
        first.append(fetch(piece.at[pl.ds(0, u_rows)], up.at[0, place(order_ref, index, u_rows)], sem()))
        first.append(fetch(piece.at[pl.ds(u_rows, d_rows)], down.at[0, place(order_ref, index, d_rows)], sem()))
    cot_copy = fetch(cot_hbm, cot_ref, sem())
    home = [
        pltpu.make_async_copy(own_up_hbm, up.at[1], sem()),
        pltpu.make_async_copy(own_down_hbm, down.at[1], sem()),
        pltpu.make_async_copy(own_bias_hbm, bias.at[1], sem()),
    ]
    away = [pltpu.make_async_copy(pieces[0].at[pl.ds(size + u_rows, PAD)], bias.at[1], sem())]
    for index, piece in enumerate(pieces):
        part = piece.at[pl.ds(size, u_rows)]
        away.append(pltpu.make_async_copy(part, up.at[1, place(order_ref, index, u_rows)], sem()))
        part = far_hbm if index == 3 else crossed_hbm.at[pl.ds(CROSSED[index] * half, half)]
        part = part.at[pl.ds(0, d_rows)]
        away.append(pltpu.make_async_copy(part, down.at[1, place(order_ref, index, d_rows)], sem()))

    @pl.when(order_ref[4] == 1)
    def _():
        for copy in home:
            copy.start()

    @pl.when(order_ref[4] == 0)
    def _():
        for copy in away:
            copy.start()

    wait_all(early)
    middle = x_ref[...].astype(F32) + (mine_ref[...].astype(F32) + other_ref[...].astype(F32))
    middle_ref[...] = middle
    late = [fetch(middle_ref, middle_hbm, sem())]
    unit, _ = normal(middle)
    low = (unit * vectors_ref[2:3, :] + vectors_ref[3:4, :]).astype(BF16)
    second[...] = low
    second_t[...] = low.T
    cot_copy.wait()
    cot_t[...] = cot_ref[...].T
    out_sum[...] = jnp.zeros_like(out_sum)
    back_sum[...] = jnp.zeros_like(back_sum)
    wait_all(first)
    def leave(slot, start, rows, refs, target):
        return [
            fetch(
                grads.at[slot, pl.ds(2 * part, 2), pl.ds(start, rows)],
                ref.at[:, pl.ds(target, rows)],
                sem(),
            )
            for part, ref in enumerate(refs)
        ]

    shared = (places_ref, second, second_t, cot_ref, cot_t)
    feed_slot(*shared, up.at[0], down.at[0], bias.at[0], grads.at[0], out_sum, back_sum, bias_one)
    late += leave(0, 0, u_rows + d_rows, leave_refs[:2], 0)

    @pl.when(order_ref[4] == 1)
    def _():
        wait_all(home)

    @pl.when(order_ref[4] == 0)
    def _():
        wait_all(away)

    feed_slot(*shared, up.at[1], down.at[1], bias.at[1], grads.at[1], out_sum, back_sum, bias_two)
    late += leave(1, 0, u_rows, leave_refs[:2], u_rows + d_rows)
    late += leave(1, u_rows, d_rows, leave_refs[2:], 0)
    out_ref[...] = out_sum[...].astype(BF16)
    back_ref[...] = back_sum[...].astype(BF16)
    wait_all(late)


def feed(order, places, x, mine, other, cot, vectors, own, pieces, crossed, crossed_far):
    rows, width = x.shape
    units = own[1].shape[0]
    size = (width + units) // 4
    rows_low = jax.ShapeDtypeStruct((rows, width), BF16)
    rows_full = jax.ShapeDtypeStruct((rows, width), F32)
    most = jax.ShapeDtypeStruct((2, size + width // 4, width), BF16)
    least = jax.ShapeDtypeStruct((2, units // 4, width), BF16)
    bias_grad = jax.ShapeDtypeStruct((1, units), F32)
    return pl.pallas_call(
        feed_kernel,
        out_shape=(rows_full, rows_low, rows_low, bias_grad, bias_grad, most, most, least, least),
        in_specs=smem(2) + vmem(1) + anywhere(13),
        out_specs=tuple(anywhere(1) + vmem(4) + anywhere(4)),
        scratch_shapes=[pltpu.VMEM((rows, width), BF16)] * 4
        + [
            pltpu.VMEM((rows, width), F32),
            pltpu.VMEM((rows, width), BF16),
            pltpu.VMEM((width, rows), BF16),
            pltpu.VMEM((width, rows), BF16),
            pltpu.VMEM((2, width, units), BF16),
            pltpu.VMEM((2, units, width), BF16),
            pltpu.VMEM((2, PAD, units), BF16),
            pltpu.VMEM((2, 4, size, width), BF16),
            pltpu.VMEM((rows, width), F32),
            pltpu.VMEM((rows, width), F32),
            pltpu.SemaphoreType.DMA((40,)),
        ],
        name="feed",
        **settings(),
    )(order, places, vectors, x, mine, other, cot, *own, *pieces, crossed, crossed_far)


def heads_back(slot, labels, places_ref, branch_ref, normed_ref, w_ref, proj_ref, packed_ref, heads_ref,
               lse_ref, packed_grad, w_grad, grads):
    rows = branch_ref.shape[0]
    depth, inner = w_ref.shape[0], proj_ref.shape[0] // 2
    label_col, label_row = labels

    def head(h):
        base = h * 3 * HEAD_DIM
        part = slice(h * HEAD_DIM + slot * inner, (h + 1) * HEAD_DIM + slot * inner)
        mixed = heads_ref[part, :]
        mixed_grad = dot(proj_ref[part, :], branch_ref[...], 1, 1).astype(BF16)
        packed = packed_ref[base : base + 3 * HEAD_DIM, :]
        queries = packed[:HEAD_DIM] * SCALE
        keys = packed[HEAD_DIM : 2 * HEAD_DIM]
        key_rows = keys.T
        value_rows = packed[2 * HEAD_DIM :].T
        inner_sum = jnp.sum(mixed.astype(F32) * mixed_grad.astype(F32), axis=0, keepdims=True)
        scores = dot(key_rows, queries) * LOG2E
        scores = jnp.where(label_col == label_row, scores, -1e30)
        prob = jnp.exp2(scores - lse_ref[h : h + 1, :])
        value_grad = dot(mixed_grad, prob.astype(BF16), 1, 1)
        prob_grad = dot(value_rows, mixed_grad)
        score_grad = (prob * (prob_grad - inner_sum)).astype(BF16)
        query_grad = dot(keys, score_grad) * SCALE
        key_grad = dot(queries, score_grad, 1, 1)
        for i, grad in enumerate((query_grad, key_grad, value_grad)):
            start = base + i * HEAD_DIM
            packed_grad[start : start + HEAD_DIM, :] = grad.astype(BF16)

    for h in range(depth // (3 * HEAD_DIM)):
        head(h)
    w_grad[:depth, :] = dot(packed_grad[...], normed_ref[...]).astype(BF16)
    w_grad[depth:, :] = dot(heads_ref[slot * inner : (slot + 1) * inner, :], branch_ref[...]).astype(BF16)
    w_size, p_size = depth // 4, inner // 4
    size = w_size + p_size
    for i in range(4):
        grads[places_ref[i], PAD : PAD + w_size, :] = w_grad[i * w_size : (i + 1) * w_size, :]
        grads[places_ref[i], PAD + w_size : PAD + size, :] = w_grad[depth + i * p_size : depth + (i + 1) * p_size, :]


def send_grads(grads, start, out_refs, sems):
    copies = [
        pltpu.make_async_copy(grads.at[i, pl.ds(start, grads.shape[1] - start)], out_ref, sems.at[i])
        for i, out_ref in enumerate(out_refs)
    ]
    for copy in copies:
        copy.start()
    for copy in copies:
        copy.wait()


def back_one_kernel(
    ends_ref,
    first_ref,
    places_ref,
    middle_ref,
    mine_ref,
    other_ref,
    cot_ref,
    vectors_ref,
    normed_ref,
    heads_ref,
    proj_ref,
    w_ref,
    packed_ref,
    lse_ref,
    middle_grad_ref,
    branch_ref,
    sums_ref,
    packed_grad_ref,
    far_ref,
    near_ref,
    side_ref,
    keep_ref,
    w_grad,
    grads,
    sems,
):
    rows = middle_ref.shape[0]
    unit, inverse = normal(middle_ref[...])
    grad = mine_ref[...].astype(F32) + other_ref[...].astype(F32)
    sums_ref[0:1, :] = jnp.sum(grad * unit, axis=0, keepdims=True) * 0.5
    sums_ref[1:2, :] = jnp.sum(grad, axis=0, keepdims=True) * 0.5
    scaled = grad * vectors_ref[2:3, :]
    mean_one = jnp.mean(scaled, axis=-1, keepdims=True)
    mean_two = jnp.mean(scaled * unit, axis=-1, keepdims=True)
    middle_grad = cot_ref[...].astype(F32) + (scaled - mean_one - unit * mean_two) * inverse
    middle_grad_ref[...] = middle_grad
    branch_ref[...] = middle_grad.astype(BF16)
    labels = [row_labels(ends_ref, first_ref[0], shape, dim) for dim, shape in ((0, (rows, 1)), (1, (1, rows)))]
    heads_back(0, labels, places_ref, branch_ref, normed_ref, w_ref, proj_ref, packed_ref, heads_ref,
                        lse_ref, packed_grad_ref, w_grad, grads)
    send_grads(grads, PAD, (far_ref, near_ref, side_ref, keep_ref), sems)


def back_two_kernel(
    ends_ref,
    first_ref,
    places_ref,
    branch_ref,
    x_ref,
    normed_ref,
    heads_ref,
    proj_ref,
    packed_grad_one_ref,
    w_one_ref,
    w_ref,
    packed_ref,
    lse_ref,
    sums_ref,
    first_grad_ref,
    far_ref,
    near_ref,
    side_ref,
    keep_ref,
    packed_grad,
    w_grad,
    grads,
    sems,
):
    rows = branch_ref.shape[0]
    labels = [row_labels(ends_ref, first_ref[0], shape, dim) for dim, shape in ((0, (rows, 1)), (1, (1, rows)))]
    heads_back(1, labels, places_ref, branch_ref, normed_ref, w_ref, proj_ref, packed_ref, heads_ref,
                        lse_ref, packed_grad, w_grad, grads)
    grad = dot(packed_grad_one_ref[...], w_one_ref[...], 0, 0) + dot(
        packed_grad[...], w_ref[...], 0, 0
    )
    first_grad_ref[...] = grad.astype(BF16)
    unit, _ = normal(x_ref[...].astype(F32))
    sums = [jnp.sum(grad * unit, axis=0, keepdims=True), jnp.sum(grad, axis=0, keepdims=True)]
    for i in range(4):
        pair = sums if i == 0 else [sums_ref[2 * i - 2 : 2 * i - 1, :], sums_ref[2 * i - 1 : 2 * i, :]]
        lines = lax.broadcasted_iota(jnp.int32, (PAD, grads.shape[2]), 0)
        grads[places_ref[i], :PAD, :] = jnp.where(
            lines == 0, pair[0], jnp.where(lines == 1, pair[1], 0.0)
        ).astype(BF16)
    send_grads(grads, 0, (far_ref, near_ref, side_ref, keep_ref), sems)


def back_scratch(depth, inner, width):
    return [
        pltpu.VMEM((depth + inner, width), BF16),
        pltpu.VMEM((4, PAD + (depth + inner) // 4, width), BF16),
        pltpu.SemaphoreType.DMA((4,)),
    ]


def back_one(ends, first, places, middle, mine, other, cot, vectors, shared, slot):
    rows, width = middle.shape
    depth, inner = slot[0].shape[0], shared[2].shape[0] // 2
    part = jax.ShapeDtypeStruct(((depth + inner) // 4, width), BF16)
    outs = pl.pallas_call(
        back_one_kernel,
        out_shape=(
            jax.ShapeDtypeStruct((rows, width), F32),
            jax.ShapeDtypeStruct((rows, width), BF16),
            jax.ShapeDtypeStruct((2, width), F32),
            jax.ShapeDtypeStruct((depth, rows), BF16),
            part,
            part,
            part,
            part,
        ),
        in_specs=smem(3) + vmem(11),
        out_specs=tuple(vmem(4) + anywhere(4)),
        scratch_shapes=back_scratch(depth, inner, width),
        name="back_one",
        **settings(),
    )(ends, first, places, middle, mine, other, cot, vectors, *shared, *slot)
    return outs[:4], outs[4:]


def back_two(ends, first, places, branch, x, shared, grad_one, w_one, slot, sums):
    rows, width = branch.shape
    depth, inner = slot[0].shape[0], shared[2].shape[0] // 2
    part = jax.ShapeDtypeStruct(((depth + inner) // 4 + PAD, width), BF16)
    outs = pl.pallas_call(
        back_two_kernel,
        out_shape=(
            jax.ShapeDtypeStruct((rows, width), BF16),
            part,
            part,
            part,
            part,
        ),
        in_specs=smem(3) + vmem(11),
        out_specs=tuple(vmem(1) + anywhere(4)),
        scratch_shapes=[pltpu.VMEM((depth, rows), BF16)] + back_scratch(depth, inner, width),
        name="back_two",
        **settings(),
    )(ends, first, places, branch, x, *shared, grad_one, w_one, *slot, sums)
    return outs[0], outs[1:]


def settle_some_kernel(order_ref, *refs):
    pieces, others_ref, outs = refs[:3], refs[3], refs[4:]
    up_ref, down_ref, qkv_ref, proj_ref, sums_ref = outs
    feed_rows = up_ref.shape[0] // 4
    qkv_rows, proj_rows = qkv_ref.shape[0] // 4, proj_ref.shape[0] // 4
    size = pieces[0].shape[0]
    early = size - feed_rows - PAD
    late = qkv_rows - early

    def put(out, index, rows, offset, count, value):
        start = pl.multiple_of(order_ref[index] * rows + offset, 8)
        out[pl.ds(start, count), :] = value.astype(F32)

    def first_half(index, ref, base):
        put(up_ref, index, feed_rows, 0, feed_rows, ref[base : base + feed_rows, :])
        base = base + feed_rows
        put(sums_ref, index, PAD, 0, PAD, ref[base : base + PAD, :])
        put(qkv_ref, index, qkv_rows, 0, early, ref[base + PAD : base + PAD + early, :])

    def second_half(index, ref, base):
        put(down_ref, index, feed_rows, 0, feed_rows, ref[base : base + feed_rows, :])
        base = base + feed_rows
        put(qkv_ref, index, qkv_rows, early, late, ref[base : base + late, :])
        base = base + late
        put(proj_ref, index, proj_rows, 0, proj_rows, ref[base : base + proj_rows, :])

    halves = (first_half, second_half)
    for core in range(2):

        @pl.when(order_ref[5] == core)
        def _():
            for index, piece in enumerate(pieces):
                halves[core](index, piece, 0)
                halves[1 - core](index, others_ref, CROSSED[index] * size)


def settle_last_kernel(order_ref, piece_ref, others_ref, *refs):
    outs, buffers, sems = refs[5:10], refs[10:15], refs[15]
    up, down, qkv, proj, sums = buffers
    size, feed_rows = piece_ref.shape[0], up.shape[0]
    early = size - feed_rows - PAD
    late = qkv.shape[0] - early

    def first_half(ref):
        up[...] = ref[:feed_rows, :].astype(F32)
        sums[...] = ref[feed_rows : feed_rows + PAD, :].astype(F32)
        qkv[:early, :] = ref[feed_rows + PAD :, :].astype(F32)

    def second_half(ref):
        down[...] = ref[:feed_rows, :].astype(F32)
        qkv[early:, :] = ref[feed_rows : feed_rows + late, :].astype(F32)
        proj[...] = ref[feed_rows + late : feed_rows + late + proj.shape[0], :].astype(F32)

    @pl.when(order_ref[5] == 0)
    def _():
        first_half(piece_ref)
        second_half(others_ref)

    @pl.when(order_ref[5] == 1)
    def _():
        first_half(others_ref)
        second_half(piece_ref)

    copies = []
    for i, (buffer, out) in enumerate(zip(buffers, outs)):
        rows = buffer.shape[0]
        start = pl.multiple_of(order_ref[3] * rows, 8)
        copies.append(pltpu.make_async_copy(buffer, out.at[pl.ds(start, rows)], sems.at[i]))
    for copy in copies:
        copy.start()
    for copy in copies:
        copy.wait()


def settle(order, pieces, others, sizes, settled):
    width, units, depth, inner = sizes
    shapes = [(width, units), (units, width), (depth, width), (inner, width), (4 * PAD, width)]
    out_shape = tuple(jax.ShapeDtypeStruct(shape, F32) for shape in shapes)
    if not settled:
        return pl.pallas_call(
            settle_some_kernel,
            out_shape=out_shape,
            in_specs=smem(1) + vmem(4),
            out_specs=tuple(vmem(5)),
            name="settle",
            **settings(),
        )(order, *pieces, others)
    return pl.pallas_call(
        settle_last_kernel,
        out_shape=out_shape,
        in_specs=smem(1) + vmem(2) + anywhere(5),
        out_specs=tuple(anywhere(5)),
        scratch_shapes=[pltpu.VMEM((rows // 4, columns), F32) for rows, columns in shapes]
        + [pltpu.SemaphoreType.DMA((5,))],
        input_output_aliases={3 + i: i for i in range(5)},
        name="settle_last",
        **settings(),
    )(order, *pieces, others, *settled)


def spread(piece, *before):
    near = lax.ppermute(piece, LAYER, FIRST)
    side = lax.ppermute(piece, LAYER, SECOND)
    far = lax.ppermute(after(near, side, *before) if before else near, LAYER, SECOND)
    return piece, near, side, far


def scatter_at_once(far, near, side, keep):
    return keep, tuple(
        lax.ppermute(part, LAYER, pairs)
        for part, pairs in ((near, FIRST), (side, SECOND), (far, BOTH))
    )


def add_low(*parts):
    total = parts[0].astype(F32)
    for part in parts[1:]:
        total = total + part.astype(F32)
    return total.astype(BF16)


def to_shard(sum_one, sum_two):
    return (
        lax.ppermute(sum_one, CORE_T, ROUND_ONE_BACK),
        lax.ppermute(sum_two, CORE_T, ROUND_TWO_BACK),
    )


def over_outer(share, outer):
    return lax.psum(share.astype(F32), "o").astype(BF16) if outer > 1 else share


def half_rows(parts, place):
    rows = parts[0].shape[0] // 2
    return add_low(*(lax.dynamic_slice_in_dim(part, place * rows, rows, 0) for part in parts))


def after(value, *others):
    return lax.optimization_barrier((value,) + others)[0] if others else value


def local(
    patches,
    item_patches,
    attn_gain,
    attn_bias,
    qkv_weight,
    proj_weight,
    mlp_gain,
    mlp_bias,
    up_weight,
    up_bias,
    down_weight,
    cotangent,
):
    c, t, x, y = (lax.axis_index(name) for name in ("c", "t", "x", "y"))
    outer = lax.axis_size("o")
    quarter = 2 * y + x
    member = t & 1
    own_rows, width = patches.shape
    first_bit = 1 + c
    home = (t // 2 == c).astype(jnp.int32)
    order = jnp.stack([quarter, quarter ^ first_bit, quarter ^ (3 - first_bit), quarter ^ 3, home, c])
    steps = jnp.arange(4) ^ quarter
    places = jnp.where(
        steps == 3, 0, jnp.where(steps == first_bit, 1, jnp.where(steps == 0, 3, 2))
    )

    def exchange(array):
        return lax.ppermute(array, "c", SWAP)

    def both_halves(array, *before):
        other = exchange(after(array, *before))
        return jnp.where(
            c == 0, jnp.concatenate([array, other], 0), jnp.concatenate([other, array], 0)
        )

    def cut(array):
        rows = array.shape[0] // 4
        return lax.dynamic_slice_in_dim(array, quarter * rows, rows, 0)

    qkv_t = qkv_weight.T
    depth, units, inner = qkv_t.shape[0], down_weight.shape[0], proj_weight.shape[0]
    piece_a = jnp.concatenate([cut(qkv_t), cut(proj_weight)], 0)
    half_a = piece_a.shape[0] // 2
    piece_a_two = lax.dynamic_slice_in_dim(piece_a, home * half_a, half_a, 0)
    piece_a, piece_a_two, patches = lax.optimization_barrier((piece_a, piece_a_two, patches))
    a_one = lax.ppermute(piece_a, CORE_T, ROUND_ONE)
    a_two = lax.ppermute(piece_a_two, CORE_T, ROUND_TWO)
    inputs = lax.ppermute(patches, CORE_T, ROW_SWAP)
    items = exchange(item_patches)
    ends = jnp.cumsum(jnp.where(member == c, item_patches, items)[0])
    first = (t // 2 * BLOCK).astype(jnp.int32).reshape(1)
    vectors = jnp.stack([attn_gain, attn_bias, mlp_gain, mlp_bias])
    bias_rows = jnp.broadcast_to(up_bias[None, :], (PAD, units))
    cut_up, cut_down = cut(up_weight), cut(down_weight)
    piece_b = jnp.concatenate([cut_up, cut_down, bias_rows], 0)
    half_b = jnp.concatenate([jnp.where(home == 1, cut_down, cut_up), bias_rows], 0)
    block_in = both_halves(inputs)
    a_one, a_two, block_in, ends, first, order, places, vectors, piece_b, half_b, bias_rows = (
        lax.optimization_barrier(
            (a_one, a_two, block_in, ends, first, order, places, vectors, piece_b, half_b, bias_rows)
        )
    )
    b_one = lax.ppermute(piece_b, CORE_T, ROUND_ONE)
    b_two = lax.ppermute(half_b, CORE_T, ROUND_TWO)
    pieces_a = spread(jnp.concatenate([a_one, a_two], 0))
    crossed_a = lax.ppermute(
        jnp.concatenate([piece[2 * half_a :] for piece in pieces_a], 0), "c", SWAP
    )
    both_b = jnp.concatenate([b_one, b_two], 0)
    shared, one, two = attention(
        ends, first, order, after(block_in, both_b), vectors, (qkv_t, proj_weight), pieces_a, crossed_a
    )
    normed, mine, heads_out, proj = shared
    shared = (normed, heads_out, proj)
    pieces_b = spread(both_b, mine)
    other = exchange(mine)
    block_cot = both_halves(lax.ppermute(after(cotangent, both_b), CORE_T, ROW_SWAP), mine)
    crossed_b = exchange(jnp.concatenate([piece[piece_b.shape[0] :] for piece in pieces_b[:3]], 0))
    crossed_far = exchange(pieces_b[3][piece_b.shape[0] :])
    middle, out_part, back_part, bias_one, bias_two, send, keep, send_last, keep_last = feed(
        order, places, block_in, mine, other, block_cot, vectors,
        (up_weight, down_weight, bias_rows), pieces_b, crossed_b, crossed_far,
    )
    hop = lax.ppermute(send, LAYER, FIRST)

    def own(array):
        return lax.dynamic_slice_in_dim(array, c * own_rows, own_rows, 0)

    (middle_grad, branch, mlp_sums, grad_one), back_one_out = back_one(
        ends, first, places, middle, back_part, exchange(back_part), block_cot, vectors, shared, one
    )
    hop = after(hop, branch)
    hop_last = lax.ppermute(after(send_last, hop), LAYER, FIRST)
    next_hop = add_low(keep[0], hop[0])
    far = lax.ppermute(next_hop, LAYER, SECOND)
    keep_one, got_one = scatter_at_once(*back_one_out)
    slot_one = 2 * c + jnp.where(t // 2 == c, 1 - member, member ^ c)
    shards = jnp.arange(4)[:, None]
    bias_part = jnp.where(shards == slot_one, bias_one, 0.0) + jnp.where(
        shards == (slot_one ^ 1), bias_two, 0.0
    )
    small = jnp.concatenate([mlp_sums, bias_part], 0)
    first_part, back_two_out = back_two(
        ends, first, places, after(branch, next_hop), block_in, shared, grad_one, one[0], two, small
    )
    far, hop_last = after((far, hop_last), first_part)
    far_last = lax.ppermute(add_low(keep_last[0], hop_last[0]), LAYER, SECOND)
    feed_sum = add_low(keep[1], hop[1], far)
    size = (width + units) // 4
    feed_sums = (
        feed_sum[:size],
        jnp.concatenate([feed_sum[size:], add_low(keep_last[1], hop_last[1], far_last)], 0),
    )
    feed_parts = to_shard(*feed_sums)
    keep_one, back_two_out, first_part, out_part, _ = lax.optimization_barrier(
        (keep_one, back_two_out, first_part, out_part, feed_sum)
    )
    keep_two, got_two = scatter_at_once(*back_two_out)

    unit, inverse = normal(inputs.astype(F32))
    first_grad = own(first_part).astype(F32) + own(exchange(first_part)).astype(F32)
    scaled = first_grad * attn_gain
    mean_one = jnp.mean(scaled, axis=-1, keepdims=True)
    mean_two = jnp.mean(scaled * unit, axis=-1, keepdims=True)
    grad_in = own(middle_grad) + (scaled - mean_one - unit * mean_two) * inverse
    grad_in = grad_in.astype(BF16)
    result = own(middle) + own(out_part).astype(F32) + own(exchange(out_part)).astype(F32)
    result = result.astype(BF16)
    got_one, got_two = after((got_one, got_two), feed_parts)
    back_sum_two = add_low(keep_two, *got_two)
    small = add_low(back_sum_two[:PAD], exchange(back_sum_two[:PAD]))
    blank = jnp.zeros((PAD, width), BF16)
    back_sum_one = jnp.concatenate([small, add_low(keep_one, *got_one), blank], 0)
    back_sum_two = jnp.concatenate([small, back_sum_two[PAD:], blank], 0)
    back_parts = to_shard(back_sum_one, back_sum_two)

    def halves(place):
        return jnp.concatenate([half_rows(feed_parts, place), half_rows(back_parts, place)], 0)

    share = add_low(halves(c), exchange(halves(1 - c)))
    share = over_outer(share, outer)
    share, grad_in, result = lax.optimization_barrier((share, grad_in, result))
    patches_grad = lax.ppermute(grad_in, CORE_T, ROW_SWAP).astype(F32)
    result = lax.ppermute(result, CORE_T, ROW_SWAP)
    near = lax.ppermute(share, LAYER, FIRST)
    side = lax.ppermute(share, LAYER, SECOND)
    near, side, patches_grad, result = lax.optimization_barrier((near, side, patches_grad, result))
    far = lax.ppermute(near, LAYER, SECOND)
    others = exchange(jnp.concatenate([share, near, side], 0))
    settled = settle(order, (share, near, side), others, (width, units, depth, inner), ())
    far, *settled = lax.optimization_barrier((far, *settled))
    up_sum, down_sum, qkv_sum, proj_sum, sums = settle(
        order, (far,), exchange(far), (width, units, depth, inner), settled
    )
    sums = sums.reshape(4, PAD, width)[:, :2].reshape(8, width)
    up_bias_sum = lax.dynamic_index_in_dim(sums, 4 + t, 0, keepdims=False)
    return (
        result,
        patches_grad,
        sums[0],
        sums[1],
        qkv_sum.T,
        proj_sum,
        sums[2],
        sums[3],
        up_sum,
        up_bias_sum,
        down_sum,
    )


def solution(mesh):
    dp, tensor = mesh.shape["dp"], mesh.shape["tensor"]
    grid = Mesh(mesh.devices.reshape(dp // 8, 2, 2, 2, tensor), ("o", "y", "x", "c", "t"))
    dp_axes = ("o", "y", "x", "c")
    rows = P(dp_axes + ("t",), None)
    return jax.shard_map(
        local,
        mesh=grid,
        in_specs=(
            rows,
            P(dp_axes, None),
            P(),
            P(),
            P(None, "t"),
            P("t", None),
            P(),
            P(),
            P(None, "t"),
            P("t"),
            P("t", None),
            rows,
        ),
        out_specs=(
            rows,
            rows,
            P(),
            P(),
            P(None, "t"),
            P("t", None),
            P(),
            P(),
            P(None, "t"),
            P("t"),
            P("t", None),
        ),
        check_vma=False,
    )
```

```python
import jax
import jax.numpy as jnp
from jax import lax
from jax.experimental import pallas as pl
from jax.experimental.pallas import tpu as pltpu
from jax.sharding import Mesh
from jax.sharding import PartitionSpec as P

HEAD_DIM = 64
BLOCK = 784
NORM_EPS = 1e-06
SCALE = HEAD_DIM**-0.5
LOG2E = 1.4426950408889634
F32 = jnp.float32
BF16 = jnp.bfloat16
VMEM_LIMIT = 30 * 1024 * 1024
SWAP = [(0, 1), (1, 0)]
PAD = 16

CORE_T = ("c", "t")
ROUND_ONE = [(0, 1), (4, 2), (1, 0), (5, 3), (6, 7), (2, 5), (7, 6), (3, 4)]
ROUND_TWO = [(4, 3), (5, 2), (2, 4), (3, 5), (0, 7), (1, 6), (6, 0), (7, 1)]
ROUND_ONE_BACK = [(b, a) for a, b in ROUND_ONE]
ROUND_TWO_BACK = [(3, 4), (2, 5), (4, 2), (5, 3), (0, 0), (1, 1), (6, 6), (7, 7)]
ROW_SWAP = [(4, 1), (1, 4), (6, 3), (3, 6), (0, 0), (2, 2), (5, 5), (7, 7)]
LAYER = ("y", "x", "c")
FIRST = [(i, i ^ (4 if i & 1 else 2)) for i in range(8)]
SECOND = [(i, i ^ (2 if i & 1 else 4)) for i in range(8)]
BOTH = [(i, i ^ 6) for i in range(8)]


def dot(left, right, left_dim=1, right_dim=0):
    return lax.dot_general(
        left, right, (((left_dim,), (right_dim,)), ((), ())), preferred_element_type=F32
    )


def normal(rows):
    centre = rows - jnp.mean(rows, axis=-1, keepdims=True)
    spread = jnp.mean(centre * centre, axis=-1, keepdims=True)
    inverse = lax.rsqrt(spread + NORM_EPS)
    return centre * inverse, inverse


def row_labels(ends_ref, first, shape, dim):
    places = lax.broadcasted_iota(jnp.int32, shape, dim) + first
    labels = jnp.zeros(shape, jnp.int32)
    for slot in range(ends_ref.shape[0]):
        labels = labels + (places >= ends_ref[slot]).astype(jnp.int32)
    return labels


def smem(count):
    return [pl.BlockSpec(memory_space=pltpu.SMEM)] * count


def vmem(count):
    return [pl.BlockSpec(memory_space=pltpu.VMEM)] * count


def anywhere(count):
    return [pl.BlockSpec(memory_space=pl.ANY)] * count


def settings(limit=VMEM_LIMIT):
    return dict(
        compiler_params=pltpu.CompilerParams(vmem_limit_bytes=limit),
        cost_estimate=pl.CostEstimate(
            flops=int(1e9), bytes_accessed=int(1e6), transcendentals=0
        ),
    )


def heads_forward(labels, normed_ref, w_ref, packed_ref, heads_ref, base_head, lse_ref):
    rows = normed_ref.shape[0]
    label_col, label_row = labels

    def head(h):
        part = slice(h * 3 * HEAD_DIM, (h + 1) * 3 * HEAD_DIM)
        packed = dot(w_ref[part, :], normed_ref[...], 1, 1).astype(BF16)
        packed_ref[part, :] = packed
        queries = packed[:HEAD_DIM] * SCALE
        key_rows = packed[HEAD_DIM : 2 * HEAD_DIM].T
        values = packed[2 * HEAD_DIM :]
        scores = dot(key_rows, queries) * LOG2E
        scores = jnp.where(label_col == label_row, scores, -1e30)
        top = jnp.max(scores, axis=0, keepdims=True)
        weights = jnp.exp2(scores - top)
        total = jnp.sum(weights, axis=0, keepdims=True)
        mixed = dot(values, weights.astype(BF16)) * (1.0 / total)
        start = (h + base_head) * HEAD_DIM
        heads_ref[start : start + HEAD_DIM, :] = mixed.astype(BF16)
        lse_ref[h : h + 1, :] = top + jnp.log2(total)

    for h in range(w_ref.shape[0] // (3 * HEAD_DIM)):
        head(h)


CROSSED = (0, 2, 1, 3)


def place(order_ref, index, rows):
    return pl.ds(pl.multiple_of(order_ref[index] * rows, 16), rows)


def attention_kernel(*refs):
    ends_ref, first_ref, order_ref, x_ref, vectors_ref, own_w_ref, own_proj_ref = refs[:7]
    pieces, crossed_ref, refs = refs[7:11], refs[11], refs[12:]
    normed_ref, mine_ref, heads_ref, proj_ref = refs[:4]
    w_one, packed_one, lse_one, w_two, packed_two, lse_two = refs[4:]
    rows = x_ref.shape[0]
    depth, inner = own_w_ref.shape[0], own_proj_ref.shape[0]
    w_rows, p_rows = depth // 4, inner // 4
    size = w_rows + p_rows
    half = size // 2
    rest = w_rows - half
    for index, piece in enumerate(pieces):
        w_one[place(order_ref, index, w_rows), :] = piece[:w_rows, :]
        proj_ref[place(order_ref, index, p_rows), :] = piece[w_rows:size, :]

    @pl.when(order_ref[4] == 1)
    def _():
        w_two[...] = own_w_ref[...]
        proj_ref[inner:, :] = own_proj_ref[...]

    @pl.when(order_ref[4] == 0)
    def _():
        for index, piece in enumerate(pieces):
            base = pl.multiple_of(order_ref[index] * w_rows, 16)
            w_two[pl.ds(base, half), :] = piece[size:, :]
            start = CROSSED[index] * half
            w_two[pl.ds(base + half, rest), :] = crossed_ref[start : start + rest, :]
            base = pl.multiple_of(order_ref[index] * p_rows + inner, 16)
            proj_ref[pl.ds(base, p_rows), :] = crossed_ref[start + rest : start + half, :]

    unit, _ = normal(x_ref[...].astype(F32))
    normed_ref[...] = (unit * vectors_ref[0:1, :] + vectors_ref[1:2, :]).astype(BF16)
    labels = [row_labels(ends_ref, first_ref[0], shape, dim) for dim, shape in ((0, (rows, 1)), (1, (1, rows)))]
    heads_forward(labels, normed_ref, w_one, packed_one, heads_ref, 0, lse_one)
    heads_forward(labels, normed_ref, w_two, packed_two, heads_ref, inner // HEAD_DIM, lse_two)
    mine_ref[...] = dot(heads_ref[...], proj_ref[...], 0, 0).astype(BF16)


def attention(ends, first, order, x, vectors, own, pieces, crossed):
    rows, width = x.shape
    depth, inner = own[0].shape[0], own[1].shape[0]
    rows_low = jax.ShapeDtypeStruct((rows, width), BF16)
    slot = (
        jax.ShapeDtypeStruct((depth, width), BF16),
        jax.ShapeDtypeStruct((depth, rows), BF16),
        jax.ShapeDtypeStruct((8, rows), F32),
    )
    outs = pl.pallas_call(
        attention_kernel,
        out_shape=(
            rows_low,
            rows_low,
            jax.ShapeDtypeStruct((2 * inner, rows), BF16),
            jax.ShapeDtypeStruct((2 * inner, width), BF16),
        )
        + slot
        + slot,
        in_specs=smem(3) + vmem(9),
        out_specs=tuple(vmem(10)),
        name="attention",
        **settings(),
    )(ends, first, order, x, vectors, *own, *pieces, crossed)
    return outs[:4], outs[4:7], outs[7:]


def feed_slot(places_ref, second, second_t, cot_ref, cot_t, up, down, bias, grads, bias_grad):
    width, units = up.shape
    d_rows, u_rows = units // 4, width // 4
    pre = dot(second[...], up[...]) + bias[...].astype(F32)[0:1]
    gate = 0.5 * (1.0 + lax.erf(pre * (2.0**-0.5)))
    slope = gate + pre * (jnp.exp2(pre * pre * (-0.5 * LOG2E)) * (0.5 / 3.141592653589793) ** 0.5)
    hidden = (pre * gate).astype(BF16)
    out = dot(hidden, down[...])
    down_grad = dot(cot_t[...], hidden).T.astype(BF16)
    for i in range(4):
        grads[places_ref[i], u_rows:, :] = down_grad[i * d_rows : (i + 1) * d_rows]
    act = (dot(cot_ref[...], down[...], 1, 1) * slope).astype(BF16)
    bias_grad[...] = jnp.sum(act.astype(F32), axis=0, keepdims=True)
    back = dot(act, up[...], 1, 1)
    up_grad = dot(second_t[...], act).astype(BF16)
    for i in range(4):
        grads[places_ref[i], :u_rows, :] = up_grad[i * u_rows : (i + 1) * u_rows]
    return out, back


def fetch(source, target, sem):
    copy = pltpu.make_async_copy(source, target, sem)
    copy.start()
    return copy


def wait_all(copies):
    for copy in copies:
        copy.wait()


def feed_kernel(*refs):
    order_ref, places_ref, vectors_ref, x_hbm, mine_hbm, other_hbm, cot_hbm = refs[:7]
    own_up_hbm, own_down_hbm, own_bias_hbm, pieces, crossed_hbm, far_hbm, refs = (
        refs[7], refs[8], refs[9], refs[10:14], refs[14], refs[15], refs[16:],
    )
    middle_hbm, out_ref, back_ref, bias_one, bias_two, *leave_refs = refs[:9]
    x_ref, mine_ref, other_ref, cot_ref, middle_ref, second, second_t, cot_t, up, down, bias, grads, out_sum, back_sum, sems = refs[9:]
    _, width, units = up.shape
    u_rows, d_rows = width // 4, units // 4
    size = u_rows + d_rows + PAD
    half = u_rows + PAD
    free = iter(range(40))
    sem = lambda: sems.at[next(free)]
    early = [fetch(*pair, sem()) for pair in ((x_hbm, x_ref), (mine_hbm, mine_ref), (other_hbm, other_ref))]
    first = [fetch(pieces[0].at[pl.ds(size - PAD, PAD)], bias.at[0], sem())]
    for index, piece in enumerate(pieces):
        first.append(fetch(piece.at[pl.ds(0, u_rows)], up.at[0, place(order_ref, index, u_rows)], sem()))
        first.append(fetch(piece.at[pl.ds(u_rows, d_rows)], down.at[0, place(order_ref, index, d_rows)], sem()))
    cot_copy = fetch(cot_hbm, cot_ref, sem())
    home = [
        pltpu.make_async_copy(own_up_hbm, up.at[1], sem()),
        pltpu.make_async_copy(own_down_hbm, down.at[1], sem()),
        pltpu.make_async_copy(own_bias_hbm, bias.at[1], sem()),
    ]
    away = [pltpu.make_async_copy(pieces[0].at[pl.ds(size + u_rows, PAD)], bias.at[1], sem())]
    for index, piece in enumerate(pieces):
        part = piece.at[pl.ds(size, u_rows)]
        away.append(pltpu.make_async_copy(part, up.at[1, place(order_ref, index, u_rows)], sem()))
        part = far_hbm if index == 3 else crossed_hbm.at[pl.ds(CROSSED[index] * half, half)]
        part = part.at[pl.ds(0, d_rows)]
        away.append(pltpu.make_async_copy(part, down.at[1, place(order_ref, index, d_rows)], sem()))

    @pl.when(order_ref[4] == 1)
    def _():
        for copy in home:
            copy.start()

    @pl.when(order_ref[4] == 0)
    def _():
        for copy in away:
            copy.start()

    wait_all(early)
    middle = x_ref[...].astype(F32) + (mine_ref[...].astype(F32) + other_ref[...].astype(F32))
    middle_ref[...] = middle
    late = [fetch(middle_ref, middle_hbm, sem())]
    unit, _ = normal(middle)
    low = (unit * vectors_ref[2:3, :] + vectors_ref[3:4, :]).astype(BF16)
    second[...] = low
    second_t[...] = low.T
    cot_copy.wait()
    cot_t[...] = cot_ref[...].T
    wait_all(first)
    def leave(slot, start, rows, refs, target):
        return [
            fetch(
                grads.at[slot, pl.ds(2 * part, 2), pl.ds(start, rows)],
                ref.at[:, pl.ds(target, rows)],
                sem(),
            )
            for part, ref in enumerate(refs)
        ]

    shared = (places_ref, second, second_t, cot_ref, cot_t)
    out, back = feed_slot(*shared, up.at[0], down.at[0], bias.at[0], grads.at[0], bias_one)
    out_sum[...] = out
    back_sum[...] = back
    late += leave(0, 0, u_rows + d_rows, leave_refs[:2], 0)

    @pl.when(order_ref[4] == 1)
    def _():
        wait_all(home)

    @pl.when(order_ref[4] == 0)
    def _():
        wait_all(away)

    out, back = feed_slot(*shared, up.at[1], down.at[1], bias.at[1], grads.at[1], bias_two)
    late += leave(1, 0, u_rows, leave_refs[:2], u_rows + d_rows)
    late += leave(1, u_rows, d_rows, leave_refs[2:], 0)
    out_ref[...] = (out_sum[...] + out).astype(BF16)
    back_ref[...] = (back_sum[...] + back).astype(BF16)
    wait_all(late)


def feed(order, places, x, mine, other, cot, vectors, own, pieces, crossed, crossed_far):
    rows, width = x.shape
    units = own[1].shape[0]
    size = (width + units) // 4
    rows_low = jax.ShapeDtypeStruct((rows, width), BF16)
    rows_full = jax.ShapeDtypeStruct((rows, width), F32)
    most = jax.ShapeDtypeStruct((2, size + width // 4, width), BF16)
    least = jax.ShapeDtypeStruct((2, units // 4, width), BF16)
    bias_grad = jax.ShapeDtypeStruct((1, units), F32)
    return pl.pallas_call(
        feed_kernel,
        out_shape=(rows_full, rows_low, rows_low, bias_grad, bias_grad, most, most, least, least),
        in_specs=smem(2) + vmem(1) + anywhere(13),
        out_specs=tuple(anywhere(1) + vmem(4) + anywhere(4)),
        scratch_shapes=[pltpu.VMEM((rows, width), BF16)] * 4
        + [
            pltpu.VMEM((rows, width), F32),
            pltpu.VMEM((rows, width), BF16),
            pltpu.VMEM((width, rows), BF16),
            pltpu.VMEM((width, rows), BF16),
            pltpu.VMEM((2, width, units), BF16),
            pltpu.VMEM((2, units, width), BF16),
            pltpu.VMEM((2, PAD, units), BF16),
            pltpu.VMEM((2, 4, size, width), BF16),
            pltpu.VMEM((rows, width), F32),
            pltpu.VMEM((rows, width), F32),
            pltpu.SemaphoreType.DMA((40,)),
        ],
        name="feed",
        **settings(44 * 1024 * 1024),
    )(order, places, vectors, x, mine, other, cot, *own, *pieces, crossed, crossed_far)


def heads_back(slot, labels, places_ref, branch_ref, normed_ref, w_ref, proj_ref, packed_ref, heads_ref,
               lse_ref, packed_grad, w_grad, grads):
    rows = branch_ref.shape[0]
    depth, inner = w_ref.shape[0], proj_ref.shape[0] // 2
    label_col, label_row = labels

    def head(h):
        base = h * 3 * HEAD_DIM
        part = slice(h * HEAD_DIM + slot * inner, (h + 1) * HEAD_DIM + slot * inner)
        mixed = heads_ref[part, :]
        mixed_grad = dot(proj_ref[part, :], branch_ref[...], 1, 1).astype(BF16)
        packed = packed_ref[base : base + 3 * HEAD_DIM, :]
        queries = packed[:HEAD_DIM] * SCALE
        keys = packed[HEAD_DIM : 2 * HEAD_DIM]
        key_rows = keys.T
        value_rows = packed[2 * HEAD_DIM :].T
        inner_sum = jnp.sum(mixed.astype(F32) * mixed_grad.astype(F32), axis=0, keepdims=True)
        scores = dot(key_rows, queries) * LOG2E
        scores = jnp.where(label_col == label_row, scores, -1e30)
        prob = jnp.exp2(scores - lse_ref[h : h + 1, :])
        value_grad = dot(mixed_grad, prob.astype(BF16), 1, 1)
        prob_grad = dot(value_rows, mixed_grad)
        score_grad = (prob * (prob_grad - inner_sum)).astype(BF16)
        query_grad = dot(keys, score_grad) * SCALE
        key_grad = dot(queries, score_grad, 1, 1)
        for i, grad in enumerate((query_grad, key_grad, value_grad)):
            start = base + i * HEAD_DIM
            packed_grad[start : start + HEAD_DIM, :] = grad.astype(BF16)

    for h in range(depth // (3 * HEAD_DIM)):
        head(h)
    w_grad[:depth, :] = dot(packed_grad[...], normed_ref[...]).astype(BF16)
    w_grad[depth:, :] = dot(heads_ref[slot * inner : (slot + 1) * inner, :], branch_ref[...]).astype(BF16)
    w_size, p_size = depth // 4, inner // 4
    size = w_size + p_size
    for i in range(4):
        grads[places_ref[i], PAD : PAD + w_size, :] = w_grad[i * w_size : (i + 1) * w_size, :]
        grads[places_ref[i], PAD + w_size : PAD + size, :] = w_grad[depth + i * p_size : depth + (i + 1) * p_size, :]


def send_grads(grads, start, out_refs, sems):
    copies = [
        pltpu.make_async_copy(grads.at[i, pl.ds(start, grads.shape[1] - start)], out_ref, sems.at[i])
        for i, out_ref in enumerate(out_refs)
    ]
    for copy in copies:
        copy.start()
    for copy in copies:
        copy.wait()


def back_one_kernel(
    ends_ref,
    first_ref,
    places_ref,
    middle_ref,
    mine_ref,
    other_ref,
    cot_ref,
    vectors_ref,
    normed_ref,
    heads_ref,
    proj_ref,
    w_ref,
    packed_ref,
    lse_ref,
    middle_grad_ref,
    branch_ref,
    sums_ref,
    packed_grad_ref,
    far_ref,
    near_ref,
    side_ref,
    keep_ref,
    w_grad,
    grads,
    sems,
):
    rows = middle_ref.shape[0]
    unit, inverse = normal(middle_ref[...])
    grad = mine_ref[...].astype(F32) + other_ref[...].astype(F32)
    sums_ref[0:1, :] = jnp.sum(grad * unit, axis=0, keepdims=True) * 0.5
    sums_ref[1:2, :] = jnp.sum(grad, axis=0, keepdims=True) * 0.5
    scaled = grad * vectors_ref[2:3, :]
    mean_one = jnp.mean(scaled, axis=-1, keepdims=True)
    mean_two = jnp.mean(scaled * unit, axis=-1, keepdims=True)
    middle_grad = cot_ref[...].astype(F32) + (scaled - mean_one - unit * mean_two) * inverse
    middle_grad_ref[...] = middle_grad
    branch_ref[...] = middle_grad.astype(BF16)
    labels = [row_labels(ends_ref, first_ref[0], shape, dim) for dim, shape in ((0, (rows, 1)), (1, (1, rows)))]
    heads_back(0, labels, places_ref, branch_ref, normed_ref, w_ref, proj_ref, packed_ref, heads_ref,
                        lse_ref, packed_grad_ref, w_grad, grads)
    send_grads(grads, PAD, (far_ref, near_ref, side_ref, keep_ref), sems)


def back_two_kernel(
    ends_ref,
    first_ref,
    places_ref,
    branch_ref,
    normed_ref,
    heads_ref,
    proj_ref,
    w_ref,
    packed_ref,
    lse_ref,
    packed_grad_ref,
    far_ref,
    near_ref,
    side_ref,
    keep_ref,
    w_grad,
    grads,
    sems,
):
    rows = branch_ref.shape[0]
    labels = [row_labels(ends_ref, first_ref[0], shape, dim) for dim, shape in ((0, (rows, 1)), (1, (1, rows)))]
    heads_back(1, labels, places_ref, branch_ref, normed_ref, w_ref, proj_ref, packed_ref, heads_ref,
                        lse_ref, packed_grad_ref, w_grad, grads)
    send_grads(grads, PAD, (far_ref, near_ref, side_ref, keep_ref), sems)


def first_back_kernel(grad_one_ref, grad_two_ref, w_one_ref, w_two_ref, x_ref, first_grad_ref, sums_ref):
    grad = dot(grad_one_ref[...], w_one_ref[...], 0, 0) + dot(
        grad_two_ref[...], w_two_ref[...], 0, 0
    )
    first_grad_ref[...] = grad.astype(BF16)
    unit, _ = normal(x_ref[...].astype(F32))
    sums_ref[0:1, :] = jnp.sum(grad * unit, axis=0, keepdims=True)
    sums_ref[1:2, :] = jnp.sum(grad, axis=0, keepdims=True)


def first_back(grad_one, grad_two, w_one, w_two, x):
    return pl.pallas_call(
        first_back_kernel,
        out_shape=(
            jax.ShapeDtypeStruct(x.shape, BF16),
            jax.ShapeDtypeStruct((2, x.shape[1]), F32),
        ),
        in_specs=vmem(5),
        out_specs=tuple(vmem(2)),
        name="first_back",
        **settings(),
    )(grad_one, grad_two, w_one, w_two, x)


def back_scratch(depth, inner, width):
    return [
        pltpu.VMEM((depth + inner, width), BF16),
        pltpu.VMEM((4, PAD + (depth + inner) // 4, width), BF16),
        pltpu.SemaphoreType.DMA((4,)),
    ]


def back_one(ends, first, places, middle, mine, other, cot, vectors, shared, slot):
    rows, width = middle.shape
    depth, inner = slot[0].shape[0], shared[2].shape[0] // 2
    part = jax.ShapeDtypeStruct(((depth + inner) // 4, width), BF16)
    outs = pl.pallas_call(
        back_one_kernel,
        out_shape=(
            jax.ShapeDtypeStruct((rows, width), F32),
            jax.ShapeDtypeStruct((rows, width), BF16),
            jax.ShapeDtypeStruct((2, width), F32),
            jax.ShapeDtypeStruct((depth, rows), BF16),
            part,
            part,
            part,
            part,
        ),
        in_specs=smem(3) + vmem(11),
        out_specs=tuple(vmem(4) + anywhere(4)),
        scratch_shapes=back_scratch(depth, inner, width),
        name="back_one",
        **settings(),
    )(ends, first, places, middle, mine, other, cot, vectors, *shared, *slot)
    return outs[:4], outs[4:]


def back_two(ends, first, places, branch, shared, slot):
    rows, width = branch.shape
    depth, inner = slot[0].shape[0], shared[2].shape[0] // 2
    part = jax.ShapeDtypeStruct(((depth + inner) // 4, width), BF16)
    outs = pl.pallas_call(
        back_two_kernel,
        out_shape=(jax.ShapeDtypeStruct((depth, rows), BF16), part, part, part, part),
        in_specs=smem(3) + vmem(7),
        out_specs=tuple(vmem(1) + anywhere(4)),
        scratch_shapes=back_scratch(depth, inner, width),
        name="back_two",
        **settings(),
    )(ends, first, places, branch, *shared, *slot)
    return outs[0], outs[1:]


def settle_some_kernel(order_ref, *refs):
    pieces, others_ref, outs = refs[:3], refs[3], refs[4:]
    up_ref, down_ref, qkv_ref, proj_ref, sums_ref = outs
    feed_rows = up_ref.shape[0] // 4
    qkv_rows, proj_rows = qkv_ref.shape[0] // 4, proj_ref.shape[0] // 4
    size = pieces[0].shape[0]
    early = size - feed_rows - PAD
    late = qkv_rows - early

    def put(out, index, rows, offset, count, value):
        start = pl.multiple_of(order_ref[index] * rows + offset, 8)
        out[pl.ds(start, count), :] = value.astype(F32)

    def first_half(index, ref, base):
        put(up_ref, index, feed_rows, 0, feed_rows, ref[base : base + feed_rows, :])
        base = base + feed_rows
        put(sums_ref, index, PAD, 0, PAD, ref[base : base + PAD, :])
        put(qkv_ref, index, qkv_rows, 0, early, ref[base + PAD : base + PAD + early, :])

    def second_half(index, ref, base):
        put(down_ref, index, feed_rows, 0, feed_rows, ref[base : base + feed_rows, :])
        base = base + feed_rows
        put(qkv_ref, index, qkv_rows, early, late, ref[base : base + late, :])
        base = base + late
        put(proj_ref, index, proj_rows, 0, proj_rows, ref[base : base + proj_rows, :])

    halves = (first_half, second_half)
    for core in range(2):

        @pl.when(order_ref[5] == core)
        def _():
            for index, piece in enumerate(pieces):
                halves[core](index, piece, 0)
                halves[1 - core](index, others_ref, CROSSED[index] * size)


def settle_last_kernel(order_ref, piece_ref, others_ref, *refs):
    outs, buffers, sems = refs[5:10], refs[10:15], refs[15]
    up, down, qkv, proj, sums = buffers
    size, feed_rows = piece_ref.shape[0], up.shape[0]
    early = size - feed_rows - PAD
    late = qkv.shape[0] - early

    def first_half(ref):
        up[...] = ref[:feed_rows, :].astype(F32)
        sums[...] = ref[feed_rows : feed_rows + PAD, :].astype(F32)
        qkv[:early, :] = ref[feed_rows + PAD :, :].astype(F32)

    def second_half(ref):
        down[...] = ref[:feed_rows, :].astype(F32)
        qkv[early:, :] = ref[feed_rows : feed_rows + late, :].astype(F32)
        proj[...] = ref[feed_rows + late : feed_rows + late + proj.shape[0], :].astype(F32)

    @pl.when(order_ref[5] == 0)
    def _():
        first_half(piece_ref)
        second_half(others_ref)

    @pl.when(order_ref[5] == 1)
    def _():
        first_half(others_ref)
        second_half(piece_ref)

    copies = []
    for i, (buffer, out) in enumerate(zip(buffers, outs)):
        rows = buffer.shape[0]
        start = pl.multiple_of(order_ref[3] * rows, 8)
        copies.append(pltpu.make_async_copy(buffer, out.at[pl.ds(start, rows)], sems.at[i]))
    for copy in copies:
        copy.start()
    for copy in copies:
        copy.wait()


def settle(order, pieces, others, sizes, settled):
    width, units, depth, inner = sizes
    shapes = [(width, units), (units, width), (depth, width), (inner, width), (4 * PAD, width)]
    out_shape = tuple(jax.ShapeDtypeStruct(shape, F32) for shape in shapes)
    if not settled:
        return pl.pallas_call(
            settle_some_kernel,
            out_shape=out_shape,
            in_specs=smem(1) + vmem(4),
            out_specs=tuple(vmem(5)),
            name="settle",
            **settings(),
        )(order, *pieces, others)
    return pl.pallas_call(
        settle_last_kernel,
        out_shape=out_shape,
        in_specs=smem(1) + vmem(2) + anywhere(5),
        out_specs=tuple(anywhere(5)),
        scratch_shapes=[pltpu.VMEM((rows // 4, columns), F32) for rows, columns in shapes]
        + [pltpu.SemaphoreType.DMA((5,))],
        input_output_aliases={3 + i: i for i in range(5)},
        name="settle_last",
        **settings(),
    )(order, *pieces, others, *settled)


def spread(piece, *before):
    near = lax.ppermute(piece, LAYER, FIRST)
    side = lax.ppermute(piece, LAYER, SECOND)
    far = lax.ppermute(after(near, side, *before) if before else near, LAYER, SECOND)
    return piece, near, side, far


def scatter_at_once(far, near, side, keep):
    return keep, tuple(
        lax.ppermute(part, LAYER, pairs)
        for part, pairs in ((near, FIRST), (side, SECOND), (far, BOTH))
    )


def add_low(*parts):
    total = parts[0].astype(F32)
    for part in parts[1:]:
        total = total + part.astype(F32)
    return total.astype(BF16)


def to_shard(sum_one, sum_two):
    return (
        lax.ppermute(sum_one, CORE_T, ROUND_ONE_BACK),
        lax.ppermute(sum_two, CORE_T, ROUND_TWO_BACK),
    )


def over_outer(share, outer):
    return lax.psum(share.astype(F32), "o").astype(BF16) if outer > 1 else share


def half_rows(parts, place):
    rows = parts[0].shape[0] // 2
    return add_low(*(lax.dynamic_slice_in_dim(part, place * rows, rows, 0) for part in parts))


def after(value, *others):
    return lax.optimization_barrier((value,) + others)[0] if others else value


def local(
    patches,
    item_patches,
    attn_gain,
    attn_bias,
    qkv_weight,
    proj_weight,
    mlp_gain,
    mlp_bias,
    up_weight,
    up_bias,
    down_weight,
    cotangent,
):
    c, t, x, y = (lax.axis_index(name) for name in ("c", "t", "x", "y"))
    outer = lax.axis_size("o")
    quarter = 2 * y + x
    member = t & 1
    own_rows, width = patches.shape
    first_bit = 1 + c
    home = (t // 2 == c).astype(jnp.int32)
    order = jnp.stack([quarter, quarter ^ first_bit, quarter ^ (3 - first_bit), quarter ^ 3, home, c])
    steps = jnp.arange(4) ^ quarter
    places = jnp.where(
        steps == 3, 0, jnp.where(steps == first_bit, 1, jnp.where(steps == 0, 3, 2))
    )

    def exchange(array):
        return lax.ppermute(array, "c", SWAP)

    def both_halves(array, *before):
        other = exchange(after(array, *before))
        return jnp.where(
            c == 0, jnp.concatenate([array, other], 0), jnp.concatenate([other, array], 0)
        )

    def cut(array):
        rows = array.shape[0] // 4
        return lax.dynamic_slice_in_dim(array, quarter * rows, rows, 0)

    qkv_t = qkv_weight.T
    depth, units, inner = qkv_t.shape[0], down_weight.shape[0], proj_weight.shape[0]
    piece_a = jnp.concatenate([cut(qkv_t), cut(proj_weight)], 0)
    half_a = piece_a.shape[0] // 2
    piece_a_two = lax.dynamic_slice_in_dim(piece_a, home * half_a, half_a, 0)
    piece_a, piece_a_two, patches = lax.optimization_barrier((piece_a, piece_a_two, patches))
    a_one = lax.ppermute(piece_a, CORE_T, ROUND_ONE)
    a_two = lax.ppermute(piece_a_two, CORE_T, ROUND_TWO)
    inputs = lax.ppermute(patches, CORE_T, ROW_SWAP)
    items = exchange(item_patches)
    ends = jnp.cumsum(jnp.where(member == c, item_patches, items)[0])
    first = (t // 2 * BLOCK).astype(jnp.int32).reshape(1)
    vectors = jnp.stack([attn_gain, attn_bias, mlp_gain, mlp_bias])
    bias_rows = jnp.broadcast_to(up_bias[None, :], (PAD, units))
    cut_up, cut_down = cut(up_weight), cut(down_weight)
    piece_b = jnp.concatenate([cut_up, cut_down, bias_rows], 0)
    half_b = jnp.concatenate([jnp.where(home == 1, cut_down, cut_up), bias_rows], 0)
    block_in = both_halves(inputs)
    a_one, a_two, block_in, ends, first, order, places, vectors, piece_b, half_b, bias_rows = (
        lax.optimization_barrier(
            (a_one, a_two, block_in, ends, first, order, places, vectors, piece_b, half_b, bias_rows)
        )
    )
    b_one = lax.ppermute(piece_b, CORE_T, ROUND_ONE)
    b_two = lax.ppermute(half_b, CORE_T, ROUND_TWO)
    pieces_a = spread(jnp.concatenate([a_one, a_two], 0))
    crossed_a = lax.ppermute(
        jnp.concatenate([piece[2 * half_a :] for piece in pieces_a], 0), "c", SWAP
    )
    both_b = jnp.concatenate([b_one, b_two], 0)
    shared, one, two = attention(
        ends, first, order, after(block_in, both_b), vectors, (qkv_t, proj_weight), pieces_a, crossed_a
    )
    normed, mine, heads_out, proj = shared
    shared = (normed, heads_out, proj)
    pieces_b = spread(both_b, mine)
    other = exchange(mine)
    block_cot = both_halves(lax.ppermute(after(cotangent, both_b), CORE_T, ROW_SWAP), mine)
    crossed_b = exchange(jnp.concatenate([piece[piece_b.shape[0] :] for piece in pieces_b[:3]], 0))
    crossed_far = exchange(pieces_b[3][piece_b.shape[0] :])
    middle, out_part, back_part, bias_one, bias_two, send, keep, send_last, keep_last = feed(
        order, places, block_in, mine, other, block_cot, vectors,
        (up_weight, down_weight, bias_rows), pieces_b, crossed_b, crossed_far,
    )
    hop = lax.ppermute(send, LAYER, FIRST)

    def own(array):
        return lax.dynamic_slice_in_dim(array, c * own_rows, own_rows, 0)

    (middle_grad, branch, mlp_sums, grad_one), back_one_out = back_one(
        ends, first, places, middle, back_part, exchange(back_part), block_cot, vectors, shared, one
    )
    hop = after(hop, branch)
    hop_last = lax.ppermute(after(send_last, hop), LAYER, FIRST)
    next_hop = add_low(keep[0], hop[0])
    far = lax.ppermute(next_hop, LAYER, SECOND)
    keep_one, got_one = scatter_at_once(*back_one_out)
    grad_two, back_two_out = back_two(
        ends, first, places, after(branch, next_hop), shared, two
    )
    far, hop_last = after((far, hop_last), grad_two)
    far_last = lax.ppermute(add_low(keep_last[0], hop_last[0]), LAYER, SECOND)
    feed_sum = add_low(keep[1], hop[1], far)
    size = (width + units) // 4
    back_two_out, feed_sum, grad_two = lax.optimization_barrier((back_two_out, feed_sum, grad_two))
    part_one = lax.ppermute(feed_sum[:size], CORE_T, ROUND_ONE_BACK)
    keep_two, got_two = scatter_at_once(*back_two_out)
    first_part, attn_sums = first_back(grad_one, grad_two, one[0], two[0], block_in)
    far_last, out_part = after((far_last, out_part), first_part)
    feed_sum_two = jnp.concatenate(
        [feed_sum[size:], add_low(keep_last[1], hop_last[1], far_last)], 0
    )
    feed_parts = (part_one, lax.ppermute(feed_sum_two, CORE_T, ROUND_TWO_BACK))
    slot_one = 2 * c + jnp.where(t // 2 == c, 1 - member, member ^ c)
    shards = jnp.arange(4)[:, None]
    bias_part = jnp.where(shards == slot_one, bias_one, 0.0) + jnp.where(
        shards == (slot_one ^ 1), bias_two, 0.0
    )
    small = jnp.concatenate(
        [attn_sums, mlp_sums, bias_part, jnp.zeros((PAD - 8, width), F32)], 0
    ).astype(BF16)
    small = add_low(small, exchange(small))

    unit, inverse = normal(inputs.astype(F32))
    first_grad = own(first_part).astype(F32) + own(exchange(first_part)).astype(F32)
    scaled = first_grad * attn_gain
    mean_one = jnp.mean(scaled, axis=-1, keepdims=True)
    mean_two = jnp.mean(scaled * unit, axis=-1, keepdims=True)
    grad_in = own(middle_grad) + (scaled - mean_one - unit * mean_two) * inverse
    grad_in = grad_in.astype(BF16)
    result = own(middle) + own(out_part).astype(F32) + own(exchange(out_part)).astype(F32)
    result = result.astype(BF16)
    got_one, got_two = after((got_one, got_two), feed_parts)
    blank = jnp.zeros((PAD, width), BF16)
    back_sum_one = jnp.concatenate([small, add_low(keep_one, *got_one), blank], 0)
    back_sum_two = jnp.concatenate([small, add_low(keep_two, *got_two), blank], 0)
    back_parts = to_shard(back_sum_one, back_sum_two)

    def halves(place):
        return jnp.concatenate([half_rows(feed_parts, place), half_rows(back_parts, place)], 0)

    share = add_low(halves(c), exchange(halves(1 - c)))
    share = over_outer(share, outer)
    share, grad_in, result = lax.optimization_barrier((share, grad_in, result))
    patches_grad = lax.ppermute(grad_in, CORE_T, ROW_SWAP).astype(F32)
    result = lax.ppermute(result, CORE_T, ROW_SWAP)
    near = lax.ppermute(share, LAYER, FIRST)
    side = lax.ppermute(share, LAYER, SECOND)
    near, side, patches_grad, result = lax.optimization_barrier((near, side, patches_grad, result))
    far = lax.ppermute(near, LAYER, SECOND)
    others = exchange(jnp.concatenate([share, near, side], 0))
    settled = settle(order, (share, near, side), others, (width, units, depth, inner), ())
    far, *settled = lax.optimization_barrier((far, *settled))
    up_sum, down_sum, qkv_sum, proj_sum, sums = settle(
        order, (far,), exchange(far), (width, units, depth, inner), settled
    )
    sums = jnp.sum(sums.reshape(4, PAD, width)[:, :8], axis=0)
    up_bias_sum = lax.dynamic_index_in_dim(sums, 4 + t, 0, keepdims=False)
    return (
        result,
        patches_grad,
        sums[0],
        sums[1],
        qkv_sum.T,
        proj_sum,
        sums[2],
        sums[3],
        up_sum,
        up_bias_sum,
        down_sum,
    )


def solution(mesh):
    dp, tensor = mesh.shape["dp"], mesh.shape["tensor"]
    grid = Mesh(mesh.devices.reshape(dp // 8, 2, 2, 2, tensor), ("o", "y", "x", "c", "t"))
    dp_axes = ("o", "y", "x", "c")
    rows = P(dp_axes + ("t",), None)
    return jax.shard_map(
        local,
        mesh=grid,
        in_specs=(
            rows,
            P(dp_axes, None),
            P(),
            P(),
            P(None, "t"),
            P("t", None),
            P(),
            P(),
            P(None, "t"),
            P("t"),
            P("t", None),
            rows,
        ),
        out_specs=(
            rows,
            rows,
            P(),
            P(),
            P(None, "t"),
            P("t", None),
            P(),
            P(),
            P(None, "t"),
            P("t"),
            P("t", None),
        ),
        check_vma=False,
    )
```

```python
import jax
import jax.numpy as jnp
from jax import lax
from jax.experimental import pallas as pl
from jax.experimental.pallas import tpu as pltpu
from jax.sharding import Mesh
from jax.sharding import PartitionSpec as P

HEAD_DIM = 64
BLOCK = 784
NORM_EPS = 1e-06
SCALE = HEAD_DIM**-0.5
LOG2E = 1.4426950408889634
F32 = jnp.float32
BF16 = jnp.bfloat16
VMEM_LIMIT = 24 * 1024 * 1024
SWAP = [(0, 1), (1, 0)]
PAD = 16

CORE_T = ("c", "t")
ROUND_ONE = [(0, 1), (4, 2), (1, 0), (5, 3), (6, 7), (2, 5), (7, 6), (3, 4)]
ROUND_TWO = [(4, 3), (5, 2), (2, 4), (3, 5), (0, 7), (1, 6), (6, 0), (7, 1)]
ROUND_ONE_BACK = [(b, a) for a, b in ROUND_ONE]
ROUND_TWO_BACK = [(3, 4), (2, 5), (4, 2), (5, 3), (0, 0), (1, 1), (6, 6), (7, 7)]
ROW_SWAP = [(4, 1), (1, 4), (6, 3), (3, 6), (0, 0), (2, 2), (5, 5), (7, 7)]
LAYER = ("y", "x", "c")
FIRST = [(i, i ^ (4 if i & 1 else 2)) for i in range(8)]
SECOND = [(i, i ^ (2 if i & 1 else 4)) for i in range(8)]
BOTH = [(i, i ^ 6) for i in range(8)]


def dot(left, right, left_dim=1, right_dim=0):
    return lax.dot_general(
        left, right, (((left_dim,), (right_dim,)), ((), ())), preferred_element_type=F32
    )


def normal(rows):
    centre = rows - jnp.mean(rows, axis=-1, keepdims=True)
    spread = jnp.mean(centre * centre, axis=-1, keepdims=True)
    inverse = lax.rsqrt(spread + NORM_EPS)
    return centre * inverse, inverse


def row_labels(ends_ref, first, shape, dim):
    places = lax.broadcasted_iota(jnp.int32, shape, dim) + first
    labels = jnp.zeros(shape, jnp.int32)
    for slot in range(ends_ref.shape[0]):
        labels = labels + (places >= ends_ref[slot]).astype(jnp.int32)
    return labels


def smem(count):
    return [pl.BlockSpec(memory_space=pltpu.SMEM)] * count


def vmem(count):
    return [pl.BlockSpec(memory_space=pltpu.VMEM)] * count


def anywhere(count):
    return [pl.BlockSpec(memory_space=pl.ANY)] * count


def settings(limit=VMEM_LIMIT):
    return dict(
        compiler_params=pltpu.CompilerParams(vmem_limit_bytes=limit),
        cost_estimate=pl.CostEstimate(
            flops=int(1e9), bytes_accessed=int(1e6), transcendentals=0
        ),
    )


def heads_forward(labels, normed_ref, w_ref, packed_ref, heads_ref, base_head, lse_ref):
    rows = normed_ref.shape[0]
    label_col, label_row = labels

    def head(h):
        part = slice(h * 3 * HEAD_DIM, (h + 1) * 3 * HEAD_DIM)
        packed = dot(w_ref[part, :], normed_ref[...], 1, 1).astype(BF16)
        packed_ref[part, :] = packed
        queries = packed[:HEAD_DIM] * SCALE
        key_rows = packed[HEAD_DIM : 2 * HEAD_DIM].T
        values = packed[2 * HEAD_DIM :]
        scores = dot(key_rows, queries) * LOG2E
        scores = jnp.where(label_col == label_row, scores, -1e30)
        top = jnp.max(scores, axis=0, keepdims=True)
        weights = jnp.exp2(scores - top)
        total = jnp.sum(weights, axis=0, keepdims=True)
        mixed = dot(values, weights.astype(BF16)) * (1.0 / total)
        start = (h + base_head) * HEAD_DIM
        heads_ref[start : start + HEAD_DIM, :] = mixed.astype(BF16)
        lse_ref[h : h + 1, :] = top + jnp.log2(total)

    for h in range(w_ref.shape[0] // (3 * HEAD_DIM)):
        head(h)


CROSSED = (0, 2, 1, 3)


def place(order_ref, index, rows):
    return pl.ds(pl.multiple_of(order_ref[index] * rows, 16), rows)


def attention_kernel(*refs):
    ends_ref, first_ref, order_ref, x_ref, vectors_ref, own_w_ref, own_proj_ref = refs[:7]
    pieces, crossed_ref, refs = refs[7:11], refs[11], refs[12:]
    normed_ref, mine_ref, heads_ref, proj_ref = refs[:4]
    w_one, packed_one, lse_one, w_two, packed_two, lse_two = refs[4:]
    rows = x_ref.shape[0]
    depth, inner = own_w_ref.shape[0], own_proj_ref.shape[0]
    w_rows, p_rows = depth // 4, inner // 4
    size = w_rows + p_rows
    half = size // 2
    rest = w_rows - half
    for index, piece in enumerate(pieces):
        w_one[place(order_ref, index, w_rows), :] = piece[:w_rows, :]
        proj_ref[place(order_ref, index, p_rows), :] = piece[w_rows:size, :]

    @pl.when(order_ref[4] == 1)
    def _():
        w_two[...] = own_w_ref[...]
        proj_ref[inner:, :] = own_proj_ref[...]

    @pl.when(order_ref[4] == 0)
    def _():
        for index, piece in enumerate(pieces):
            base = pl.multiple_of(order_ref[index] * w_rows, 16)
            w_two[pl.ds(base, half), :] = piece[size:, :]
            start = CROSSED[index] * half
            w_two[pl.ds(base + half, rest), :] = crossed_ref[start : start + rest, :]
            base = pl.multiple_of(order_ref[index] * p_rows + inner, 16)
            proj_ref[pl.ds(base, p_rows), :] = crossed_ref[start + rest : start + half, :]

    unit, _ = normal(x_ref[...].astype(F32))
    normed_ref[...] = (unit * vectors_ref[0:1, :] + vectors_ref[1:2, :]).astype(BF16)
    labels = [row_labels(ends_ref, first_ref[0], shape, dim) for dim, shape in ((0, (rows, 1)), (1, (1, rows)))]
    heads_forward(labels, normed_ref, w_one, packed_one, heads_ref, 0, lse_one)
    heads_forward(labels, normed_ref, w_two, packed_two, heads_ref, inner // HEAD_DIM, lse_two)
    mine_ref[...] = dot(heads_ref[...], proj_ref[...], 0, 0).astype(BF16)


def attention(ends, first, order, x, vectors, own, pieces, crossed):
    rows, width = x.shape
    depth, inner = own[0].shape[0], own[1].shape[0]
    rows_low = jax.ShapeDtypeStruct((rows, width), BF16)
    slot = (
        jax.ShapeDtypeStruct((depth, width), BF16),
        jax.ShapeDtypeStruct((depth, rows), BF16),
        jax.ShapeDtypeStruct((8, rows), F32),
    )
    outs = pl.pallas_call(
        attention_kernel,
        out_shape=(
            rows_low,
            rows_low,
            jax.ShapeDtypeStruct((2 * inner, rows), BF16),
            jax.ShapeDtypeStruct((2 * inner, width), BF16),
        )
        + slot
        + slot,
        in_specs=smem(3) + vmem(9),
        out_specs=tuple(vmem(10)),
        name="attention",
        **settings(),
    )(ends, first, order, x, vectors, *own, *pieces, crossed)
    return outs[:4], outs[4:7], outs[7:]


def feed_slot(places_ref, second, second_t, cot_ref, cot_t, up, down, bias, grads, bias_grad):
    width, units = up.shape
    d_rows, u_rows = units // 4, width // 4
    pre = dot(second[...], up[...]) + bias[...].astype(F32)[0:1]
    gate = 0.5 * (1.0 + lax.erf(pre * (2.0**-0.5)))
    slope = gate + pre * (jnp.exp2(pre * pre * (-0.5 * LOG2E)) * (0.5 / 3.141592653589793) ** 0.5)
    hidden = (pre * gate).astype(BF16)
    out = dot(hidden, down[...])
    down_grad = dot(cot_t[...], hidden).T.astype(BF16)
    for i in range(4):
        grads[places_ref[i], u_rows:, :] = down_grad[i * d_rows : (i + 1) * d_rows]
    act = (dot(cot_ref[...], down[...], 1, 1) * slope).astype(BF16)
    bias_grad[...] = jnp.sum(act.astype(F32), axis=0, keepdims=True)
    back = dot(act, up[...], 1, 1)
    up_grad = dot(second_t[...], act).astype(BF16)
    for i in range(4):
        grads[places_ref[i], :u_rows, :] = up_grad[i * u_rows : (i + 1) * u_rows]
    return out, back


def fetch(source, target, sem):
    copy = pltpu.make_async_copy(source, target, sem)
    copy.start()
    return copy


def wait_all(copies):
    for copy in copies:
        copy.wait()


def feed_kernel(*refs):
    order_ref, places_ref, vectors_ref, x_hbm, mine_hbm, other_hbm, cot_hbm = refs[:7]
    own_up_hbm, own_down_hbm, own_bias_hbm, pieces, crossed_hbm, far_hbm, refs = (
        refs[7], refs[8], refs[9], refs[10:14], refs[14], refs[15], refs[16:],
    )
    middle_hbm, out_ref, back_ref, bias_one, bias_two, *leave_refs = refs[:9]
    x_ref, mine_ref, other_ref, cot_ref, middle_ref, second, second_t, cot_t, up, down, bias, grads, out_sum, back_sum, sems = refs[9:]
    _, width, units = up.shape
    u_rows, d_rows = width // 4, units // 4
    size = u_rows + d_rows + PAD
    half = u_rows + PAD
    free = iter(range(40))
    sem = lambda: sems.at[next(free)]
    early = [fetch(*pair, sem()) for pair in ((x_hbm, x_ref), (mine_hbm, mine_ref), (other_hbm, other_ref))]
    first = [fetch(pieces[0].at[pl.ds(size - PAD, PAD)], bias.at[0], sem())]
    for index, piece in enumerate(pieces):
        first.append(fetch(piece.at[pl.ds(0, u_rows)], up.at[0, place(order_ref, index, u_rows)], sem()))
        first.append(fetch(piece.at[pl.ds(u_rows, d_rows)], down.at[0, place(order_ref, index, d_rows)], sem()))
    cot_copy = fetch(cot_hbm, cot_ref, sem())
    home = [
        pltpu.make_async_copy(own_up_hbm, up.at[1], sem()),
        pltpu.make_async_copy(own_down_hbm, down.at[1], sem()),
        pltpu.make_async_copy(own_bias_hbm, bias.at[1], sem()),
    ]
    away = [pltpu.make_async_copy(pieces[0].at[pl.ds(size + u_rows, PAD)], bias.at[1], sem())]
    for index, piece in enumerate(pieces):
        part = piece.at[pl.ds(size, u_rows)]
        away.append(pltpu.make_async_copy(part, up.at[1, place(order_ref, index, u_rows)], sem()))
        part = far_hbm if index == 3 else crossed_hbm.at[pl.ds(CROSSED[index] * half, half)]
        part = part.at[pl.ds(0, d_rows)]
        away.append(pltpu.make_async_copy(part, down.at[1, place(order_ref, index, d_rows)], sem()))

    @pl.when(order_ref[4] == 1)
    def _():
        for copy in home:
            copy.start()

    @pl.when(order_ref[4] == 0)
    def _():
        for copy in away:
            copy.start()

    wait_all(early)
    middle = x_ref[...].astype(F32) + (mine_ref[...].astype(F32) + other_ref[...].astype(F32))
    middle_ref[...] = middle
    late = [fetch(middle_ref, middle_hbm, sem())]
    unit, _ = normal(middle)
    low = (unit * vectors_ref[2:3, :] + vectors_ref[3:4, :]).astype(BF16)
    second[...] = low
    second_t[...] = low.T
    cot_copy.wait()
    cot_t[...] = cot_ref[...].T
    wait_all(first)
    def leave(slot, start, rows, refs, target):
        return [
            fetch(
                grads.at[slot, pl.ds(2 * part, 2), pl.ds(start, rows)],
                ref.at[:, pl.ds(target, rows)],
                sem(),
            )
            for part, ref in enumerate(refs)
        ]

    shared = (places_ref, second, second_t, cot_ref, cot_t)
    out, back = feed_slot(*shared, up.at[0], down.at[0], bias.at[0], grads.at[0], bias_one)
    out_sum[...] = out
    back_sum[...] = back
    late += leave(0, 0, u_rows + d_rows, leave_refs[:2], 0)

    @pl.when(order_ref[4] == 1)
    def _():
        wait_all(home)

    @pl.when(order_ref[4] == 0)
    def _():
        wait_all(away)

    out, back = feed_slot(*shared, up.at[1], down.at[1], bias.at[1], grads.at[1], bias_two)
    late += leave(1, 0, u_rows, leave_refs[:2], u_rows + d_rows)
    late += leave(1, u_rows, d_rows, leave_refs[2:], 0)
    out_ref[...] = (out_sum[...] + out).astype(BF16)
    back_ref[...] = (back_sum[...] + back).astype(BF16)
    wait_all(late)


def feed(order, places, x, mine, other, cot, vectors, own, pieces, crossed, crossed_far):
    rows, width = x.shape
    units = own[1].shape[0]
    size = (width + units) // 4
    rows_low = jax.ShapeDtypeStruct((rows, width), BF16)
    rows_full = jax.ShapeDtypeStruct((rows, width), F32)
    most = jax.ShapeDtypeStruct((2, size + width // 4, width), BF16)
    least = jax.ShapeDtypeStruct((2, units // 4, width), BF16)
    bias_grad = jax.ShapeDtypeStruct((1, units), F32)
    return pl.pallas_call(
        feed_kernel,
        out_shape=(rows_full, rows_low, rows_low, bias_grad, bias_grad, most, most, least, least),
        in_specs=smem(2) + vmem(1) + anywhere(13),
        out_specs=tuple(anywhere(1) + vmem(4) + anywhere(4)),
        scratch_shapes=[pltpu.VMEM((rows, width), BF16)] * 4
        + [
            pltpu.VMEM((rows, width), F32),
            pltpu.VMEM((rows, width), BF16),
            pltpu.VMEM((width, rows), BF16),
            pltpu.VMEM((width, rows), BF16),
            pltpu.VMEM((2, width, units), BF16),
            pltpu.VMEM((2, units, width), BF16),
            pltpu.VMEM((2, PAD, units), BF16),
            pltpu.VMEM((2, 4, size, width), BF16),
            pltpu.VMEM((rows, width), F32),
            pltpu.VMEM((rows, width), F32),
            pltpu.SemaphoreType.DMA((40,)),
        ],
        name="feed",
        **settings(42 * 1024 * 1024),
    )(order, places, vectors, x, mine, other, cot, *own, *pieces, crossed, crossed_far)


def heads_back(slot, labels, places_ref, branch_ref, normed_ref, w_ref, proj_ref, packed_ref, heads_ref,
               lse_ref, packed_grad, w_grad, grads):
    rows = branch_ref.shape[0]
    depth, inner = w_ref.shape[0], proj_ref.shape[0] // 2
    label_col, label_row = labels

    def head(h):
        base = h * 3 * HEAD_DIM
        part = slice(h * HEAD_DIM + slot * inner, (h + 1) * HEAD_DIM + slot * inner)
        mixed = heads_ref[part, :]
        mixed_grad = dot(proj_ref[part, :], branch_ref[...], 1, 1).astype(BF16)
        packed = packed_ref[base : base + 3 * HEAD_DIM, :]
        queries = packed[:HEAD_DIM] * SCALE
        keys = packed[HEAD_DIM : 2 * HEAD_DIM]
        key_rows = keys.T
        value_rows = packed[2 * HEAD_DIM :].T
        inner_sum = jnp.sum(mixed.astype(F32) * mixed_grad.astype(F32), axis=0, keepdims=True)
        scores = dot(key_rows, queries) * LOG2E
        scores = jnp.where(label_col == label_row, scores, -1e30)
        prob = jnp.exp2(scores - lse_ref[h : h + 1, :])
        value_grad = dot(mixed_grad, prob.astype(BF16), 1, 1)
        prob_grad = dot(value_rows, mixed_grad)
        score_grad = (prob * (prob_grad - inner_sum)).astype(BF16)
        query_grad = dot(keys, score_grad) * SCALE
        key_grad = dot(queries, score_grad, 1, 1)
        for i, grad in enumerate((query_grad, key_grad, value_grad)):
            start = base + i * HEAD_DIM
            packed_grad[start : start + HEAD_DIM, :] = grad.astype(BF16)

    for h in range(depth // (3 * HEAD_DIM)):
        head(h)
    w_grad[:depth, :] = dot(packed_grad[...], normed_ref[...]).astype(BF16)
    w_grad[depth:, :] = dot(heads_ref[slot * inner : (slot + 1) * inner, :], branch_ref[...]).astype(BF16)
    w_size, p_size = depth // 4, inner // 4
    size = w_size + p_size
    for i in range(4):
        grads[places_ref[i], PAD : PAD + w_size, :] = w_grad[i * w_size : (i + 1) * w_size, :]
        grads[places_ref[i], PAD + w_size : PAD + size, :] = w_grad[depth + i * p_size : depth + (i + 1) * p_size, :]


def send_grads(grads, start, out_refs, sems):
    copies = [
        pltpu.make_async_copy(grads.at[i, pl.ds(start, grads.shape[1] - start)], out_ref, sems.at[i])
        for i, out_ref in enumerate(out_refs)
    ]
    for copy in copies:
        copy.start()
    for copy in copies:
        copy.wait()


def back_one_kernel(
    ends_ref,
    first_ref,
    places_ref,
    middle_ref,
    mine_ref,
    other_ref,
    cot_ref,
    vectors_ref,
    normed_ref,
    heads_ref,
    proj_ref,
    w_ref,
    packed_ref,
    lse_ref,
    middle_grad_ref,
    branch_ref,
    sums_ref,
    packed_grad_ref,
    far_ref,
    near_ref,
    side_ref,
    keep_ref,
    w_grad,
    grads,
    sems,
):
    rows = middle_ref.shape[0]
    unit, inverse = normal(middle_ref[...])
    grad = mine_ref[...].astype(F32) + other_ref[...].astype(F32)
    sums_ref[0:1, :] = jnp.sum(grad * unit, axis=0, keepdims=True) * 0.5
    sums_ref[1:2, :] = jnp.sum(grad, axis=0, keepdims=True) * 0.5
    scaled = grad * vectors_ref[2:3, :]
    mean_one = jnp.mean(scaled, axis=-1, keepdims=True)
    mean_two = jnp.mean(scaled * unit, axis=-1, keepdims=True)
    middle_grad = cot_ref[...].astype(F32) + (scaled - mean_one - unit * mean_two) * inverse
    middle_grad_ref[...] = middle_grad
    branch_ref[...] = middle_grad.astype(BF16)
    labels = [row_labels(ends_ref, first_ref[0], shape, dim) for dim, shape in ((0, (rows, 1)), (1, (1, rows)))]
    heads_back(0, labels, places_ref, branch_ref, normed_ref, w_ref, proj_ref, packed_ref, heads_ref,
                        lse_ref, packed_grad_ref, w_grad, grads)
    send_grads(grads, PAD, (far_ref, near_ref, side_ref, keep_ref), sems)


def back_two_kernel(
    ends_ref,
    first_ref,
    places_ref,
    branch_ref,
    normed_ref,
    heads_ref,
    proj_ref,
    w_ref,
    packed_ref,
    lse_ref,
    packed_grad_ref,
    far_ref,
    near_ref,
    side_ref,
    keep_ref,
    w_grad,
    grads,
    sems,
):
    rows = branch_ref.shape[0]
    labels = [row_labels(ends_ref, first_ref[0], shape, dim) for dim, shape in ((0, (rows, 1)), (1, (1, rows)))]
    heads_back(1, labels, places_ref, branch_ref, normed_ref, w_ref, proj_ref, packed_ref, heads_ref,
                        lse_ref, packed_grad_ref, w_grad, grads)
    send_grads(grads, PAD, (far_ref, near_ref, side_ref, keep_ref), sems)


def first_back_kernel(grad_one_ref, grad_two_ref, w_one_ref, w_two_ref, x_ref, first_grad_ref, sums_ref):
    grad = dot(grad_one_ref[...], w_one_ref[...], 0, 0) + dot(
        grad_two_ref[...], w_two_ref[...], 0, 0
    )
    first_grad_ref[...] = grad.astype(BF16)
    unit, _ = normal(x_ref[...].astype(F32))
    sums_ref[0:1, :] = jnp.sum(grad * unit, axis=0, keepdims=True)
    sums_ref[1:2, :] = jnp.sum(grad, axis=0, keepdims=True)


def first_back(grad_one, grad_two, w_one, w_two, x):
    return pl.pallas_call(
        first_back_kernel,
        out_shape=(
            jax.ShapeDtypeStruct(x.shape, BF16),
            jax.ShapeDtypeStruct((2, x.shape[1]), F32),
        ),
        in_specs=vmem(5),
        out_specs=tuple(vmem(2)),
        name="first_back",
        **settings(),
    )(grad_one, grad_two, w_one, w_two, x)


def back_scratch(depth, inner, width):
    return [
        pltpu.VMEM((depth + inner, width), BF16),
        pltpu.VMEM((4, PAD + (depth + inner) // 4, width), BF16),
        pltpu.SemaphoreType.DMA((4,)),
    ]


def back_one(ends, first, places, middle, mine, other, cot, vectors, shared, slot):
    rows, width = middle.shape
    depth, inner = slot[0].shape[0], shared[2].shape[0] // 2
    part = jax.ShapeDtypeStruct(((depth + inner) // 4, width), BF16)
    outs = pl.pallas_call(
        back_one_kernel,
        out_shape=(
            jax.ShapeDtypeStruct((rows, width), F32),
            jax.ShapeDtypeStruct((rows, width), BF16),
            jax.ShapeDtypeStruct((2, width), F32),
            jax.ShapeDtypeStruct((depth, rows), BF16),
            part,
            part,
            part,
            part,
        ),
        in_specs=smem(3) + vmem(11),
        out_specs=tuple(vmem(4) + anywhere(4)),
        scratch_shapes=back_scratch(depth, inner, width),
        name="back_one",
        **settings(),
    )(ends, first, places, middle, mine, other, cot, vectors, *shared, *slot)
    return outs[:4], outs[4:]


def back_two(ends, first, places, branch, shared, slot):
    rows, width = branch.shape
    depth, inner = slot[0].shape[0], shared[2].shape[0] // 2
    part = jax.ShapeDtypeStruct(((depth + inner) // 4, width), BF16)
    outs = pl.pallas_call(
        back_two_kernel,
        out_shape=(jax.ShapeDtypeStruct((depth, rows), BF16), part, part, part, part),
        in_specs=smem(3) + vmem(7),
        out_specs=tuple(vmem(1) + anywhere(4)),
        scratch_shapes=back_scratch(depth, inner, width),
        name="back_two",
        **settings(),
    )(ends, first, places, branch, *shared, *slot)
    return outs[0], outs[1:]


def settle_some_kernel(order_ref, *refs):
    pieces, others_ref, outs = refs[:3], refs[3], refs[4:]
    up_ref, down_ref, qkv_ref, proj_ref, sums_ref = outs
    feed_rows = up_ref.shape[0] // 4
    qkv_rows, proj_rows = qkv_ref.shape[0] // 4, proj_ref.shape[0] // 4
    size = pieces[0].shape[0]
    early = size - feed_rows - PAD
    late = qkv_rows - early

    def put(out, index, rows, offset, count, value):
        start = pl.multiple_of(order_ref[index] * rows + offset, 8)
        out[pl.ds(start, count), :] = value.astype(F32)

    def first_half(index, ref, base):
        put(up_ref, index, feed_rows, 0, feed_rows, ref[base : base + feed_rows, :])
        base = base + feed_rows
        put(sums_ref, index, PAD, 0, PAD, ref[base : base + PAD, :])
        put(qkv_ref, index, qkv_rows, 0, early, ref[base + PAD : base + PAD + early, :])

    def second_half(index, ref, base):
        put(down_ref, index, feed_rows, 0, feed_rows, ref[base : base + feed_rows, :])
        base = base + feed_rows
        put(qkv_ref, index, qkv_rows, early, late, ref[base : base + late, :])
        base = base + late
        put(proj_ref, index, proj_rows, 0, proj_rows, ref[base : base + proj_rows, :])

    halves = (first_half, second_half)
    for core in range(2):

        @pl.when(order_ref[5] == core)
        def _():
            for index, piece in enumerate(pieces):
                halves[core](index, piece, 0)
                halves[1 - core](index, others_ref, CROSSED[index] * size)


def settle_last_kernel(order_ref, piece_ref, others_ref, *refs):
    outs, buffers, sems = refs[5:10], refs[10:15], refs[15]
    up, down, qkv, proj, sums = buffers
    size, feed_rows = piece_ref.shape[0], up.shape[0]
    early = size - feed_rows - PAD
    late = qkv.shape[0] - early

    def first_half(ref):
        up[...] = ref[:feed_rows, :].astype(F32)
        sums[...] = ref[feed_rows : feed_rows + PAD, :].astype(F32)
        qkv[:early, :] = ref[feed_rows + PAD :, :].astype(F32)

    def second_half(ref):
        down[...] = ref[:feed_rows, :].astype(F32)
        qkv[early:, :] = ref[feed_rows : feed_rows + late, :].astype(F32)
        proj[...] = ref[feed_rows + late : feed_rows + late + proj.shape[0], :].astype(F32)

    @pl.when(order_ref[5] == 0)
    def _():
        first_half(piece_ref)
        second_half(others_ref)

    @pl.when(order_ref[5] == 1)
    def _():
        first_half(others_ref)
        second_half(piece_ref)

    copies = []
    for i, (buffer, out) in enumerate(zip(buffers, outs)):
        rows = buffer.shape[0]
        start = pl.multiple_of(order_ref[3] * rows, 8)
        copies.append(pltpu.make_async_copy(buffer, out.at[pl.ds(start, rows)], sems.at[i]))
    for copy in copies:
        copy.start()
    for copy in copies:
        copy.wait()


def settle(order, pieces, others, sizes, settled):
    width, units, depth, inner = sizes
    shapes = [(width, units), (units, width), (depth, width), (inner, width), (4 * PAD, width)]
    out_shape = tuple(jax.ShapeDtypeStruct(shape, F32) for shape in shapes)
    if not settled:
        return pl.pallas_call(
            settle_some_kernel,
            out_shape=out_shape,
            in_specs=smem(1) + vmem(4),
            out_specs=tuple(vmem(5)),
            name="settle",
            **settings(18 * 1024 * 1024),
        )(order, *pieces, others)
    return pl.pallas_call(
        settle_last_kernel,
        out_shape=out_shape,
        in_specs=smem(1) + vmem(2) + anywhere(5),
        out_specs=tuple(anywhere(5)),
        scratch_shapes=[pltpu.VMEM((rows // 4, columns), F32) for rows, columns in shapes]
        + [pltpu.SemaphoreType.DMA((5,))],
        input_output_aliases={3 + i: i for i in range(5)},
        name="settle_last",
        **settings(12 * 1024 * 1024),
    )(order, *pieces, others, *settled)


def spread(piece, *before):
    near = lax.ppermute(piece, LAYER, FIRST)
    side = lax.ppermute(piece, LAYER, SECOND)
    far = lax.ppermute(after(near, side, *before) if before else near, LAYER, SECOND)
    return piece, near, side, far


def scatter_at_once(far, near, side, keep):
    return keep, tuple(
        lax.ppermute(part, LAYER, pairs)
        for part, pairs in ((near, FIRST), (side, SECOND), (far, BOTH))
    )


def add_low(*parts):
    total = parts[0].astype(F32)
    for part in parts[1:]:
        total = total + part.astype(F32)
    return total.astype(BF16)


def to_shard(sum_one, sum_two):
    return (
        lax.ppermute(sum_one, CORE_T, ROUND_ONE_BACK),
        lax.ppermute(sum_two, CORE_T, ROUND_TWO_BACK),
    )


def over_outer(share, outer):
    return lax.psum(share.astype(F32), "o").astype(BF16) if outer > 1 else share


def half_rows(parts, place):
    rows = parts[0].shape[0] // 2
    return add_low(*(lax.dynamic_slice_in_dim(part, place * rows, rows, 0) for part in parts))


def after(value, *others):
    return lax.optimization_barrier((value,) + others)[0] if others else value


def local(
    patches,
    item_patches,
    attn_gain,
    attn_bias,
    qkv_weight,
    proj_weight,
    mlp_gain,
    mlp_bias,
    up_weight,
    up_bias,
    down_weight,
    cotangent,
):
    c, t, x, y = (lax.axis_index(name) for name in ("c", "t", "x", "y"))
    outer = lax.axis_size("o")
    quarter = 2 * y + x
    member = t & 1
    own_rows, width = patches.shape
    first_bit = 1 + c
    home = (t // 2 == c).astype(jnp.int32)
    order = jnp.stack([quarter, quarter ^ first_bit, quarter ^ (3 - first_bit), quarter ^ 3, home, c])
    steps = jnp.arange(4) ^ quarter
    places = jnp.where(
        steps == 3, 0, jnp.where(steps == first_bit, 1, jnp.where(steps == 0, 3, 2))
    )

    def exchange(array):
        return lax.ppermute(array, "c", SWAP)

    def both_halves(array, *before):
        other = exchange(after(array, *before))
        return jnp.where(
            c == 0, jnp.concatenate([array, other], 0), jnp.concatenate([other, array], 0)
        )

    def cut(array):
        rows = array.shape[0] // 4
        return lax.dynamic_slice_in_dim(array, quarter * rows, rows, 0)

    qkv_t = qkv_weight.T
    depth, units, inner = qkv_t.shape[0], down_weight.shape[0], proj_weight.shape[0]
    piece_a = jnp.concatenate([cut(qkv_t), cut(proj_weight)], 0)
    half_a = piece_a.shape[0] // 2
    piece_a_two = lax.dynamic_slice_in_dim(piece_a, home * half_a, half_a, 0)
    piece_a, piece_a_two, patches = lax.optimization_barrier((piece_a, piece_a_two, patches))
    a_one = lax.ppermute(piece_a, CORE_T, ROUND_ONE)
    a_two = lax.ppermute(piece_a_two, CORE_T, ROUND_TWO)
    inputs = lax.ppermute(patches, CORE_T, ROW_SWAP)
    items = exchange(item_patches)
    ends = jnp.cumsum(jnp.where(member == c, item_patches, items)[0])
    first = (t // 2 * BLOCK).astype(jnp.int32).reshape(1)
    vectors = jnp.stack([attn_gain, attn_bias, mlp_gain, mlp_bias])
    bias_rows = jnp.broadcast_to(up_bias[None, :], (PAD, units))
    cut_up, cut_down = cut(up_weight), cut(down_weight)
    piece_b = jnp.concatenate([cut_up, cut_down, bias_rows], 0)
    half_b = jnp.concatenate([jnp.where(home == 1, cut_down, cut_up), bias_rows], 0)
    block_in = both_halves(inputs)
    a_one, a_two, block_in, ends, first, order, places, vectors, piece_b, half_b, bias_rows = (
        lax.optimization_barrier(
            (a_one, a_two, block_in, ends, first, order, places, vectors, piece_b, half_b, bias_rows)
        )
    )
    b_one = lax.ppermute(piece_b, CORE_T, ROUND_ONE)
    b_two = lax.ppermute(half_b, CORE_T, ROUND_TWO)
    pieces_a = spread(jnp.concatenate([a_one, a_two], 0))
    crossed_a = lax.ppermute(
        jnp.concatenate([piece[2 * half_a :] for piece in pieces_a], 0), "c", SWAP
    )
    both_b = jnp.concatenate([b_one, b_two], 0)
    shared, one, two = attention(
        ends, first, order, after(block_in, both_b), vectors, (qkv_t, proj_weight), pieces_a, crossed_a
    )
    normed, mine, heads_out, proj = shared
    shared = (normed, heads_out, proj)
    pieces_b = spread(both_b, mine)
    other = exchange(mine)
    block_cot = both_halves(lax.ppermute(after(cotangent, both_b), CORE_T, ROW_SWAP), mine)
    crossed_b = exchange(jnp.concatenate([piece[piece_b.shape[0] :] for piece in pieces_b[:3]], 0))
    crossed_far = exchange(pieces_b[3][piece_b.shape[0] :])
    middle, out_part, back_part, bias_one, bias_two, send, keep, send_last, keep_last = feed(
        order, places, block_in, mine, other, block_cot, vectors,
        (up_weight, down_weight, bias_rows), pieces_b, crossed_b, crossed_far,
    )
    hop = lax.ppermute(send, LAYER, FIRST)

    def own(array):
        return lax.dynamic_slice_in_dim(array, c * own_rows, own_rows, 0)

    (middle_grad, branch, mlp_sums, grad_one), back_one_out = back_one(
        ends, first, places, middle, back_part, exchange(back_part), block_cot, vectors, shared, one
    )
    hop = after(hop, branch)
    hop_last = lax.ppermute(after(send_last, hop), LAYER, FIRST)
    next_hop = add_low(keep[0], hop[0])
    far = lax.ppermute(next_hop, LAYER, SECOND)
    keep_one, got_one = scatter_at_once(*back_one_out)
    grad_two, back_two_out = back_two(
        ends, first, places, after(branch, next_hop), shared, two
    )
    far, hop_last = after((far, hop_last), grad_two)
    far_last = lax.ppermute(add_low(keep_last[0], hop_last[0]), LAYER, SECOND)
    feed_sum = add_low(keep[1], hop[1], far)
    size = (width + units) // 4
    back_two_out, feed_sum, grad_two = lax.optimization_barrier((back_two_out, feed_sum, grad_two))
    part_one = lax.ppermute(feed_sum[:size], CORE_T, ROUND_ONE_BACK)
    keep_two, got_two = scatter_at_once(*back_two_out)
    first_part, attn_sums = first_back(grad_one, grad_two, one[0], two[0], block_in)
    far_last, out_part = after((far_last, out_part), first_part)
    feed_sum_two = jnp.concatenate(
        [feed_sum[size:], add_low(keep_last[1], hop_last[1], far_last)], 0
    )
    feed_parts = (part_one, lax.ppermute(feed_sum_two, CORE_T, ROUND_TWO_BACK))
    slot_one = 2 * c + jnp.where(t // 2 == c, 1 - member, member ^ c)
    shards = jnp.arange(4)[:, None]
    bias_part = jnp.where(shards == slot_one, bias_one, 0.0) + jnp.where(
        shards == (slot_one ^ 1), bias_two, 0.0
    )
    small = jnp.concatenate(
        [attn_sums, mlp_sums, bias_part, jnp.zeros((PAD - 8, width), F32)], 0
    ).astype(BF16)
    small = add_low(small, exchange(small))

    unit, inverse = normal(inputs.astype(F32))
    first_grad = own(first_part).astype(F32) + own(exchange(first_part)).astype(F32)
    scaled = first_grad * attn_gain
    mean_one = jnp.mean(scaled, axis=-1, keepdims=True)
    mean_two = jnp.mean(scaled * unit, axis=-1, keepdims=True)
    grad_in = own(middle_grad) + (scaled - mean_one - unit * mean_two) * inverse
    grad_in = grad_in.astype(BF16)
    result = own(middle) + own(out_part).astype(F32) + own(exchange(out_part)).astype(F32)
    result = result.astype(BF16)
    got_one, got_two = after((got_one, got_two), feed_parts)
    blank = jnp.zeros((PAD, width), BF16)
    back_sum_one = jnp.concatenate([small, add_low(keep_one, *got_one), blank], 0)
    back_sum_two = jnp.concatenate([small, add_low(keep_two, *got_two), blank], 0)
    back_parts = to_shard(back_sum_one, back_sum_two)

    def halves(place):
        return jnp.concatenate([half_rows(feed_parts, place), half_rows(back_parts, place)], 0)

    share = add_low(halves(c), exchange(halves(1 - c)))
    share = over_outer(share, outer)
    share, grad_in, result = lax.optimization_barrier((share, grad_in, result))
    patches_grad = lax.ppermute(grad_in, CORE_T, ROW_SWAP).astype(F32)
    result = lax.ppermute(result, CORE_T, ROW_SWAP)
    near = lax.ppermute(share, LAYER, FIRST)
    side = lax.ppermute(share, LAYER, SECOND)
    near, side, patches_grad, result = lax.optimization_barrier((near, side, patches_grad, result))
    far = lax.ppermute(near, LAYER, SECOND)
    others = exchange(jnp.concatenate([share, near, side], 0))
    settled = settle(order, (share, near, side), others, (width, units, depth, inner), ())
    far, *settled = lax.optimization_barrier((far, *settled))
    up_sum, down_sum, qkv_sum, proj_sum, sums = settle(
        order, (far,), exchange(far), (width, units, depth, inner), settled
    )
    sums = jnp.sum(sums.reshape(4, PAD, width)[:, :8], axis=0)
    up_bias_sum = lax.dynamic_index_in_dim(sums, 4 + t, 0, keepdims=False)
    return (
        result,
        patches_grad,
        sums[0],
        sums[1],
        qkv_sum.T,
        proj_sum,
        sums[2],
        sums[3],
        up_sum,
        up_bias_sum,
        down_sum,
    )


def solution(mesh):
    dp, tensor = mesh.shape["dp"], mesh.shape["tensor"]
    grid = Mesh(mesh.devices.reshape(dp // 8, 2, 2, 2, tensor), ("o", "y", "x", "c", "t"))
    dp_axes = ("o", "y", "x", "c")
    rows = P(dp_axes + ("t",), None)
    return jax.shard_map(
        local,
        mesh=grid,
        in_specs=(
            rows,
            P(dp_axes, None),
            P(),
            P(),
            P(None, "t"),
            P("t", None),
            P(),
            P(),
            P(None, "t"),
            P("t"),
            P("t", None),
            rows,
        ),
        out_specs=(
            rows,
            rows,
            P(),
            P(),
            P(None, "t"),
            P("t", None),
            P(),
            P(),
            P(None, "t"),
            P("t"),
            P("t", None),
        ),
        check_vma=False,
    )
```
